32 devices in a mesh: replica: 4 (over y, core), fsdp: 8 (over z, x).
Axes of the slice: x: 2, y: 2, z: 4, core: 2. Of those that a mesh axis runs over, the one named last changes fastest.
Arguments:
- layer_input: bfloat16 [4, 4096, 4096], P('replica', 'fsdp'), may hold values from -36 to 36, as said below
- norm_gain: bfloat16 [4, 4096], P('replica', 'fsdp'), may hold values from 0.099609375 to 1.8984375
- kv_weight: bfloat16 [4, 4096, 1024], P('replica', 'fsdp'), may hold values from -0.09375 to 0.09375
- kv_cotangent: bfloat16 [4, 4096, 1024], P('replica', 'fsdp'), may hold values from -6 to 6
- pseudo_grad: float32 [4, 3072, 1024], P('replica', 'fsdp'), may hold values from -6 to 6
- outer_momentum: float32 [3072, 1024], P('fsdp'), may hold values from -6 to 6
- global_params: float32 [3072, 1024], P('fsdp'), may hold values from -6 to 6
- local_params: bfloat16 [4, 3072, 1024], P('replica', 'fsdp'), may hold values from -6 to 6
Outputs:
- kv_out: bfloat16 [4, 4096, 1024], P('replica', 'fsdp')
- input_grad: bfloat16 [4, 4096, 4096], P('replica', 'fsdp')
- kv_weight_grad: float32 [4, 4096, 1024], P('replica', 'fsdp')
- gain_grad: float32 [4, 4096], P('replica', 'fsdp')
- momentum_new: float32 [3072, 1024], P('fsdp')
- global_new: float32 [3072, 1024], P('fsdp')
- local_new: bfloat16 [4, 3072, 1024], P('replica', 'fsdp')
The draws below stay inside these ranges and needn't reach their ends.
Inputs may be any that keep to these rules, and one draw needn't show every extreme that they name: `layer_input`: activations of the residual stream.
All inputs are finite; a program needn't handle non-finite values.
Results may differ from the reference program's by a relative error of at most 0.0049.
Values may be sent and summed in bfloat16 or wider, within the bound.
No kernel may reach another device: no remote copies, remote signals or barrier semaphores. Data moves between devices by JAX's collectives and lax.ppermute only.
A program may use at most 128 MiB of HBM per device.

```python
import math
import jax
import jax.numpy as jnp
from jax import lax

D = 4096
HEAD = 128
KVW = 512
SEQ_LEN = 4096
TOK_DEV = 512
TOKENS = 4096
FCOLS = 1024
FROWS = 3072
N_REPLICA = 4
N_FSDP = 8


def draw_layer_input(key, part):
    first, second, third = jax.random.split(key, 3)
    shape = (N_REPLICA, TOKENS, D)
    base = jnp.clip(jax.random.normal(first, shape, jnp.float32), -4.0, 4.0)
    row_scale = jnp.exp(jax.random.uniform(second, (N_REPLICA, TOKENS, 1), jnp.float32, math.log(0.3), math.log(3.0)))
    col_scale = jnp.exp(jax.random.uniform(third, (N_REPLICA, 1, D), jnp.float32, math.log(0.3), math.log(3.0)))
    return (base * row_scale * col_scale).astype(jnp.bfloat16)


def shard_levels(rng, extent, shards, least, largest):
    def one(axis_at, shards_of):
        heights = jax.random.uniform(jax.random.fold_in(jax.random.fold_in(rng, 6), axis_at), (shards_of,), jnp.float32, least / len(shards), largest / len(shards))
        return jnp.repeat(jnp.exp(heights), extent[axis_at] // shards_of).reshape((-1,) + (1,) * (len(extent) - axis_at - 1))

    factor_of = one(*shards[0])
    for cut in shards[1:]:
        factor_of = factor_of * one(*cut)
    return factor_of


def scatter_about(key, extent, scale, limit, cuts=(), held_as=jnp.bfloat16):
    result = scale * jax.random.normal(key, extent, jnp.float32)
    if cuts:
        result = result * shard_levels(key, extent, cuts, -0.22, 0.18)
    return jnp.clip(result, -limit, limit).astype(held_as)


def setup_inputs(seed: int = 0) -> dict:
    key_of = jax.random.split(jax.random.key(seed), 9)
    layer_input = draw_layer_input(jax.random.fold_in(key_of[8], 71), 0)
    norm_gain = jnp.clip(1.0 + 0.18 * jax.random.normal(key_of[1], (N_REPLICA, D), jnp.float32), 0.099609375, 1.8984375).astype(jnp.bfloat16)
    kv_weight = scatter_about(key_of[2], (N_REPLICA, D, 2 * KVW), D ** -0.5, 0.09375, ((0, 4), (1, 8)))
    kv_cotangent = scatter_about(key_of[3], (N_REPLICA, TOKENS, 2 * KVW), 1.0, 6.0, ((0, 4), (1, 8)))
    pseudo_grad = scatter_about(key_of[4], (N_REPLICA, FROWS, FCOLS), 1.0, 6.0, ((0, 4), (1, 8)), jnp.float32)
    outer_momentum = scatter_about(key_of[5], (FROWS, FCOLS), 0.5, 6.0, ((0, 8),), jnp.float32)
    global_params = scatter_about(key_of[6], (FROWS, FCOLS), 1.0, 6.0, ((0, 8),), jnp.float32)
    local_params = scatter_about(key_of[7], (N_REPLICA, FROWS, FCOLS), 1.0, 6.0, ((0, 4), (1, 8)))
    return dict(layer_input=layer_input, norm_gain=norm_gain, kv_weight=kv_weight, kv_cotangent=kv_cotangent, pseudo_grad=pseudo_grad, outer_momentum=outer_momentum, global_params=global_params, local_params=local_params)


epsilon = 1e-05
rope_base = 500000.0
momentum_rate = 0.9
outer_rate = 0.7
mixing_rate = 0.5

def angles_for(positions, head):
    half = head // 2
    index_f = jnp.arange(half, dtype=jnp.float32)
    inverse = jnp.exp(index_f * (-2.0 * math.log(rope_base) / head))
    angle = positions.astype(jnp.float32)[:, None] * inverse[None, :]
    return (jnp.cos(angle), jnp.sin(angle))

def rotate_keys(keys, cosine, sine, head, sign):
    count = keys.shape[0]
    shaped = keys.reshape(count, -1, head)
    half = head // 2
    first = shaped[:, :, :half]
    second = shaped[:, :, half:]
    cos_b = cosine[:, None, :]
    sin_b = sine[:, None, :] * sign
    out = jnp.concatenate([first * cos_b - second * sin_b, second * cos_b + first * sin_b], axis=2)
    return out.reshape(count, -1)

def inner_step(layer_input, norm_gain, kv_weight, kv_cotangent):
    tokens = layer_input.shape[0]
    kvw = kv_weight.shape[1] // 2
    positions = jnp.arange(tokens, dtype=jnp.int32) % SEQ_LEN
    cosine, sine = angles_for(positions, HEAD)
    values = layer_input.astype(jnp.float32)
    inv_rms = lax.rsqrt(lax.optimization_barrier(jnp.mean(values * values, axis=-1, keepdims=True)) + epsilon)
    normed = values * inv_rms
    gain_f = norm_gain.astype(jnp.float32)
    hidden = (normed * gain_f).astype(jnp.bfloat16)
    key_pre = jnp.dot(hidden, kv_weight, preferred_element_type=jnp.float32)
    kv_out = jnp.concatenate([rotate_keys(key_pre[:, :kvw], cosine, sine, HEAD, 1.0), key_pre[:, kvw:]], axis=1).astype(jnp.bfloat16)
    key_back = rotate_keys(kv_cotangent[:, :kvw].astype(jnp.float32), cosine, sine, HEAD, -1.0).astype(jnp.bfloat16)
    kv_grad = jnp.concatenate([key_back, kv_cotangent[:, kvw:]], axis=1)
    hidden_grad = lax.dot_general(kv_grad, kv_weight, (((1,), (1,)), ((), ())), preferred_element_type=jnp.float32)
    scale = 1.0 / math.sqrt(tokens)
    hidden_blocks = hidden.reshape(N_FSDP, TOK_DEV, D)
    grad_blocks = kv_grad.reshape(N_FSDP, TOK_DEV, 2 * kvw)
    prod_blocks = (hidden_grad * normed).reshape(N_FSDP, TOK_DEV, D)

    def add_block(carry, block):
        weight_sum, gain_sum = carry
        hidden_part, grad_part, prod_part = block
        weight_term = lax.dot_general(hidden_part, grad_part, (((0,), (0,)), ((), ())), preferred_element_type=jnp.float32) * scale
        gain_term = lax.optimization_barrier(jnp.sum(prod_part, axis=0)) * scale
        return ((weight_sum + weight_term, gain_sum + gain_term), None)
    start = (jnp.zeros((D, 2 * kvw), jnp.float32), jnp.zeros((D,), jnp.float32))
    (weight_grad, gain_grad), unused = lax.scan(add_block, start, (hidden_blocks, grad_blocks, prod_blocks))
    normed_grad = hidden_grad * gain_f
    input_grad = (inv_rms * (normed_grad - normed * lax.optimization_barrier(jnp.mean(normed_grad * normed, axis=-1, keepdims=True)))).astype(jnp.bfloat16)
    return (kv_out, input_grad, weight_grad, gain_grad)

def reference(layer_input, norm_gain, kv_weight, kv_cotangent, pseudo_grad, outer_momentum, global_params, local_params):
    kv_out, input_grad, weight_grad, gain_grad = lax.map(lambda group: inner_step(*group), (layer_input, norm_gain, kv_weight, kv_cotangent))
    average = lax.optimization_barrier(jnp.sum(pseudo_grad, axis=0)) / N_REPLICA
    momentum_new = momentum_rate * outer_momentum + average
    global_new = global_params - outer_rate * (average + momentum_rate * momentum_new)
    local_new = (mixing_rate * local_params.astype(jnp.float32) + (1.0 - mixing_rate) * global_new[None]).astype(jnp.bfloat16)
    return (kv_out, input_grad, weight_grad, gain_grad, momentum_new, global_new, local_new)
```

```python
import math

import jax
import jax.numpy as jnp
from jax import lax
from jax.sharding import PartitionSpec as P

HEAD = 128
SEQ_LEN = 4096


epsilon = 1e-05
rope_base = 500000.0
momentum_rate = 0.9
outer_rate = 0.7
mixing_rate = 0.5


def angles_for(positions, head):
    half = head // 2
    index_f = jnp.arange(half, dtype=jnp.float32)
    inverse = jnp.exp(index_f * (-2.0 * math.log(rope_base) / head))
    angle = positions.astype(jnp.float32)[:, None] * inverse[None, :]
    return (jnp.cos(angle), jnp.sin(angle))


def rotate_keys(keys, cosine, sine, head, sign):
    count = keys.shape[0]
    shaped = keys.reshape(count, -1, head)
    half = head // 2
    first = shaped[:, :, :half]
    second = shaped[:, :, half:]
    cos_b = cosine[:, None, :]
    sin_b = sine[:, None, :] * sign
    out = jnp.concatenate([first * cos_b - second * sin_b, second * cos_b + first * sin_b], axis=2)
    return out.reshape(count, -1)


class Grid:
    def __init__(self):
        self.groups = lax.axis_size("fsdp")
        self.line = self.groups // 2
        self.me = lax.axis_index("fsdp")
        self.place = self.me // 2
        self.side = self.me % 2

    def send(self, value, step, keep):
        pairs = [
            (i, i ^ 1 if step == 0 else i + 2 * step) for i in range(self.groups) if keep(i // 2)
        ]
        return lax.ppermute(value, "fsdp", pairs)

    def flip(self, value, keep=lambda p: True):
        return self.send(value, 0, keep)

    def block(self, distance):
        return (self.place + distance) % self.line


def gather_rows(grid, piece):
    n = grid.groups
    around = [piece] + [
        lax.ppermute(piece, "fsdp", [(i, (i - m) % n) for i in range(n)]) for m in range(1, n)
    ]
    twice = jnp.stack(around + around)
    return lax.dynamic_slice_in_dim(twice, (n - grid.me) % n, n, 0).reshape(-1)


def scatter_rows(grid, term):
    n = grid.groups
    pieces = term.reshape(n, -1)
    around = lax.dynamic_slice_in_dim(jnp.concatenate([pieces, pieces]), grid.me, n, 0)
    total = around[0]
    for m in range(1, n):
        total = total + lax.ppermute(around[m], "fsdp", [(i, (i + m) % n) for i in range(n)])
    return total


def gather_line(grid, block):
    last = grid.line - 1
    up, down = [block], [block]
    for s in range(1, grid.line):
        up.append(grid.send(up[-1], 1, lambda p: s - 1 <= p < last))
        down.append(grid.send(down[-1], -1, lambda p: 1 <= p <= grid.line - s))
    return up, down


def by_distance(grid, up, down):
    out = [up[0]]
    for r in range(1, grid.line):
        out.append(jnp.where(grid.place + r < grid.line, down[r], up[grid.line - r]))
    return out


def gather_weight(grid, weight, split):
    shard, cols = weight.shape
    part_a, part_b = weight[:, :split], weight[:, split:]
    last = grid.line - 1
    other_b = grid.flip(part_b)
    up_a, down_a = gather_line(grid, part_a)
    pair_b = jnp.concatenate(
        [
            jnp.where(grid.side == 0, part_b, other_b),
            jnp.where(grid.side == 0, other_b, part_b),
        ],
        axis=0,
    )
    up_b, down_b = gather_line(grid, pair_b)
    own = grid.flip(part_a)
    up_x, down_x = [own], [own]
    for s in range(1, grid.line):
        up_x.append(grid.flip(up_a[s], lambda p: p >= s))
        down_x.append(grid.flip(down_a[s], lambda p: p <= last - s))
    near = by_distance(grid, up_a, down_a)
    far = by_distance(grid, up_x, down_x)
    both = by_distance(grid, up_b, down_b)
    whole = jnp.zeros((grid.groups * shard, cols), weight.dtype)
    for r in range(grid.line):
        base = grid.block(r) * 2 * shard
        whole = lax.dynamic_update_slice(whole, near[r], (base + grid.side * shard, 0))
        whole = lax.dynamic_update_slice(whole, far[r], (base + (1 - grid.side) * shard, 0))
        whole = lax.dynamic_update_slice(whole, both[r], (base, split))
    return whole


def scatter_line(grid, terms):
    half = jnp.bfloat16
    up = down = None
    for s in range(grid.line - 1, 0, -1):
        mine_up, mine_down = terms(s), terms(grid.line - s)
        if up is not None:
            mine_up = mine_up + up.astype(jnp.float32)
            mine_down = mine_down + down.astype(jnp.float32)
        up = grid.send(mine_up.astype(half), 1, lambda p: p + s < grid.line)
        down = grid.send(mine_down.astype(half), -1, lambda p: p >= s)
    return terms(0) + up.astype(jnp.float32) + down.astype(jnp.float32)


def scatter_weight(grid, term, shard, split):
    cols = term.shape[1]

    def cut(r, side, first, last, count):
        start = grid.block(r) * 2 * shard + side * shard
        return lax.dynamic_slice(term, (start, first), (count * shard, last - first))

    order = []
    for s in range(grid.line - 1, 0, -1):
        order += [r for r in (s, grid.line - s) if r not in order]
    order.append(0)
    paired = {}
    for r in order:
        theirs = cut(r, 1 - grid.side, 0, split, 1).astype(jnp.bfloat16)
        paired[r] = cut(r, grid.side, 0, split, 1) + grid.flip(theirs).astype(jnp.float32)
    grad_a = scatter_line(grid, lambda r: paired[r])
    pair_b = scatter_line(grid, lambda r: cut(r, 0, split, cols, 2))
    mine = lax.dynamic_slice(pair_b, (grid.side * shard, 0), (shard, cols - split))
    theirs = lax.dynamic_slice(pair_b, ((1 - grid.side) * shard, 0), (shard, cols - split))
    grad_b = mine + grid.flip(theirs.astype(jnp.bfloat16)).astype(jnp.float32)
    return jnp.concatenate([grad_a, grad_b], axis=1)


def local(
    layer_input,
    norm_gain,
    kv_weight,
    kv_cotangent,
    pseudo_grad,
    outer_momentum,
    global_params,
    local_params,
):
    grid = Grid()
    tokens_in = layer_input[0]
    gain_shard = norm_gain[0]
    weight_shard = kv_weight[0]
    cotangent = kv_cotangent[0]
    rows, width = tokens_in.shape
    shard, cols = weight_shard.shape
    kvw = cols // 2
    split = cols * 5 // 8
    weight = gather_weight(grid, weight_shard, split)
    gain_full = gather_rows(grid, gain_shard).astype(jnp.float32)

    positions = (grid.me * rows + jnp.arange(rows, dtype=jnp.int32)) % SEQ_LEN
    cosine, sine = angles_for(positions, HEAD)
    values = tokens_in.astype(jnp.float32)
    inv_rms = lax.rsqrt(jnp.mean(values * values, axis=-1, keepdims=True) + epsilon)
    normed = values * inv_rms
    hidden = (normed * gain_full[None, :]).astype(jnp.bfloat16)
    key_back = rotate_keys(cotangent[:, :kvw].astype(jnp.float32), cosine, sine, HEAD, -1.0).astype(
        jnp.bfloat16
    )
    kv_grad = jnp.concatenate([key_back, cotangent[:, kvw:]], axis=1)
    scale = 1.0 / math.sqrt(rows * grid.groups)
    weight_term = (
        lax.dot_general(
            hidden, kv_grad, (((0,), (0,)), ((), ())), preferred_element_type=jnp.float32
        )
        * scale
    )
    weight_grad = scatter_weight(grid, weight_term, shard, split)

    key_pre = jnp.dot(hidden, weight, preferred_element_type=jnp.float32)
    kv_out = jnp.concatenate(
        [rotate_keys(key_pre[:, :kvw], cosine, sine, HEAD, 1.0), key_pre[:, kvw:]], axis=1
    ).astype(jnp.bfloat16)
    hidden_grad = lax.dot_general(
        kv_grad, weight, (((1,), (1,)), ((), ())), preferred_element_type=jnp.float32
    )
    gain_product = hidden_grad * normed
    gain_term = jnp.sum(gain_product, axis=0) * scale
    gain_grad = scatter_rows(grid, gain_term)
    normed_grad = hidden_grad * gain_full
    input_grad = (
        inv_rms * (normed_grad - normed * jnp.mean(normed_grad * normed, axis=-1, keepdims=True))
    ).astype(jnp.bfloat16)

    pseudo = pseudo_grad[0]
    replicas = lax.axis_size("replica")
    average = lax.psum(pseudo, "replica") / replicas
    momentum_new = momentum_rate * outer_momentum + average
    global_new = global_params - outer_rate * (average + momentum_rate * momentum_new)
    local_new = (
        mixing_rate * local_params[0].astype(jnp.float32) + (1.0 - mixing_rate) * global_new
    ).astype(jnp.bfloat16)
    return (
        kv_out[None],
        input_grad[None],
        weight_grad[None],
        gain_grad[None],
        momentum_new,
        global_new,
        local_new[None],
    )


def solution(mesh):
    in_specs = (
        P("replica", "fsdp", None),
        P("replica", "fsdp"),
        P("replica", "fsdp", None),
        P("replica", "fsdp", None),
        P("replica", "fsdp", None),
        P("fsdp", None),
        P("fsdp", None),
        P("replica", "fsdp", None),
    )
    out_specs = (
        P("replica", "fsdp", None),
        P("replica", "fsdp", None),
        P("replica", "fsdp", None),
        P("replica", "fsdp"),
        P("fsdp", None),
        P("fsdp", None),
        P("replica", "fsdp", None),
    )
    return jax.shard_map(local, mesh=mesh, in_specs=in_specs, out_specs=out_specs, check_vma=False)
```

```python
import functools
import math

import jax
import jax.numpy as jnp
from jax import lax
from jax.experimental import pallas as pl
from jax.experimental.pallas import tpu as pltpu
from jax.sharding import PartitionSpec as P

HEAD = 128
SEQ_LEN = 4096
PAD = 16


epsilon = 1e-05
rope_base = 500000.0
momentum_rate = 0.9
outer_rate = 0.7
mixing_rate = 0.5

f32, bf16 = jnp.float32, jnp.bfloat16


class Ring:
    def __init__(self):
        self.count = lax.axis_size("fsdp")
        self.half = self.count // 2
        walk = list(range(0, self.count, 2)) + list(range(self.count - 1, 0, -2))
        after = walk[1:] + walk[:1]
        self.right = list(zip(walk, after))
        self.left = list(zip(after, walk))
        self.me = lax.axis_index("fsdp")
        self.spot = jnp.where(
            self.me % 2 == 0, self.me // 2, self.count - 1 - self.me // 2
        )

    def devices_at(self, distances):
        spot = (self.spot + self.count + jnp.array(distances, jnp.int32)) % self.count
        return jnp.where(spot < self.half, 2 * spot, 2 * (self.count - 1 - spot) + 1)

    def to_right(self, value):
        return lax.ppermute(value, "fsdp", self.right)

    def to_left(self, value):
        return lax.ppermute(value, "fsdp", self.left)


def rope_tables(positions):
    half = HEAD // 2
    index_f = jnp.arange(half, dtype=f32)
    inverse = jnp.exp(index_f * (-2.0 * math.log(rope_base) / HEAD))
    angle = positions.astype(f32)[:, None] * inverse[None, :]
    cosine, sine = jnp.cos(angle), jnp.sin(angle)
    return jnp.concatenate([cosine, cosine], axis=1), jnp.concatenate([-sine, sine], axis=1)


def first_kernel(scale, at, x, cotangent, cosine, sine, kv_grad, inv, far, near):
    step = pl.program_id(0)
    width = x.shape[1]
    shard = far.shape[0]
    kvw = cotangent.shape[1] // 2

    @pl.when(step == 0)
    def _():
        total = jnp.zeros((x.shape[0], HEAD), f32)
        for c in range(0, width, HEAD):
            part = x[:, c : c + HEAD].astype(f32)
            total = total + part * part
        mean = jnp.sum(total, axis=1, keepdims=True) / width
        inv[...] = jnp.broadcast_to(lax.rsqrt(mean + epsilon), inv.shape)
        for c in range(0, kvw, HEAD):
            part = cotangent[:, c : c + HEAD].astype(f32)
            turned = pltpu.roll(part, HEAD // 2, 1)
            kv_grad[:, c : c + HEAD] = (part * cosine[...] - turned * sine[...]).astype(bf16)
        kv_grad[:, kvw:] = cotangent[:, kvw:]

    block = x[:, pl.ds(pl.multiple_of(at[step] * shard, shard), shard)]
    normed = (block.astype(f32) * inv[:, :1]).astype(bf16)
    term = (
        lax.dot_general(normed, kv_grad[...], (((0,), (0,)), ((), ())), preferred_element_type=f32)
        * scale
    )

    @pl.when(step == 0)
    def _():
        far[...] = term.astype(bf16)

    @pl.when(step > 0)
    def _():
        near[0] = term


def first_part(ring, tokens_in, cotangent, cosine, sine, shard, scale):
    rows, width = tokens_in.shape
    cols = cotangent.shape[1]
    order = [ring.half]
    for d in range(ring.half - 1, 0, -1):
        order += [d, -d]
    order.append(0)
    n = ring.count
    fixed = lambda k, at: (0, 0)
    return pl.pallas_call(
        functools.partial(first_kernel, scale),
        grid_spec=pltpu.PrefetchScalarGridSpec(
            num_scalar_prefetch=1,
            grid=(n,),
            in_specs=[
                pl.BlockSpec((rows, width), fixed),
                pl.BlockSpec((rows, cols), fixed),
                pl.BlockSpec((rows, HEAD), fixed),
                pl.BlockSpec((rows, HEAD), fixed),
            ],
            out_specs=[
                pl.BlockSpec((rows, cols), fixed),
                pl.BlockSpec((rows, HEAD), fixed),
                pl.BlockSpec((shard, cols), fixed),
                pl.BlockSpec((1, shard, cols), lambda k, at: (jnp.maximum(k - 1, 0), 0, 0)),
            ],
        ),
        out_shape=[
            jax.ShapeDtypeStruct((rows, cols), bf16),
            jax.ShapeDtypeStruct((rows, HEAD), f32),
            jax.ShapeDtypeStruct((shard, cols), bf16),
            jax.ShapeDtypeStruct((n - 1, shard, cols), f32),
        ],
        compiler_params=pltpu.CompilerParams(vmem_limit_bytes=40 * 2**20),
        cost_estimate=pl.CostEstimate(
            flops=2 * rows * width * cols,
            bytes_accessed=2 * rows * width + 4 * width * cols,
            transcendentals=0,
        ),
        name="norm_and_weight_terms",
    )(ring.devices_at(order), tokens_in, cotangent, cosine, sine)


def second_kernel(n, at, x, kv_grad, inv, cosine, sine, *refs):
    blocks, refs = refs[: n + 1], refs[n + 1 :]
    kv_out, input_grad, xs, ws, ng, pre, out, x_sem, w_sem, o_sem = refs
    rows, width = x.shape
    shard = xs.shape[2]
    cols = pre.shape[1]
    kvw = cols // 2
    cut = shard // 2

    def columns(k):
        return pl.ds(pl.multiple_of(at[k] * shard, shard), shard)

    def x_copy(k):
        return pltpu.make_async_copy(x.at[:, columns(k)], xs.at[k], x_sem.at[k])

    def o_copy(k):
        return pltpu.make_async_copy(out.at[k], input_grad.at[:, columns(k)], o_sem.at[k])

    for k in range(n):
        x_copy(k).start()
        if k < n - 1:
            pltpu.make_async_copy(blocks[k], ws.at[k], w_sem.at[k]).start()
        else:
            pltpu.make_async_copy(blocks[k], ws.at[k, :cut], w_sem.at[k]).start()
            pltpu.make_async_copy(blocks[k + 1], ws.at[k, cut:], w_sem.at[k]).start()

    pre[...] = jnp.zeros_like(pre)

    def gather(k, total):
        x_copy(k).wait()
        pltpu.make_async_copy(ws.at[k], ws.at[k], w_sem.at[k]).wait()
        weight = ws[k, :shard, :]
        gain = ws[k, shard : shard + PAD, :shard].astype(f32)[:1]
        normed = xs[k].astype(f32) * inv[:, :1]
        hidden = (normed * gain).astype(bf16)
        pre[...] += jnp.dot(hidden, weight, preferred_element_type=f32)
        grad = (
            lax.dot_general(
                kv_grad[...], weight, (((1,), (1,)), ((), ())), preferred_element_type=f32
            )
            * gain
        )
        ng[k] = grad
        product = grad * normed
        for c in range(0, shard, HEAD):
            total = total + product[:, c : c + HEAD]
        return total

    total = lax.fori_loop(0, n, gather, jnp.zeros((rows, HEAD), f32))
    mean = jnp.sum(total, axis=1, keepdims=True) / width

    def finish(k, carry):
        scale = inv[:, :1]
        normed = xs[k].astype(f32) * scale
        out[k] = (scale * (ng[k] - normed * mean)).astype(bf16)
        o_copy(k).start()
        return carry

    lax.fori_loop(0, n, finish, 0)
    for c in range(0, kvw, HEAD):
        part = pre[:, c : c + HEAD]
        turned = pltpu.roll(part, HEAD // 2, 1)
        kv_out[:, c : c + HEAD] = (part * cosine[...] + turned * sine[...]).astype(bf16)
    kv_out[:, kvw:] = pre[:, kvw:].astype(bf16)

    def drain(k, carry):
        o_copy(k).wait()
        return carry

    lax.fori_loop(0, n, drain, 0)


def second_part(ring, tokens_in, kv_grad, inv, cosine, sine, blocks, shard):
    rows, width = tokens_in.shape
    cols = kv_grad.shape[1]
    n = ring.count
    order = [0]
    for d in range(1, ring.half):
        order += [-d, d]
    order.append(ring.half)
    whole = pl.BlockSpec(memory_space=pltpu.VMEM)
    there = pl.BlockSpec(memory_space=pl.ANY)
    return pl.pallas_call(
        functools.partial(second_kernel, n),
        in_specs=[pl.BlockSpec(memory_space=pltpu.SMEM), there]
        + [whole] * 4
        + [there] * len(blocks),
        out_specs=[whole, there],
        out_shape=[
            jax.ShapeDtypeStruct((rows, cols), bf16),
            jax.ShapeDtypeStruct((rows, width), bf16),
        ],
        scratch_shapes=[
            pltpu.VMEM((n, rows, shard), bf16),
            pltpu.VMEM((n, shard + PAD, cols), bf16),
            pltpu.VMEM((n, rows, shard), f32),
            pltpu.VMEM((rows, cols), f32),
            pltpu.VMEM((n, rows, shard), bf16),
            pltpu.SemaphoreType.DMA((n,)),
            pltpu.SemaphoreType.DMA((n,)),
            pltpu.SemaphoreType.DMA((n,)),
        ],
        compiler_params=pltpu.CompilerParams(vmem_limit_bytes=48 * 2**20),
        cost_estimate=pl.CostEstimate(
            flops=4 * rows * width * cols,
            bytes_accessed=4 * rows * width + 2 * width * cols,
            transcendentals=0,
        ),
        name="project_and_input_grad",
    )(ring.devices_at(order), tokens_in, kv_grad, inv, cosine, sine, *blocks)


def gather_blocks(ring, own, cut):
    blocks = [own]
    from_left = from_right = own
    for d in range(1, ring.half):
        from_left, from_right = ring.to_right(from_left), ring.to_left(from_right)
        blocks += [from_left, from_right]
    blocks += [ring.to_right(from_left[:cut]), ring.to_left(from_right[cut:])]
    return blocks


def scatter_terms(ring, far, near, cut):
    rest = far.shape[0] - cut
    from_left = ring.to_right(far[:cut]).astype(f32)
    from_right = ring.to_left(far[cut:]).astype(f32)
    from_left = jnp.pad(from_left, ((0, rest), (0, 0)))
    from_right = jnp.pad(from_right, ((cut, 0), (0, 0)))
    for k in range(0, 2 * (ring.half - 1), 2):
        from_left = ring.to_right((near[k] + from_left).astype(bf16)).astype(f32)
        from_right = ring.to_left((near[k + 1] + from_right).astype(bf16)).astype(f32)
    return near[-1] + from_left + from_right


def local(
    layer_input,
    norm_gain,
    kv_weight,
    kv_cotangent,
    pseudo_grad,
    outer_momentum,
    global_params,
    local_params,
):
    ring = Ring()
    tokens_in = layer_input[0]
    gain_shard = norm_gain[0]
    weight_shard = kv_weight[0]
    cotangent = kv_cotangent[0]
    rows, width = tokens_in.shape
    shard, cols = weight_shard.shape

    gain_rows = jnp.pad(gain_shard[None, :], ((0, PAD - 1), (0, cols - shard)))
    own = jnp.concatenate([weight_shard, gain_rows], axis=0)
    blocks = gather_blocks(ring, own, shard // 2)

    positions = (ring.me * rows + jnp.arange(rows, dtype=jnp.int32)) % SEQ_LEN
    cosine, sine = rope_tables(positions)
    scale = 1.0 / math.sqrt(rows * ring.count)
    kv_grad, inv, far, near = first_part(
        ring, tokens_in, cotangent, cosine, sine, shard, scale
    )
    term = scatter_terms(ring, far, near, shard // 2)
    weight_grad = term * gain_shard.astype(f32)[:, None]
    gain_grad = jnp.sum(term * weight_shard.astype(f32), axis=1)

    replicas = lax.axis_size("replica")
    average = lax.psum(pseudo_grad[0], "replica") / replicas
    momentum_new = momentum_rate * outer_momentum + average
    global_new = global_params - outer_rate * (average + momentum_rate * momentum_new)
    local_new = (
        mixing_rate * local_params[0].astype(f32) + (1.0 - mixing_rate) * global_new
    ).astype(bf16)

    kv_out, input_grad = second_part(
        ring, tokens_in, kv_grad, inv, cosine, sine, blocks, shard
    )
    return (
        kv_out[None],
        input_grad[None],
        weight_grad[None],
        gain_grad[None],
        momentum_new,
        global_new,
        local_new[None],
    )


def solution(mesh):
    in_specs = (
        P("replica", "fsdp", None),
        P("replica", "fsdp"),
        P("replica", "fsdp", None),
        P("replica", "fsdp", None),
        P("replica", "fsdp", None),
        P("fsdp", None),
        P("fsdp", None),
        P("replica", "fsdp", None),
    )
    out_specs = (
        P("replica", "fsdp", None),
        P("replica", "fsdp", None),
        P("replica", "fsdp", None),
        P("replica", "fsdp"),
        P("fsdp", None),
        P("fsdp", None),
        P("replica", "fsdp", None),
    )
    return jax.shard_map(local, mesh=mesh, in_specs=in_specs, out_specs=out_specs, check_vma=False)
```

```python
import functools
import math

import jax
import jax.numpy as jnp
from jax import lax
from jax.experimental import pallas as pl
from jax.experimental.pallas import tpu as pltpu
from jax.sharding import PartitionSpec as P

HEAD = 128
SEQ_LEN = 4096
PAD = 16


epsilon = 1e-05
rope_base = 500000.0
momentum_rate = 0.9
outer_rate = 0.7
mixing_rate = 0.5

f32, bf16 = jnp.float32, jnp.bfloat16


class Ring:
    def __init__(self):
        self.count = lax.axis_size("fsdp")
        self.half = self.count // 2
        walk = list(range(0, self.count, 2)) + list(range(self.count - 1, 0, -2))
        after = walk[1:] + walk[:1]
        self.right = list(zip(walk, after))
        self.left = list(zip(after, walk))
        self.me = lax.axis_index("fsdp")
        self.spot = jnp.where(
            self.me % 2 == 0, self.me // 2, self.count - 1 - self.me // 2
        )

    def devices_at(self, distances):
        spot = (self.spot + self.count + jnp.array(distances, jnp.int32)) % self.count
        return jnp.where(spot < self.half, 2 * spot, 2 * (self.count - 1 - spot) + 1)

    def to_right(self, value):
        return lax.ppermute(value, "fsdp", self.right)

    def to_left(self, value):
        return lax.ppermute(value, "fsdp", self.left)


def after(value, *others):
    return lax.optimization_barrier((value, others))[0]


def rope_tables(positions):
    half = HEAD // 2
    index_f = jnp.arange(half, dtype=f32)
    inverse = jnp.exp(index_f * (-2.0 * math.log(rope_base) / HEAD))
    angle = positions.astype(f32)[:, None] * inverse[None, :]
    cosine, sine = jnp.cos(angle), jnp.sin(angle)
    return jnp.concatenate([cosine, cosine], axis=1), jnp.concatenate([-sine, sine], axis=1)


def first_kernel(scale, at, x, cotangent, cosine, sine, kv_grad, inv, top, bottom, near):
    step = pl.program_id(0)
    width = x.shape[1]
    shard, cut = near.shape[1], top.shape[0]
    kvw = cotangent.shape[1] // 2

    @pl.when(step == 0)
    def _():
        total = jnp.zeros((x.shape[0], HEAD), f32)
        for c in range(0, width, HEAD):
            part = x[:, c : c + HEAD].astype(f32)
            total = total + part * part
        mean = jnp.sum(total, axis=1, keepdims=True) / width
        inv[...] = jnp.broadcast_to(lax.rsqrt(mean + epsilon), inv.shape)
        for c in range(0, kvw, HEAD):
            part = cotangent[:, c : c + HEAD].astype(f32)
            turned = pltpu.roll(part, HEAD // 2, 1)
            kv_grad[:, c : c + HEAD] = (part * cosine[...] - turned * sine[...]).astype(bf16)
        kv_grad[:, kvw:] = cotangent[:, kvw:]

    block = x[:, pl.ds(pl.multiple_of(at[step] * shard, shard), shard)]
    normed = (block.astype(f32) * inv[:, :1]).astype(bf16)
    term = (
        lax.dot_general(normed, kv_grad[...], (((0,), (0,)), ((), ())), preferred_element_type=f32)
        * scale
    )

    @pl.when(step == 0)
    def _():
        top[...] = term[:cut].astype(bf16)
        bottom[...] = term[cut:].astype(bf16)

    @pl.when(step > 0)
    def _():
        near[0] = term


def first_part(ring, tokens_in, cotangent, cosine, sine, shard, scale):
    rows, width = tokens_in.shape
    cols = cotangent.shape[1]
    order = [ring.half]
    for d in range(ring.half - 1, 0, -1):
        order += [d, -d]
    order.append(0)
    n = ring.count
    fixed = lambda k, at: (0, 0)
    return pl.pallas_call(
        functools.partial(first_kernel, scale),
        grid_spec=pltpu.PrefetchScalarGridSpec(
            num_scalar_prefetch=1,
            grid=(n,),
            in_specs=[
                pl.BlockSpec((rows, width), fixed),
                pl.BlockSpec((rows, cols), fixed),
                pl.BlockSpec((rows, HEAD), fixed),
                pl.BlockSpec((rows, HEAD), fixed),
            ],
            out_specs=[
                pl.BlockSpec((rows, cols), fixed),
                pl.BlockSpec((rows, HEAD), fixed),
                pl.BlockSpec((shard // 2, cols), fixed),
                pl.BlockSpec((shard - shard // 2, cols), fixed),
                pl.BlockSpec((1, shard, cols), lambda k, at: (jnp.maximum(k - 1, 0), 0, 0)),
            ],
        ),
        out_shape=[
            jax.ShapeDtypeStruct((rows, cols), bf16),
            jax.ShapeDtypeStruct((rows, HEAD), f32),
            jax.ShapeDtypeStruct((shard // 2, cols), bf16),
            jax.ShapeDtypeStruct((shard - shard // 2, cols), bf16),
            jax.ShapeDtypeStruct((n - 1, shard, cols), f32),
        ],
        compiler_params=pltpu.CompilerParams(vmem_limit_bytes=40 * 2**20),
        cost_estimate=pl.CostEstimate(
            flops=2 * rows * width * cols,
            bytes_accessed=2 * rows * width + 4 * width * cols,
            transcendentals=0,
        ),
        name="norm_and_weight_terms",
    )(ring.devices_at(order), tokens_in, cotangent, cosine, sine)


def second_kernel(n, at, x, kv_grad, inv, cosine, sine, *refs):
    blocks, refs = refs[: n + 1], refs[n + 1 :]
    kv_out, input_grad, xs, ws, ng, pre, out, x_sem, w_sem, o_sem = refs
    rows, width = x.shape
    shard = xs.shape[2]
    cols = pre.shape[1]
    kvw = cols // 2
    cut = shard // 2

    def columns(k):
        return pl.ds(pl.multiple_of(at[k] * shard, shard), shard)

    def x_copy(k):
        return pltpu.make_async_copy(x.at[:, columns(k)], xs.at[k], x_sem.at[k])

    def o_copy(k):
        return pltpu.make_async_copy(out.at[k], input_grad.at[:, columns(k)], o_sem.at[k])

    for k in range(n):
        x_copy(k).start()
        if k < n - 1:
            pltpu.make_async_copy(blocks[k], ws.at[k], w_sem.at[k]).start()
        else:
            pltpu.make_async_copy(blocks[k], ws.at[k, :cut], w_sem.at[k]).start()
            pltpu.make_async_copy(blocks[k + 1], ws.at[k, cut:], w_sem.at[k]).start()

    pre[...] = jnp.zeros_like(pre)

    def gather(k, total):
        x_copy(k).wait()
        pltpu.make_async_copy(ws.at[k], ws.at[k], w_sem.at[k]).wait()
        weight = ws[k, :shard, :]
        gain = ws[k, shard : shard + PAD, :shard].astype(f32)[:1]
        normed = xs[k].astype(f32) * inv[:, :1]
        hidden = (normed * gain).astype(bf16)
        pre[...] += jnp.dot(hidden, weight, preferred_element_type=f32)
        grad = (
            lax.dot_general(
                kv_grad[...], weight, (((1,), (1,)), ((), ())), preferred_element_type=f32
            )
            * gain
        )
        ng[k] = grad
        product = grad * normed
        for c in range(0, shard, HEAD):
            total = total + product[:, c : c + HEAD]
        return total

    total = lax.fori_loop(0, n, gather, jnp.zeros((rows, HEAD), f32))
    mean = jnp.sum(total, axis=1, keepdims=True) / width

    def finish(k, carry):
        scale = inv[:, :1]
        normed = xs[k].astype(f32) * scale
        out[k] = (scale * (ng[k] - normed * mean)).astype(bf16)
        o_copy(k).start()
        return carry

    lax.fori_loop(0, n, finish, 0)
    for c in range(0, kvw, HEAD):
        part = pre[:, c : c + HEAD]
        turned = pltpu.roll(part, HEAD // 2, 1)
        kv_out[:, c : c + HEAD] = (part * cosine[...] + turned * sine[...]).astype(bf16)
    kv_out[:, kvw:] = pre[:, kvw:].astype(bf16)

    def drain(k, carry):
        o_copy(k).wait()
        return carry

    lax.fori_loop(0, n, drain, 0)


def second_part(ring, tokens_in, kv_grad, inv, cosine, sine, blocks, shard):
    rows, width = tokens_in.shape
    cols = kv_grad.shape[1]
    n = ring.count
    order = [0]
    for d in range(1, ring.half):
        order += [-d, d]
    order.append(ring.half)
    whole = pl.BlockSpec(memory_space=pltpu.VMEM)
    there = pl.BlockSpec(memory_space=pl.ANY)
    return pl.pallas_call(
        functools.partial(second_kernel, n),
        in_specs=[pl.BlockSpec(memory_space=pltpu.SMEM), there]
        + [whole] * 4
        + [there] * len(blocks),
        out_specs=[whole, there],
        out_shape=[
            jax.ShapeDtypeStruct((rows, cols), bf16),
            jax.ShapeDtypeStruct((rows, width), bf16),
        ],
        scratch_shapes=[
            pltpu.VMEM((n, rows, shard), bf16),
            pltpu.VMEM((n, shard + PAD, cols), bf16),
            pltpu.VMEM((n, rows, shard), f32),
            pltpu.VMEM((rows, cols), f32),
            pltpu.VMEM((n, rows, shard), bf16),
            pltpu.SemaphoreType.DMA((n,)),
            pltpu.SemaphoreType.DMA((n,)),
            pltpu.SemaphoreType.DMA((n,)),
        ],
        compiler_params=pltpu.CompilerParams(vmem_limit_bytes=48 * 2**20),
        cost_estimate=pl.CostEstimate(
            flops=4 * rows * width * cols,
            bytes_accessed=4 * rows * width + 2 * width * cols,
            transcendentals=0,
        ),
        name="project_and_input_grad",
    )(ring.devices_at(order), tokens_in, kv_grad, inv, cosine, sine, *blocks)


def replica_sum(value):
    replicas = lax.axis_size("replica")
    if replicas & (replicas - 1):
        return lax.psum(value, "replica")
    step = 1
    while step < replicas:
        pairs = [(r, r ^ step) for r in range(replicas)]
        value = value + lax.ppermute(value, "replica", pairs)
        step *= 2
    return value


def gather_blocks(ring, own, cut, other):
    blocks = [own]
    from_left = from_right = own
    for d in range(1, ring.half):
        from_left, from_right = ring.to_right(from_left), ring.to_left(from_right)
        blocks += [from_left, from_right]
    from_left, from_right = after(from_left, other), after(from_right, other)
    blocks += [ring.to_right(from_left[:cut]), ring.to_left(from_right[cut:])]
    return blocks


def scatter_terms(ring, top, bottom, near):
    cut, rest = top.shape[0], bottom.shape[0]
    from_left, from_right = ring.to_right(top), ring.to_left(bottom)
    for k in range(0, 2 * (ring.half - 1), 2):
        from_left, from_right = lax.optimization_barrier((from_left, from_right))
        if k == 0:
            from_left = jnp.pad(from_left, ((0, rest), (0, 0)))
            from_right = jnp.pad(from_right, ((cut, 0), (0, 0)))
        from_left = ring.to_right((near[k] + from_left.astype(f32)).astype(bf16))
        from_right = ring.to_left((near[k + 1] + from_right.astype(f32)).astype(bf16))
    from_left, from_right = from_left.astype(f32), from_right.astype(f32)
    return near[-1] + from_left + from_right


def local(
    layer_input,
    norm_gain,
    kv_weight,
    kv_cotangent,
    pseudo_grad,
    outer_momentum,
    global_params,
    local_params,
):
    ring = Ring()
    tokens_in = layer_input[0]
    gain_shard = norm_gain[0]
    weight_shard = kv_weight[0]
    cotangent = kv_cotangent[0]
    rows, width = tokens_in.shape
    shard, cols = weight_shard.shape

    gain_rows = jnp.pad(gain_shard[None, :], ((0, PAD - 1), (0, cols - shard)))
    own = jnp.concatenate([weight_shard, gain_rows], axis=0)
    total = replica_sum(pseudo_grad[0])
    blocks = gather_blocks(ring, own, shard // 2, total)

    positions = (ring.me * rows + jnp.arange(rows, dtype=jnp.int32)) % SEQ_LEN
    cosine, sine = rope_tables(positions)
    scale = 1.0 / math.sqrt(rows * ring.count)
    kv_grad, inv, top, bottom, near = first_part(
        ring, tokens_in, cotangent, cosine, sine, shard, scale
    )
    top, bottom = after((top, bottom), blocks[1], blocks[2])
    term = scatter_terms(ring, top, bottom, near)
    weight_grad = term * gain_shard.astype(f32)[:, None]
    gain_grad = jnp.sum(term * weight_shard.astype(f32), axis=1)

    replicas = lax.axis_size("replica")
    average = total / replicas
    momentum_new = momentum_rate * outer_momentum + average
    global_new = global_params - outer_rate * (average + momentum_rate * momentum_new)
    local_new = (
        mixing_rate * local_params[0].astype(f32) + (1.0 - mixing_rate) * global_new
    ).astype(bf16)

    kv_out, input_grad = second_part(
        ring, tokens_in, kv_grad, inv, cosine, sine, blocks, shard
    )
    return (
        kv_out[None],
        input_grad[None],
        weight_grad[None],
        gain_grad[None],
        momentum_new,
        global_new,
        local_new[None],
    )


def solution(mesh):
    in_specs = (
        P("replica", "fsdp", None),
        P("replica", "fsdp"),
        P("replica", "fsdp", None),
        P("replica", "fsdp", None),
        P("replica", "fsdp", None),
        P("fsdp", None),
        P("fsdp", None),
        P("replica", "fsdp", None),
    )
    out_specs = (
        P("replica", "fsdp", None),
        P("replica", "fsdp", None),
        P("replica", "fsdp", None),
        P("replica", "fsdp"),
        P("fsdp", None),
        P("fsdp", None),
        P("replica", "fsdp", None),
    )
    return jax.shard_map(local, mesh=mesh, in_specs=in_specs, out_specs=out_specs, check_vma=False)
```

```python
import functools
import math

import jax
import jax.numpy as jnp
from jax import lax
from jax.experimental import pallas as pl
from jax.experimental.pallas import tpu as pltpu
from jax.sharding import PartitionSpec as P

HEAD = 128
SEQ_LEN = 4096
PAD = 16


epsilon = 1e-05
rope_base = 500000.0
momentum_rate = 0.9
outer_rate = 0.7
mixing_rate = 0.5

f32, bf16 = jnp.float32, jnp.bfloat16


class Plane:
    def __init__(self):
        self.count = lax.axis_size("fsdp")
        self.line = self.count // 2
        self.me = lax.axis_index("fsdp")
        self.place, self.side = self.me // 2, self.me % 2

    def device(self, distance, other):
        return (self.place + distance) % self.line * 2 + (self.side + other) % 2

    def up(self, value, first, last):
        pairs = [(2 * p + i, 2 * p + 2 + i) for p in range(first, last + 1) for i in range(2)]
        return lax.ppermute(value, "fsdp", pairs)

    def down(self, value, first, last):
        pairs = [(2 * p + i, 2 * p - 2 + i) for p in range(first, last + 1) for i in range(2)]
        return lax.ppermute(value, "fsdp", pairs)

    def flip(self, value, first, last):
        pairs = [(2 * p + i, 2 * p + 1 - i) for p in range(first, last + 1) for i in range(2)]
        return lax.ppermute(value, "fsdp", pairs)


def after(value, *others):
    return lax.optimization_barrier((value, others))[0]


def rope_tables(positions):
    half = HEAD // 2
    index_f = jnp.arange(half, dtype=f32)
    inverse = jnp.exp(index_f * (-2.0 * math.log(rope_base) / HEAD))
    angle = positions.astype(f32)[:, None] * inverse[None, :]
    cosine, sine = jnp.cos(angle), jnp.sin(angle)
    return jnp.concatenate([cosine, cosine], axis=1), jnp.concatenate([-sine, sine], axis=1)


def first_kernel(scale, line, at, x, cotangent, cosine, sine, kv_grad, inv, near_a, near_b, *far_a):
    step = pl.program_id(0)
    width = x.shape[1]
    cut, rest = near_a.shape[1], near_b.shape[2]
    shard = cut + rest
    kvw = cotangent.shape[1] // 2

    @pl.when(step == 0)
    def _():
        total = jnp.zeros((x.shape[0], HEAD), f32)
        for c in range(0, width, HEAD):
            part = x[:, c : c + HEAD].astype(f32)
            total = total + part * part
        mean = jnp.sum(total, axis=1, keepdims=True) / width
        inv[...] = jnp.broadcast_to(lax.rsqrt(mean + epsilon), inv.shape)
        for c in range(0, kvw, HEAD):
            part = cotangent[:, c : c + HEAD].astype(f32)
            turned = pltpu.roll(part, HEAD // 2, 1)
            kv_grad[:, c : c + HEAD] = (part * cosine[...] - turned * sine[...]).astype(bf16)
        kv_grad[:, kvw:] = cotangent[:, kvw:]

    block = x[:, pl.ds(pl.multiple_of(at[step] * shard, shard), shard)]
    normed = (block.astype(f32) * inv[:, :1]).astype(bf16)
    term = (
        lax.dot_general(normed, kv_grad[...], (((0,), (0,)), ((), ())), preferred_element_type=f32)
        * scale
    )
    near_b[0, 0] = term[cut:]

    @pl.when(step % 2 == 0)
    def _():
        near_a[0] = term[:cut]

    for j in range(line):

        @pl.when(step == 2 * j + 1)
        def _(j=j):
            far_a[j][...] = term[:cut].astype(bf16)


def first_part(plane, tokens_in, cotangent, cosine, sine, shard, cut, distances, scale):
    rows, width = tokens_in.shape
    cols = cotangent.shape[1]
    line, rest = plane.line, shard - cut
    at = jnp.stack([plane.device(r, e) for r in distances for e in range(2)]).astype(jnp.int32)
    fixed = lambda k, at: (0, 0)
    outs = pl.pallas_call(
        functools.partial(first_kernel, scale, line),
        grid_spec=pltpu.PrefetchScalarGridSpec(
            num_scalar_prefetch=1,
            grid=(2 * line,),
            in_specs=[
                pl.BlockSpec((rows, width), fixed),
                pl.BlockSpec((rows, cols), fixed),
                pl.BlockSpec((rows, HEAD), fixed),
                pl.BlockSpec((rows, HEAD), fixed),
            ],
            out_specs=[
                pl.BlockSpec((rows, cols), fixed),
                pl.BlockSpec((rows, HEAD), fixed),
                pl.BlockSpec((1, cut, cols), lambda k, at: (k // 2, 0, 0)),
                pl.BlockSpec((1, 1, rest, cols), lambda k, at: (k // 2, k % 2, 0, 0)),
            ]
            + [pl.BlockSpec((cut, cols), fixed)] * line,
        ),
        out_shape=[
            jax.ShapeDtypeStruct((rows, cols), bf16),
            jax.ShapeDtypeStruct((rows, HEAD), f32),
            jax.ShapeDtypeStruct((line, cut, cols), f32),
            jax.ShapeDtypeStruct((line, 2, rest, cols), f32),
        ]
        + [jax.ShapeDtypeStruct((cut, cols), bf16)] * line,
        compiler_params=pltpu.CompilerParams(vmem_limit_bytes=40 * 2**20),
        cost_estimate=pl.CostEstimate(
            flops=2 * rows * width * cols,
            bytes_accessed=2 * rows * width + 4 * width * cols,
            transcendentals=0,
        ),
        name="norm_and_weight_terms",
    )(at, tokens_in, cotangent, cosine, sine)
    kv_grad, inv, near_a, near_b, *far_a = outs
    place = {r: j for j, r in enumerate(distances)}
    near_a = {r: near_a[j] for r, j in place.items()}
    near_b = {r: near_b[j].reshape(2 * rest, cols) for r, j in place.items()}
    return kv_grad, inv, near_a, near_b, {r: far_a[j] for r, j in place.items()}


def second_kernel(line, at, x, kv_grad, inv, cosine, sine, *refs):
    n = 2 * line
    own_a, own_x, own_b = refs[:3]
    up_a, down_a, up_x, down_x, up_b, down_b = [
        (None,) + refs[3 + i * (line - 1) : 3 + (i + 1) * (line - 1)] for i in range(6)
    ]
    kv_out, input_grad, xs, ws, ng, pre, out, x_sem, w_sem, o_sem = refs[3 + 6 * (line - 1) :]
    rows, width = x.shape
    shard = xs.shape[2]
    cols = pre.shape[1]
    kvw = cols // 2
    cut, rest = own_a.shape[0], own_b.shape[0] // 2

    def columns(k):
        return pl.ds(pl.multiple_of(at[k] * shard, shard), shard)

    def x_copy(k):
        return pltpu.make_async_copy(x.at[:, columns(k)], xs.at[k], x_sem.at[k])

    def o_copy(k):
        return pltpu.make_async_copy(out.at[k], input_grad.at[:, columns(k)], o_sem.at[k])

    def w_start(k, near, far, both):
        for e, part in enumerate((near, far)):
            sem = w_sem.at[k + e]
            pltpu.make_async_copy(part, ws.at[k + e, :cut], sem).start()
            half = both.at[e * rest : (e + 1) * rest]
            pltpu.make_async_copy(half, ws.at[k + e, cut:], sem).start()

    for r in range(line):
        x_copy(2 * r).start()
        x_copy(2 * r + 1).start()
        if r == 0:
            w_start(0, own_a, own_x, own_b)
        else:
            above = at[n] + r < line

            @pl.when(above)
            def _():
                w_start(2 * r, down_a[r], down_x[r], down_b[r])

            @pl.when(jnp.logical_not(above))
            def _():
                w_start(2 * r, up_a[line - r], up_x[line - r], up_b[line - r])

    pre[...] = jnp.zeros_like(pre)

    def gather(k, total):
        x_copy(k).wait()
        pltpu.make_async_copy(ws.at[k], ws.at[k], w_sem.at[k]).wait()
        weight = ws[k, :shard, :]
        gain = ws[k, shard : shard + PAD, :shard].astype(f32)[:1]
        normed = xs[k].astype(f32) * inv[:, :1]
        hidden = (normed * gain).astype(bf16)
        pre[...] += jnp.dot(hidden, weight, preferred_element_type=f32)
        grad = (
            lax.dot_general(
                kv_grad[...], weight, (((1,), (1,)), ((), ())), preferred_element_type=f32
            )
            * gain
        )
        ng[k] = grad
        product = grad * normed
        for c in range(0, shard, HEAD):
            total = total + product[:, c : c + HEAD]
        return total

    total = lax.fori_loop(0, n, gather, jnp.zeros((rows, HEAD), f32))
    mean = jnp.sum(total, axis=1, keepdims=True) / width

    def finish(k, carry):
        scale = inv[:, :1]
        normed = xs[k].astype(f32) * scale
        out[k] = (scale * (ng[k] - normed * mean)).astype(bf16)
        o_copy(k).start()
        return carry

    lax.fori_loop(0, n, finish, 0)
    for c in range(0, kvw, HEAD):
        part = pre[:, c : c + HEAD]
        turned = pltpu.roll(part, HEAD // 2, 1)
        kv_out[:, c : c + HEAD] = (part * cosine[...] + turned * sine[...]).astype(bf16)
    kv_out[:, kvw:] = pre[:, kvw:].astype(bf16)

    def drain(k, carry):
        o_copy(k).wait()
        return carry

    lax.fori_loop(0, n, drain, 0)


def second_part(plane, tokens_in, kv_grad, inv, cosine, sine, blocks, shard):
    rows, width = tokens_in.shape
    cols = kv_grad.shape[1]
    n = plane.count
    at = [plane.device(r, e) for r in range(plane.line) for e in range(2)] + [plane.place]
    whole = pl.BlockSpec(memory_space=pltpu.VMEM)
    there = pl.BlockSpec(memory_space=pl.ANY)
    return pl.pallas_call(
        functools.partial(second_kernel, plane.line),
        in_specs=[pl.BlockSpec(memory_space=pltpu.SMEM), there]
        + [whole] * 4
        + [there] * len(blocks),
        out_specs=[whole, there],
        out_shape=[
            jax.ShapeDtypeStruct((rows, cols), bf16),
            jax.ShapeDtypeStruct((rows, width), bf16),
        ],
        scratch_shapes=[
            pltpu.VMEM((n, rows, shard), bf16),
            pltpu.VMEM((n, shard + PAD, cols), bf16),
            pltpu.VMEM((n, rows, shard), f32),
            pltpu.VMEM((rows, cols), f32),
            pltpu.VMEM((n, rows, shard), bf16),
            pltpu.SemaphoreType.DMA((n,)),
            pltpu.SemaphoreType.DMA((n,)),
            pltpu.SemaphoreType.DMA((n,)),
        ],
        compiler_params=pltpu.CompilerParams(vmem_limit_bytes=48 * 2**20),
        cost_estimate=pl.CostEstimate(
            flops=4 * rows * width * cols,
            bytes_accessed=4 * rows * width + 2 * width * cols,
            transcendentals=0,
        ),
        name="project_and_input_grad",
    )(jnp.stack(at).astype(jnp.int32), tokens_in, kv_grad, inv, cosine, sine, *blocks)


def replica_sum(value):
    replicas = lax.axis_size("replica")
    if replicas & (replicas - 1):
        return lax.psum(value, "replica")
    step = 1
    while step < replicas:
        pairs = [(r, r ^ step) for r in range(replicas)]
        value = value + lax.ppermute(value, "replica", pairs)
        step *= 2
    return value


def gather_a(plane, own):
    last = plane.line - 1
    up, down = [own], [own]
    up_x, down_x = [plane.flip(own, 0, last)], [None]
    for s in range(1, plane.line):
        up.append(plane.up(up[-1], s - 1, last - 1))
        down.append(plane.down(down[-1], 1, last - s + 1))
        up[s], down[s] = lax.optimization_barrier((up[s], down[s]))
        up_x.append(plane.flip(up[s], s, last))
        down_x.append(plane.flip(down[s], 0, last - s))
    return up, down, up_x, down_x


def gather_b(plane, own):
    last = plane.line - 1
    pair = jnp.concatenate([own, plane.flip(own, 0, last)], axis=0)
    up, down = [pair], [pair]
    for s in range(1, plane.line):
        up.append(plane.up(up[-1], s - 1, last - 1))
        down.append(plane.down(down[-1], 1, last - s + 1))
        up[s], down[s] = lax.optimization_barrier((up[s], down[s]))
    return up, down


def scatter_line(plane, terms):
    last = plane.line - 1
    up, down = [], []
    for s in range(last, 0, -1):
        up = plane.up(sum(terms(s) + up).astype(bf16), 0, last - s)
        down = plane.down(sum(terms(plane.line - s) + down).astype(bf16), s, last)
        up, down = lax.optimization_barrier((up, down))
        up, down = [up.astype(f32)], [down.astype(f32)]
    return sum(terms(0) + up + down)


def scatter_a(plane, near, far, distances):
    last = plane.line - 1
    other = {r: plane.flip(far[r], 0, last) for r in distances}
    return scatter_line(plane, lambda r: [near[r], other[r].astype(f32)])


def scatter_b(plane, near):
    both = scatter_line(plane, lambda r: [near[r]])
    rest = both.shape[0] // 2
    other = plane.flip(both[rest:].astype(bf16), 0, plane.line - 1)
    return both[:rest] + other.astype(f32)


def local(
    layer_input,
    norm_gain,
    kv_weight,
    kv_cotangent,
    pseudo_grad,
    outer_momentum,
    global_params,
    local_params,
):
    plane = Plane()
    tokens_in = layer_input[0]
    gain_shard = norm_gain[0]
    weight_shard = kv_weight[0]
    cotangent = kv_cotangent[0]
    rows, width = tokens_in.shape
    shard, cols = weight_shard.shape
    cut = shard * 5 // 8 // PAD * PAD

    total = replica_sum(pseudo_grad[0])
    gain_rows = jnp.pad(gain_shard[None, :], ((0, PAD - 1), (0, cols - shard)))
    own_a = weight_shard[:cut]
    own_b = jnp.concatenate([weight_shard[cut:], gain_rows], axis=0)
    up_a, down_a, up_x, down_x = gather_a(plane, own_a)
    up_b, down_b = gather_b(plane, own_b)
    blocks = [own_a, up_x[0], up_b[0]]
    for part in (up_a, down_a, up_x, down_x, up_b, down_b):
        blocks += part[1:]

    positions = (plane.me * rows + jnp.arange(rows, dtype=jnp.int32)) % SEQ_LEN
    cosine, sine = rope_tables(positions)
    scale = 1.0 / math.sqrt(rows * plane.count)
    distances = []
    for s in range(plane.line - 1, 0, -1):
        distances += [s, plane.line - s]
    distances = list(dict.fromkeys(distances)) + [0]
    kv_grad, inv, near_a, near_b, far_a = first_part(
        plane, tokens_in, cotangent, cosine, sine, shard, cut, distances, scale
    )
    (far_a, near_b) = after((far_a, near_b), up_a[1], down_a[1])
    term_a = scatter_a(plane, near_a, far_a, distances)
    term_b = scatter_b(plane, near_b)
    term = jnp.concatenate([term_a, term_b], axis=0)
    weight_grad = term * gain_shard.astype(f32)[:, None]
    gain_grad = jnp.sum(term * weight_shard.astype(f32), axis=1)

    replicas = lax.axis_size("replica")
    average = total / replicas
    momentum_new = momentum_rate * outer_momentum + average
    global_new = global_params - outer_rate * (average + momentum_rate * momentum_new)
    local_new = (
        mixing_rate * local_params[0].astype(f32) + (1.0 - mixing_rate) * global_new
    ).astype(bf16)

    kv_out, input_grad = second_part(
        plane, tokens_in, kv_grad, inv, cosine, sine, blocks, shard
    )
    return (
        kv_out[None],
        input_grad[None],
        weight_grad[None],
        gain_grad[None],
        momentum_new,
        global_new,
        local_new[None],
    )


def solution(mesh):
    in_specs = (
        P("replica", "fsdp", None),
        P("replica", "fsdp"),
        P("replica", "fsdp", None),
        P("replica", "fsdp", None),
        P("replica", "fsdp", None),
        P("fsdp", None),
        P("fsdp", None),
        P("replica", "fsdp", None),
    )
    out_specs = (
        P("replica", "fsdp", None),
        P("replica", "fsdp", None),
        P("replica", "fsdp", None),
        P("replica", "fsdp"),
        P("fsdp", None),
        P("fsdp", None),
        P("replica", "fsdp", None),
    )
    return jax.shard_map(local, mesh=mesh, in_specs=in_specs, out_specs=out_specs, check_vma=False)
```

```python
import functools
import math

import jax
import jax.numpy as jnp
from jax import lax
from jax.experimental import pallas as pl
from jax.experimental.pallas import tpu as pltpu
from jax.sharding import PartitionSpec as P

HEAD = 128
SEQ_LEN = 4096


epsilon = 1e-05
rope_base = 500000.0
momentum_rate = 0.9
outer_rate = 0.7
mixing_rate = 0.5

f32, bf16 = jnp.float32, jnp.bfloat16


class Ring:
    def __init__(self):
        self.count = lax.axis_size("fsdp")
        self.half = self.count // 2
        walk = list(range(0, self.count, 2)) + list(range(self.count - 1, 0, -2))
        after = walk[1:] + walk[:1]
        self.right = list(zip(walk, after))
        self.left = list(zip(after, walk))
        self.me = lax.axis_index("fsdp")
        self.spot = jnp.where(
            self.me % 2 == 0, self.me // 2, self.count - 1 - self.me // 2
        )

    def devices_at(self, distances):
        spot = (self.spot + self.count + jnp.array(distances, jnp.int32)) % self.count
        return jnp.where(spot < self.half, 2 * spot, 2 * (self.count - 1 - spot) + 1)

    def to_right(self, value, skip=()):
        return lax.ppermute(value, "fsdp", [p for p in self.right if p[0] not in skip])

    def to_left(self, value, skip=()):
        return lax.ppermute(value, "fsdp", [p for p in self.left if p[0] not in skip])


class Plane(Ring):
    first, second = (2, 5), (4, 3)
    chords = [(2, 3), (3, 2), (4, 5), (5, 4)]
    inward = [(0, 2), (6, 4), (7, 5), (1, 3)]
    outward = [(2, 0), (4, 6), (5, 7), (3, 1)]

    def __init__(self):
        super().__init__()
        self.is_first = (self.me == 2) | (self.me == 5)
        self.is_second = (self.me == 4) | (self.me == 3)

    def send(self, value, pairs):
        return lax.ppermute(value, "fsdp", pairs)


def after(value, *others):
    return lax.optimization_barrier((value, others))[0]


def rope_tables(positions):
    half = HEAD // 2
    index_f = jnp.arange(half, dtype=f32)
    inverse = jnp.exp(index_f * (-2.0 * math.log(rope_base) / HEAD))
    angle = positions.astype(f32)[:, None] * inverse[None, :]
    cosine, sine = jnp.cos(angle), jnp.sin(angle)
    return jnp.concatenate([cosine, cosine], axis=1), jnp.concatenate([-sine, sine], axis=1)


def first_kernel(scale, at, x, cotangent, cosine, sine, kv_grad, inv, far, near):
    step = pl.program_id(0)
    width = x.shape[1]
    shard = far.shape[0]
    kvw = cotangent.shape[1] // 2

    @pl.when(step == 0)
    def _():
        total = jnp.zeros((x.shape[0], HEAD), f32)
        for c in range(0, width, HEAD):
            part = x[:, c : c + HEAD].astype(f32)
            total = total + part * part
        mean = jnp.sum(total, axis=1, keepdims=True) / width
        inv[...] = jnp.broadcast_to(lax.rsqrt(mean + epsilon), inv.shape)
        for c in range(0, kvw, HEAD):
            part = cotangent[:, c : c + HEAD].astype(f32)
            turned = pltpu.roll(part, HEAD // 2, 1)
            kv_grad[:, c : c + HEAD] = (part * cosine[...] - turned * sine[...]).astype(bf16)
        kv_grad[:, kvw:] = cotangent[:, kvw:]

    block = x[:, pl.ds(pl.multiple_of(at[step] * shard, shard), shard)]
    normed = (block.astype(f32) * inv[:, :1]).astype(bf16)
    term = (
        lax.dot_general(normed, kv_grad[...], (((0,), (0,)), ((), ())), preferred_element_type=f32)
        * scale
    )

    @pl.when(step == 0)
    def _():
        far[...] = term.astype(bf16)

    @pl.when(step > 0)
    def _():
        near[0] = term


def first_part(ring, tokens_in, cotangent, cosine, sine, shard, scale):
    rows, width = tokens_in.shape
    cols = cotangent.shape[1]
    order = [ring.half]
    for d in range(ring.half - 1, 0, -1):
        order += [d, -d]
    order.append(0)
    n = ring.count
    fixed = lambda k, at: (0, 0)
    return pl.pallas_call(
        functools.partial(first_kernel, scale),
        grid_spec=pltpu.PrefetchScalarGridSpec(
            num_scalar_prefetch=1,
            grid=(n,),
            in_specs=[
                pl.BlockSpec((rows, width), fixed),
                pl.BlockSpec((rows, cols), fixed),
                pl.BlockSpec((rows, HEAD), fixed),
                pl.BlockSpec((rows, HEAD), fixed),
            ],
            out_specs=[
                pl.BlockSpec((rows, cols), fixed),
                pl.BlockSpec((rows, HEAD), fixed),
                pl.BlockSpec((shard, cols), fixed),
                pl.BlockSpec((1, shard, cols), lambda k, at: (jnp.maximum(k - 1, 0), 0, 0)),
            ],
        ),
        out_shape=[
            jax.ShapeDtypeStruct((rows, cols), bf16),
            jax.ShapeDtypeStruct((rows, HEAD), f32),
            jax.ShapeDtypeStruct((shard, cols), bf16),
            jax.ShapeDtypeStruct((n - 1, shard, cols), f32),
        ],
        compiler_params=pltpu.CompilerParams(vmem_limit_bytes=40 * 2**20),
        cost_estimate=pl.CostEstimate(
            flops=2 * rows * width * cols,
            bytes_accessed=2 * rows * width + 4 * width * cols,
            transcendentals=0,
        ),
        name="norm_and_weight_terms",
    )(ring.devices_at(order), tokens_in, cotangent, cosine, sine)


def second_kernel(plan, at, x, kv_grad, inv, cosine, sine, *refs):
    n = len(plan)
    blocks, refs = refs[:-10], refs[-10:]
    kv_out, input_grad, xs, ws, ng, pre, out, x_sem, w_sem, o_sem = refs
    rows, width = x.shape
    shard = xs.shape[2]
    kvw = pre.shape[1] // 2

    def columns(k):
        return pl.ds(pl.multiple_of(at[k] * shard, shard), shard)

    def x_copy(k):
        return pltpu.make_async_copy(x.at[:, columns(k)], xs.at[k], x_sem.at[k])

    def o_copy(k):
        return pltpu.make_async_copy(out.at[k], input_grad.at[:, columns(k)], o_sem.at[k])

    for k in range(n):
        x_copy(k).start()
        for flag, block, start, stop in plan[k]:
            copy = pltpu.make_async_copy(blocks[block], ws.at[k, start:stop], w_sem.at[k])
            if flag is None:
                copy.start()
            else:

                @pl.when(at[n + flag] == 1)
                def _(copy=copy):
                    copy.start()

    pre[...] = jnp.zeros_like(pre)

    def gather(k, total):
        x_copy(k).wait()
        pltpu.make_async_copy(ws.at[k], ws.at[k], w_sem.at[k]).wait()
        weight = ws[k]
        normed = xs[k].astype(f32) * inv[:, :1]
        pre[...] += jnp.dot(normed.astype(bf16), weight, preferred_element_type=f32)
        grad = lax.dot_general(
            kv_grad[...], weight, (((1,), (1,)), ((), ())), preferred_element_type=f32
        )
        ng[k] = grad
        product = grad * normed
        for c in range(0, shard, HEAD):
            total = total + product[:, c : c + HEAD]
        return total

    total = lax.fori_loop(0, n, gather, jnp.zeros((rows, HEAD), f32))
    mean = jnp.sum(total, axis=1, keepdims=True) / width

    def finish(k, carry):
        scale = inv[:, :1]
        normed = xs[k].astype(f32) * scale
        out[k] = (scale * (ng[k] - normed * mean)).astype(bf16)
        o_copy(k).start()
        return carry

    lax.fori_loop(0, n, finish, 0)
    for c in range(0, kvw, HEAD):
        part = pre[:, c : c + HEAD]
        turned = pltpu.roll(part, HEAD // 2, 1)
        kv_out[:, c : c + HEAD] = (part * cosine[...] + turned * sine[...]).astype(bf16)
    kv_out[:, kvw:] = pre[:, kvw:].astype(bf16)

    def drain(k, carry):
        o_copy(k).wait()
        return carry

    lax.fori_loop(0, n, drain, 0)


def second_part(ring, tokens_in, kv_grad, inv, cosine, sine, blocks, plan, flags, shard):
    rows, width = tokens_in.shape
    cols = kv_grad.shape[1]
    n = ring.count
    order = [0]
    for d in range(1, ring.half):
        order += [-d, d]
    order.append(ring.half)
    at = jnp.concatenate([ring.devices_at(order).astype(jnp.int32), flags.astype(jnp.int32)])
    whole = pl.BlockSpec(memory_space=pltpu.VMEM)
    there = pl.BlockSpec(memory_space=pl.ANY)
    return pl.pallas_call(
        functools.partial(second_kernel, plan),
        in_specs=[pl.BlockSpec(memory_space=pltpu.SMEM), there]
        + [whole] * 4
        + [there] * len(blocks),
        out_specs=[whole, there],
        out_shape=[
            jax.ShapeDtypeStruct((rows, cols), bf16),
            jax.ShapeDtypeStruct((rows, width), bf16),
        ],
        scratch_shapes=[
            pltpu.VMEM((n, rows, shard), bf16),
            pltpu.VMEM((n, shard, cols), bf16),
            pltpu.VMEM((n, rows, shard), f32),
            pltpu.VMEM((rows, cols), f32),
            pltpu.VMEM((n, rows, shard), bf16),
            pltpu.SemaphoreType.DMA((n,)),
            pltpu.SemaphoreType.DMA((n,)),
            pltpu.SemaphoreType.DMA((n,)),
        ],
        compiler_params=pltpu.CompilerParams(vmem_limit_bytes=48 * 2**20),
        cost_estimate=pl.CostEstimate(
            flops=4 * rows * width * cols,
            bytes_accessed=4 * rows * width + 2 * width * cols,
            transcendentals=0,
        ),
        name="project_and_input_grad",
    )(at, tokens_in, kv_grad, inv, cosine, sine, *blocks)


def replica_sum(value):
    replicas = lax.axis_size("replica")
    if replicas & (replicas - 1):
        return lax.psum(value, "replica")
    step = 1
    while step < replicas:
        pairs = [(r, r ^ step) for r in range(replicas)]
        value = value + lax.ppermute(value, "replica", pairs)
        step *= 2
    return value


def exchange_ring(ring, own, far, near, pseudo):
    total = replica_sum(pseudo)
    shard, cut = own.shape[0], own.shape[0] // 2
    blocks = [own]
    from_left = from_right = own
    for d in range(1, ring.half):
        from_left, from_right = ring.to_right(from_left), ring.to_left(from_right)
        blocks += [from_left, from_right]
    from_left, from_right = after((from_left, from_right), total)
    blocks += [ring.to_right(from_left[:cut]), ring.to_left(from_right[cut:])]
    last = len(blocks) - 2
    plan = [((None, k, 0, shard),) for k in range(last)]
    plan.append(((None, last, 0, cut), (None, last + 1, cut, shard)))

    far = after(far, blocks[1], blocks[2])
    from_left, from_right = ring.to_right(far[:cut]), ring.to_left(far[cut:])
    for k in range(0, 2 * (ring.half - 1), 2):
        from_left, from_right = lax.optimization_barrier((from_left, from_right))
        if k == 0:
            from_left = jnp.pad(from_left, ((0, shard - cut), (0, 0)))
            from_right = jnp.pad(from_right, ((cut, 0), (0, 0)))
        from_left = ring.to_right((near[k] + from_left.astype(f32)).astype(bf16))
        from_right = ring.to_left((near[k + 1] + from_right.astype(f32)).astype(bf16))
    term = near[-1] + from_left.astype(f32) + from_right.astype(f32)
    return blocks, plan, jnp.zeros((1,), jnp.int32), term, total


def exchange_plane(plane, own, far, near, pseudo):
    first, second = plane.first, plane.second
    left1, right1 = plane.to_right(own), plane.to_left(own)
    partner = plane.send(own, plane.chords)
    left1, right1, partner = lax.optimization_barrier((left1, right1, partner))
    left2, right2 = plane.to_right(left1), plane.to_left(right1)
    far_inner = plane.send(jnp.where(plane.is_second, left1, right1), plane.chords)
    total = replica_sum(after(pseudo, left1, right1))
    left2, right2 = lax.optimization_barrier((left2, right2))
    far = after(far, left2, right2)
    left3, right3 = plane.to_right(left2, (0, 7)), plane.to_left(right2, (6, 1))
    from_outer = plane.send(far, plane.inward)
    left3, right3, from_outer, far_inner, far = lax.optimization_barrier(
        (left3, right3, from_outer, far_inner, far)
    )
    far_outer = plane.send(jnp.where(plane.is_second, left3, right3), plane.outward)
    from_inner = plane.send(far, plane.chords)
    from_outer = from_outer.astype(f32)
    sum_r = plane.to_right((near[0] + from_outer).astype(bf16), second)
    sum_l = plane.to_left((near[1] + from_outer).astype(bf16), first)
    sum_r, sum_l, far_outer, from_inner, total = lax.optimization_barrier(
        (sum_r, sum_l, far_outer, from_inner, total)
    )
    for_partner = after(jnp.where(plane.is_first, near[1], near[0]).astype(bf16), sum_r)
    from_partner = plane.send(for_partner, plane.chords)
    sum_r = plane.to_right((near[2] + sum_r.astype(f32)).astype(bf16))
    sum_l = plane.to_left((near[3] + sum_l.astype(f32)).astype(bf16))
    sum_r, sum_l = lax.optimization_barrier((sum_r, sum_l))
    from_inner = from_inner.astype(f32)
    more_r = near[4] + jnp.where(plane.is_first, from_inner, 0.0)
    more_l = near[5] + jnp.where(plane.is_second, from_inner, 0.0)
    sum_r = plane.to_right((more_r + sum_r.astype(f32)).astype(bf16))
    sum_l = plane.to_left((more_l + sum_l.astype(f32)).astype(bf16))
    term = near[6] + from_partner.astype(f32) + sum_r.astype(f32) + sum_l.astype(f32)

    blocks = [own, left1, right1, left2, right2, left3, right3, partner, far_inner, far_outer]
    shard = own.shape[0]
    plan = [((None, k, 0, shard),) for k in range(5)]
    plan.append(((0, 7, 0, shard), (1, 5, 0, shard)))
    plan.append(((2, 7, 0, shard), (3, 6, 0, shard)))
    plan.append(((4, 8, 0, shard), (5, 9, 0, shard)))
    inner = plane.is_first | plane.is_second
    flags = [plane.is_first, ~plane.is_first, plane.is_second, ~plane.is_second, inner, ~inner]
    return blocks, plan, jnp.stack(flags), term, total


def local(
    layer_input,
    norm_gain,
    kv_weight,
    kv_cotangent,
    pseudo_grad,
    outer_momentum,
    global_params,
    local_params,
):
    small = lax.axis_size("fsdp") == 8
    ring = Plane() if small else Ring()
    tokens_in = layer_input[0]
    gain_shard = norm_gain[0].astype(f32)[:, None]
    weight_shard = kv_weight[0]
    cotangent = kv_cotangent[0]
    rows, width = tokens_in.shape
    shard, cols = weight_shard.shape

    weight_f = weight_shard.astype(f32)
    own = (weight_f * gain_shard).astype(bf16)
    positions = (ring.me * rows + jnp.arange(rows, dtype=jnp.int32)) % SEQ_LEN
    cosine, sine = rope_tables(positions)
    scale = 1.0 / math.sqrt(rows * ring.count)
    kv_grad, inv, far, near = first_part(
        ring, tokens_in, cotangent, cosine, sine, shard, scale
    )
    exchange = exchange_plane if small else exchange_ring
    blocks, plan, flags, term, total = exchange(ring, own, far, near, pseudo_grad[0])
    weight_grad = term * gain_shard
    gain_grad = jnp.sum(term * weight_f, axis=1)

    replicas = lax.axis_size("replica")
    average = total / replicas
    momentum_new = momentum_rate * outer_momentum + average
    global_new = global_params - outer_rate * (average + momentum_rate * momentum_new)
    local_new = (
        mixing_rate * local_params[0].astype(f32) + (1.0 - mixing_rate) * global_new
    ).astype(bf16)

    kv_out, input_grad = second_part(
        ring, tokens_in, kv_grad, inv, cosine, sine, blocks, plan, flags, shard
    )
    return (
        kv_out[None],
        input_grad[None],
        weight_grad[None],
        gain_grad[None],
        momentum_new,
        global_new,
        local_new[None],
    )


def solution(mesh):
    in_specs = (
        P("replica", "fsdp", None),
        P("replica", "fsdp"),
        P("replica", "fsdp", None),
        P("replica", "fsdp", None),
        P("replica", "fsdp", None),
        P("fsdp", None),
        P("fsdp", None),
        P("replica", "fsdp", None),
    )
    out_specs = (
        P("replica", "fsdp", None),
        P("replica", "fsdp", None),
        P("replica", "fsdp", None),
        P("replica", "fsdp"),
        P("fsdp", None),
        P("fsdp", None),
        P("replica", "fsdp", None),
    )
    return jax.shard_map(local, mesh=mesh, in_specs=in_specs, out_specs=out_specs, check_vma=False)
```

```python
import functools
import math

import jax
import jax.numpy as jnp
from jax import lax
from jax.experimental import pallas as pl
from jax.experimental.pallas import tpu as pltpu
from jax.sharding import PartitionSpec as P

HEAD = 128
SEQ_LEN = 4096


epsilon = 1e-05
rope_base = 500000.0
momentum_rate = 0.9
outer_rate = 0.7
mixing_rate = 0.5

f32, bf16 = jnp.float32, jnp.bfloat16


class Ring:
    def __init__(self):
        self.count = lax.axis_size("fsdp")
        self.half = self.count // 2
        walk = list(range(0, self.count, 2)) + list(range(self.count - 1, 0, -2))
        after = walk[1:] + walk[:1]
        self.right = list(zip(walk, after))
        self.left = list(zip(after, walk))
        self.me = lax.axis_index("fsdp")
        self.spot = jnp.where(
            self.me % 2 == 0, self.me // 2, self.count - 1 - self.me // 2
        )

    def devices_at(self, distances):
        spot = (self.spot + self.count + jnp.array(distances, jnp.int32)) % self.count
        return jnp.where(spot < self.half, 2 * spot, 2 * (self.count - 1 - spot) + 1)

    def to_right(self, value):
        return lax.ppermute(value, "fsdp", self.right)

    def to_left(self, value):
        return lax.ppermute(value, "fsdp", self.left)


class Plane(Ring):
    def __init__(self):
        super().__init__()
        self.at = [self.spot % 4 == i for i in range(4)]

    def over_chord(self, value):
        return lax.ppermute(value, "fsdp", [(2, 3), (3, 2), (4, 5), (5, 4)])


def after(value, *others):
    return lax.optimization_barrier((value, others))[0]


def rope_tables(positions):
    half = HEAD // 2
    index_f = jnp.arange(half, dtype=f32)
    inverse = jnp.exp(index_f * (-2.0 * math.log(rope_base) / HEAD))
    angle = positions.astype(f32)[:, None] * inverse[None, :]
    cosine, sine = jnp.cos(angle), jnp.sin(angle)
    return jnp.concatenate([cosine, cosine], axis=1), jnp.concatenate([-sine, sine], axis=1)


def first_kernel(scale, at, x, cotangent, cosine, sine, kv_grad, inv, far, near):
    step = pl.program_id(0)
    width = x.shape[1]
    shard = far.shape[0]
    kvw = cotangent.shape[1] // 2

    @pl.when(step == 0)
    def _():
        total = jnp.zeros((x.shape[0], HEAD), f32)
        for c in range(0, width, HEAD):
            part = x[:, c : c + HEAD].astype(f32)
            total = total + part * part
        mean = jnp.sum(total, axis=1, keepdims=True) / width
        inv[...] = jnp.broadcast_to(lax.rsqrt(mean + epsilon), inv.shape)
        for c in range(0, kvw, HEAD):
            part = cotangent[:, c : c + HEAD].astype(f32)
            turned = pltpu.roll(part, HEAD // 2, 1)
            kv_grad[:, c : c + HEAD] = (part * cosine[...] - turned * sine[...]).astype(bf16)
        kv_grad[:, kvw:] = cotangent[:, kvw:]

    block = x[:, pl.ds(pl.multiple_of(at[step] * shard, shard), shard)]
    normed = (block.astype(f32) * inv[:, :1]).astype(bf16)
    term = (
        lax.dot_general(normed, kv_grad[...], (((0,), (0,)), ((), ())), preferred_element_type=f32)
        * scale
    )

    @pl.when(step == 0)
    def _():
        far[...] = term.astype(bf16)

    @pl.when(step > 0)
    def _():
        near[0] = term


def first_part(ring, tokens_in, cotangent, cosine, sine, shard, scale):
    rows, width = tokens_in.shape
    cols = cotangent.shape[1]
    order = [ring.half]
    for d in range(ring.half - 1, 0, -1):
        order += [d, -d]
    order.append(0)
    n = ring.count
    fixed = lambda k, at: (0, 0)
    return pl.pallas_call(
        functools.partial(first_kernel, scale),
        grid_spec=pltpu.PrefetchScalarGridSpec(
            num_scalar_prefetch=1,
            grid=(n,),
            in_specs=[
                pl.BlockSpec((rows, width), fixed),
                pl.BlockSpec((rows, cols), fixed),
                pl.BlockSpec((rows, HEAD), fixed),
                pl.BlockSpec((rows, HEAD), fixed),
            ],
            out_specs=[
                pl.BlockSpec((rows, cols), fixed),
                pl.BlockSpec((rows, HEAD), fixed),
                pl.BlockSpec((shard, cols), fixed),
                pl.BlockSpec((1, shard, cols), lambda k, at: (jnp.maximum(k - 1, 0), 0, 0)),
            ],
        ),
        out_shape=[
            jax.ShapeDtypeStruct((rows, cols), bf16),
            jax.ShapeDtypeStruct((rows, HEAD), f32),
            jax.ShapeDtypeStruct((shard, cols), bf16),
            jax.ShapeDtypeStruct((n - 1, shard, cols), f32),
        ],
        compiler_params=pltpu.CompilerParams(vmem_limit_bytes=40 * 2**20),
        cost_estimate=pl.CostEstimate(
            flops=2 * rows * width * cols,
            bytes_accessed=2 * rows * width + 4 * width * cols,
            transcendentals=0,
        ),
        name="norm_and_weight_terms",
    )(ring.devices_at(order), tokens_in, cotangent, cosine, sine)


def second_kernel(plan, at, x, kv_grad, inv, cosine, sine, *refs):
    n = len(plan)
    blocks, refs = refs[:-10], refs[-10:]
    kv_out, input_grad, xs, ws, ng, pre, out, x_sem, w_sem, o_sem = refs
    rows, width = x.shape
    shard = xs.shape[2]
    kvw = pre.shape[1] // 2

    def columns(k):
        return pl.ds(pl.multiple_of(at[k] * shard, shard), shard)

    def x_copy(k):
        return pltpu.make_async_copy(x.at[:, columns(k)], xs.at[k], x_sem.at[k])

    def o_copy(k):
        return pltpu.make_async_copy(out.at[k], input_grad.at[:, columns(k)], o_sem.at[k])

    for k in range(n):
        x_copy(k).start()
        for flag, block, start, stop in plan[k]:
            copy = pltpu.make_async_copy(blocks[block], ws.at[k, start:stop], w_sem.at[k])
            if flag is None:
                copy.start()
            else:

                @pl.when(at[n + flag] == 1)
                def _(copy=copy):
                    copy.start()

    pre[...] = jnp.zeros_like(pre)

    def gather(k, total):
        x_copy(k).wait()
        pltpu.make_async_copy(ws.at[k], ws.at[k], w_sem.at[k]).wait()
        weight = ws[k]
        normed = xs[k].astype(f32) * inv[:, :1]
        pre[...] += jnp.dot(normed.astype(bf16), weight, preferred_element_type=f32)
        grad = lax.dot_general(
            kv_grad[...], weight, (((1,), (1,)), ((), ())), preferred_element_type=f32
        )
        ng[k] = grad
        product = grad * normed
        for c in range(0, shard, HEAD):
            total = total + product[:, c : c + HEAD]
        return total

    total = lax.fori_loop(0, n, gather, jnp.zeros((rows, HEAD), f32))
    mean = jnp.sum(total, axis=1, keepdims=True) / width

    def finish(k, carry):
        scale = inv[:, :1]
        normed = xs[k].astype(f32) * scale
        out[k] = (scale * (ng[k] - normed * mean)).astype(bf16)
        o_copy(k).start()
        return carry

    lax.fori_loop(0, n, finish, 0)
    for c in range(0, kvw, HEAD):
        part = pre[:, c : c + HEAD]
        turned = pltpu.roll(part, HEAD // 2, 1)
        kv_out[:, c : c + HEAD] = (part * cosine[...] + turned * sine[...]).astype(bf16)
    kv_out[:, kvw:] = pre[:, kvw:].astype(bf16)

    def drain(k, carry):
        o_copy(k).wait()
        return carry

    lax.fori_loop(0, n, drain, 0)


def second_part(ring, tokens_in, kv_grad, inv, cosine, sine, blocks, plan, flags, shard):
    rows, width = tokens_in.shape
    cols = kv_grad.shape[1]
    n = ring.count
    order = [0]
    for d in range(1, ring.half):
        order += [-d, d]
    order.append(ring.half)
    at = jnp.concatenate([ring.devices_at(order).astype(jnp.int32), flags.astype(jnp.int32)])
    whole = pl.BlockSpec(memory_space=pltpu.VMEM)
    there = pl.BlockSpec(memory_space=pl.ANY)
    return pl.pallas_call(
        functools.partial(second_kernel, plan),
        in_specs=[pl.BlockSpec(memory_space=pltpu.SMEM), there]
        + [whole] * 4
        + [there] * len(blocks),
        out_specs=[whole, there],
        out_shape=[
            jax.ShapeDtypeStruct((rows, cols), bf16),
            jax.ShapeDtypeStruct((rows, width), bf16),
        ],
        scratch_shapes=[
            pltpu.VMEM((n, rows, shard), bf16),
            pltpu.VMEM((n, shard, cols), bf16),
            pltpu.VMEM((n, rows, shard), f32),
            pltpu.VMEM((rows, cols), f32),
            pltpu.VMEM((n, rows, shard), bf16),
            pltpu.SemaphoreType.DMA((n,)),
            pltpu.SemaphoreType.DMA((n,)),
            pltpu.SemaphoreType.DMA((n,)),
        ],
        compiler_params=pltpu.CompilerParams(vmem_limit_bytes=48 * 2**20),
        cost_estimate=pl.CostEstimate(
            flops=4 * rows * width * cols,
            bytes_accessed=4 * rows * width + 2 * width * cols,
            transcendentals=0,
        ),
        name="project_and_input_grad",
    )(at, tokens_in, kv_grad, inv, cosine, sine, *blocks)


def replica_sum(value):
    replicas = lax.axis_size("replica")
    if replicas != 4:
        total = lax.psum(value, "replica")
        return total, total
    swap = lambda v, step: lax.ppermute(v, "replica", [(r, r ^ step) for r in range(4)])
    odd = lax.axis_index("replica") % 2
    half = value.shape[0] // 2
    mine = lax.dynamic_slice_in_dim(value, odd * half, half, 0)
    theirs = lax.dynamic_slice_in_dim(value, (1 - odd) * half, half, 0)
    came = swap(theirs, 1)
    mine = mine + came
    mine = mine + swap(mine, 2)
    theirs = swap(mine, 1)
    low, high = jnp.where(odd == 0, mine, theirs), jnp.where(odd == 0, theirs, mine)
    return (low, high), came


def exchange_ring(ring, own, far, near, pseudo):
    total, came = replica_sum(pseudo)
    shard, cut = own.shape[0], own.shape[0] // 2
    blocks = [own]
    from_left = from_right = own
    for d in range(1, ring.half):
        from_left, from_right = ring.to_right(from_left), ring.to_left(from_right)
        blocks += [from_left, from_right]
    from_left, from_right = after((from_left, from_right), total)
    blocks += [ring.to_right(from_left[:cut]), ring.to_left(from_right[cut:])]
    last = len(blocks) - 2
    plan = [((None, k, 0, shard),) for k in range(last)]
    plan.append(((None, last, 0, cut), (None, last + 1, cut, shard)))

    far = after(far, blocks[1], blocks[2])
    from_left, from_right = ring.to_right(far[:cut]), ring.to_left(far[cut:])
    for k in range(0, 2 * (ring.half - 1), 2):
        from_left, from_right = lax.optimization_barrier((from_left, from_right))
        if k == 0:
            from_left = jnp.pad(from_left, ((0, shard - cut), (0, 0)))
            from_right = jnp.pad(from_right, ((cut, 0), (0, 0)))
        from_left = ring.to_right((near[k] + from_left.astype(f32)).astype(bf16))
        from_right = ring.to_left((near[k + 1] + from_right.astype(f32)).astype(bf16))
    term = near[-1] + from_left.astype(f32) + from_right.astype(f32)
    return blocks, plan, jnp.zeros((1,), jnp.int32), term, total


def exchange_plane(plane, own, far, near, pseudo):
    shard, cols = own.shape
    at0, at1, at2, at3 = plane.at
    zero = jnp.zeros((), f32)
    pieces = [(0, shard // 2), (shard // 2, shard)]
    halves = range(2)
    wide = lambda v: v.astype(f32)
    pick = jnp.where
    sent = [own]

    def part(value, h):
        return value[pieces[h][0] : pieces[h][1]]

    def ring(to_right, to_left):
        sent[0] = to_right, to_left
        return lax.optimization_barrier((plane.to_right(to_right), plane.to_left(to_left)))

    def later(*values):
        return after(values, sent[0])

    one = [ring(*later(part(own, h), part(own, h))) for h in halves]
    total, came = replica_sum(pseudo)
    one[0], far, came = lax.optimization_barrier((one[0], far, came))
    two = [ring(*later(*one[h])) for h in halves]
    two[1], total = lax.optimization_barrier((two[1], total))
    partner = plane.over_chord(after(own, total))
    three = []
    for h in halves:
        left, right = later(*two[h])
        terms = part(far, h)
        three.append(ring(pick(at0, terms, left), pick(at3, terms, right)))
    three[1], partner = lax.optimization_barrier((three[1], partner))
    from_inner = plane.over_chord(after(far, partner))
    four = []
    for h in halves:
        left, right = later(*three[h])
        to_right = wide(part(near[0], h)) + pick(at1, wide(left), zero)
        to_left = wide(part(near[1], h)) + pick(at2, wide(right), zero)
        four.append(
            ring(
                pick(at2, left, to_right.astype(bf16)),
                pick(at1, right, to_left.astype(bf16)),
            )
        )
    four[1], from_inner = lax.optimization_barrier((four[1], from_inner))
    join = jnp.concatenate([pick(at2, *one[h]) for h in halves])
    far_inner = plane.over_chord(after(join, from_inner))
    five = []
    for h in halves:
        left, right = later(*four[h])
        to_right = part(near[2], h) + pick(at3, zero, wide(left))
        to_left = part(near[3], h) + pick(at0, zero, wide(right))
        five.append(ring(to_right.astype(bf16), to_left.astype(bf16)))
    five[1], far_inner = lax.optimization_barrier((five[1], far_inner))
    for_partner = pick(at1, near[1], near[0]).astype(bf16)
    from_partner = plane.over_chord(after(for_partner, far_inner))
    six = []
    for h in halves:
        left, right = later(*five[h])
        chord = wide(part(from_inner, h))
        to_right = part(near[4], h) + wide(left) + pick(at1, chord, zero)
        to_left = part(near[5], h) + wide(right) + pick(at2, chord, zero)
        six.append(ring(to_right.astype(bf16), to_left.astype(bf16)))
    term = [
        part(near[6], h) + wide(part(from_partner, h)) + wide(six[h][0]) + wide(six[h][1])
        for h in halves
    ]

    blocks = [own, partner, far_inner]
    plan = [[(None, 0, 0, shard)]]

    def add(flag, arrays):
        entry = []
        for (start, stop), array in zip(pieces, arrays):
            entry.append((flag, len(blocks), start, stop))
            blocks.append(array)
        return entry

    for step in (one, two):
        for way in range(2):
            plan.append(add(None, [step[h][way] for h in halves]))
    for way in range(2):
        plan.append([(way, 1, 0, shard)] + add(2 + way, [three[h][way] for h in halves]))
    plan.append([(4, 2, 0, shard)])
    for way in range(2):
        plan[-1] += add(5 + way, [four[h][way] for h in halves])
    flags = [at1, at2, ~at1, ~at2, at1 | at2, at3, at0]
    plan = tuple(tuple(entry) for entry in plan)
    return blocks, plan, jnp.stack(flags), jnp.concatenate(term), total


def local(
    layer_input,
    norm_gain,
    kv_weight,
    kv_cotangent,
    pseudo_grad,
    outer_momentum,
    global_params,
    local_params,
):
    small = lax.axis_size("fsdp") == 8
    ring = Plane() if small else Ring()
    tokens_in = layer_input[0]
    gain_shard = norm_gain[0].astype(f32)[:, None]
    weight_shard = kv_weight[0]
    cotangent = kv_cotangent[0]
    rows, width = tokens_in.shape
    shard, cols = weight_shard.shape

    own = (weight_shard.astype(f32) * gain_shard).astype(bf16)
    positions = (ring.me * rows + jnp.arange(rows, dtype=jnp.int32)) % SEQ_LEN
    cosine, sine = rope_tables(positions)
    scale = 1.0 / math.sqrt(rows * ring.count)
    kv_grad, inv, far, near = first_part(
        ring, tokens_in, cotangent, cosine, sine, shard, scale
    )
    exchange = exchange_plane if small else exchange_ring
    blocks, plan, flags, term, total = exchange(ring, own, far, near, pseudo_grad[0])
    weight_grad = term * gain_shard
    gain_grad = jnp.sum(term * weight_shard.astype(f32), axis=1)

    if isinstance(total, tuple):
        total = jnp.concatenate(total)
    average = total / lax.axis_size("replica")
    momentum_new = momentum_rate * outer_momentum + average
    global_new = global_params - outer_rate * (average + momentum_rate * momentum_new)
    local_new = (
        mixing_rate * local_params[0].astype(f32) + (1.0 - mixing_rate) * global_new
    ).astype(bf16)

    kv_out, input_grad = second_part(
        ring, tokens_in, kv_grad, inv, cosine, sine, blocks, plan, flags, shard
    )
    return (
        kv_out[None],
        input_grad[None],
        weight_grad[None],
        gain_grad[None],
        momentum_new,
        global_new,
        local_new[None],
    )


def solution(mesh):
    in_specs = (
        P("replica", "fsdp", None),
        P("replica", "fsdp"),
        P("replica", "fsdp", None),
        P("replica", "fsdp", None),
        P("replica", "fsdp", None),
        P("fsdp", None),
        P("fsdp", None),
        P("replica", "fsdp", None),
    )
    out_specs = (
        P("replica", "fsdp", None),
        P("replica", "fsdp", None),
        P("replica", "fsdp", None),
        P("replica", "fsdp"),
        P("fsdp", None),
        P("fsdp", None),
        P("replica", "fsdp", None),
    )
    return jax.shard_map(local, mesh=mesh, in_specs=in_specs, out_specs=out_specs, check_vma=False)
```

```python
import functools
import math

import jax
import jax.numpy as jnp
from jax import lax
from jax.experimental import pallas as pl
from jax.experimental.pallas import tpu as pltpu
from jax.sharding import PartitionSpec as P

HEAD = 128
SEQ_LEN = 4096


epsilon = 1e-05
rope_base = 500000.0
momentum_rate = 0.9
outer_rate = 0.7
mixing_rate = 0.5

f32, bf16 = jnp.float32, jnp.bfloat16


class Ring:
    def __init__(self):
        self.count = lax.axis_size("fsdp")
        self.half = self.count // 2
        walk = list(range(0, self.count, 2)) + list(range(self.count - 1, 0, -2))
        after = walk[1:] + walk[:1]
        self.right = list(zip(walk, after))
        self.left = list(zip(after, walk))
        self.me = lax.axis_index("fsdp")
        self.spot = jnp.where(
            self.me % 2 == 0, self.me // 2, self.count - 1 - self.me // 2
        )

    def devices_at(self, distances):
        spot = (self.spot + self.count + jnp.array(distances, jnp.int32)) % self.count
        return jnp.where(spot < self.half, 2 * spot, 2 * (self.count - 1 - spot) + 1)

    def to_right(self, value):
        return lax.ppermute(value, "fsdp", self.right)

    def to_left(self, value):
        return lax.ppermute(value, "fsdp", self.left)


class Plane(Ring):
    def __init__(self):
        super().__init__()
        self.at = [self.spot % 4 == i for i in range(4)]

    def over_chord(self, value):
        return lax.ppermute(value, "fsdp", [(2, 3), (3, 2), (4, 5), (5, 4)])


def after(value, *others):
    return lax.optimization_barrier((value, others))[0]


def rope_tables(positions):
    half = HEAD // 2
    index_f = jnp.arange(half, dtype=f32)
    inverse = jnp.exp(index_f * (-2.0 * math.log(rope_base) / HEAD))
    angle = positions.astype(f32)[:, None] * inverse[None, :]
    cosine, sine = jnp.cos(angle), jnp.sin(angle)
    return jnp.concatenate([cosine, cosine], axis=1), jnp.concatenate([-sine, sine], axis=1)


def first_kernel(scale, at, x, cotangent, cosine, sine, kv_grad, inv, far, near):
    step = pl.program_id(0)
    width = x.shape[1]
    shard = far.shape[0]
    kvw = cotangent.shape[1] // 2

    @pl.when(step == 0)
    def _():
        total = jnp.zeros((x.shape[0], HEAD), f32)
        for c in range(0, width, HEAD):
            part = x[:, c : c + HEAD].astype(f32)
            total = total + part * part
        mean = jnp.sum(total, axis=1, keepdims=True) / width
        inv[...] = jnp.broadcast_to(lax.rsqrt(mean + epsilon), inv.shape)
        for c in range(0, kvw, HEAD):
            part = cotangent[:, c : c + HEAD].astype(f32)
            turned = pltpu.roll(part, HEAD // 2, 1)
            kv_grad[:, c : c + HEAD] = (part * cosine[...] - turned * sine[...]).astype(bf16)
        kv_grad[:, kvw:] = cotangent[:, kvw:]

    block = x[:, pl.ds(pl.multiple_of(at[step] * shard, shard), shard)]
    normed = (block.astype(f32) * inv[:, :1]).astype(bf16)
    term = (
        lax.dot_general(normed, kv_grad[...], (((0,), (0,)), ((), ())), preferred_element_type=f32)
        * scale
    )

    @pl.when(step == 0)
    def _():
        far[...] = term.astype(bf16)

    @pl.when(step > 0)
    def _():
        near[0] = term


def first_part(ring, tokens_in, cotangent, cosine, sine, shard, scale):
    rows, width = tokens_in.shape
    cols = cotangent.shape[1]
    order = [ring.half]
    for d in range(ring.half - 1, 0, -1):
        order += [d, -d]
    order.append(0)
    n = ring.count
    fixed = lambda k, at: (0, 0)
    return pl.pallas_call(
        functools.partial(first_kernel, scale),
        grid_spec=pltpu.PrefetchScalarGridSpec(
            num_scalar_prefetch=1,
            grid=(n,),
            in_specs=[
                pl.BlockSpec((rows, width), fixed),
                pl.BlockSpec((rows, cols), fixed),
                pl.BlockSpec((rows, HEAD), fixed),
                pl.BlockSpec((rows, HEAD), fixed),
            ],
            out_specs=[
                pl.BlockSpec((rows, cols), fixed),
                pl.BlockSpec((rows, HEAD), fixed),
                pl.BlockSpec((shard, cols), fixed),
                pl.BlockSpec((1, shard, cols), lambda k, at: (jnp.maximum(k - 1, 0), 0, 0)),
            ],
        ),
        out_shape=[
            jax.ShapeDtypeStruct((rows, cols), bf16),
            jax.ShapeDtypeStruct((rows, HEAD), f32),
            jax.ShapeDtypeStruct((shard, cols), bf16),
            jax.ShapeDtypeStruct((n - 1, shard, cols), f32),
        ],
        compiler_params=pltpu.CompilerParams(vmem_limit_bytes=40 * 2**20),
        cost_estimate=pl.CostEstimate(
            flops=2 * rows * width * cols,
            bytes_accessed=2 * rows * width + 4 * width * cols,
            transcendentals=0,
        ),
        name="norm_and_weight_terms",
    )(ring.devices_at(order), tokens_in, cotangent, cosine, sine)


def second_kernel(plan, at, x, kv_grad, inv, cosine, sine, *refs):
    n = len(plan)
    blocks, refs = refs[:-10], refs[-10:]
    kv_out, input_grad, xs, ws, ng, pre, out, x_sem, w_sem, o_sem = refs
    rows, width = x.shape
    shard = xs.shape[2]
    kvw = pre.shape[1] // 2

    def columns(k):
        return pl.ds(pl.multiple_of(at[k] * shard, shard), shard)

    def x_copy(k):
        return pltpu.make_async_copy(x.at[:, columns(k)], xs.at[k], x_sem.at[k])

    def o_copy(k):
        return pltpu.make_async_copy(out.at[k], input_grad.at[:, columns(k)], o_sem.at[k])

    for k in range(n):
        x_copy(k).start()
        for flag, block, start, stop in plan[k]:
            copy = pltpu.make_async_copy(blocks[block], ws.at[k, start:stop], w_sem.at[k])
            if flag is None:
                copy.start()
            else:

                @pl.when(at[n + flag] == 1)
                def _(copy=copy):
                    copy.start()

    pre[...] = jnp.zeros_like(pre)

    def gather(k, total):
        x_copy(k).wait()
        pltpu.make_async_copy(ws.at[k], ws.at[k], w_sem.at[k]).wait()
        weight = ws[k]
        normed = xs[k].astype(f32) * inv[:, :1]
        pre[...] += jnp.dot(normed.astype(bf16), weight, preferred_element_type=f32)
        grad = lax.dot_general(
            kv_grad[...], weight, (((1,), (1,)), ((), ())), preferred_element_type=f32
        )
        ng[k] = grad
        product = grad * normed
        for c in range(0, shard, HEAD):
            total = total + product[:, c : c + HEAD]
        return total

    total = lax.fori_loop(0, n, gather, jnp.zeros((rows, HEAD), f32))
    mean = jnp.sum(total, axis=1, keepdims=True) / width

    def finish(k, carry):
        scale = inv[:, :1]
        normed = xs[k].astype(f32) * scale
        out[k] = (scale * (ng[k] - normed * mean)).astype(bf16)
        o_copy(k).start()
        return carry

    lax.fori_loop(0, n, finish, 0)
    for c in range(0, kvw, HEAD):
        part = pre[:, c : c + HEAD]
        turned = pltpu.roll(part, HEAD // 2, 1)
        kv_out[:, c : c + HEAD] = (part * cosine[...] + turned * sine[...]).astype(bf16)
    kv_out[:, kvw:] = pre[:, kvw:].astype(bf16)

    def drain(k, carry):
        o_copy(k).wait()
        return carry

    lax.fori_loop(0, n, drain, 0)


def second_part(ring, tokens_in, kv_grad, inv, cosine, sine, blocks, plan, flags, shard):
    rows, width = tokens_in.shape
    cols = kv_grad.shape[1]
    n = ring.count
    order = [0]
    for d in range(1, ring.half):
        order += [-d, d]
    order.append(ring.half)
    at = jnp.concatenate([ring.devices_at(order).astype(jnp.int32), flags.astype(jnp.int32)])
    whole = pl.BlockSpec(memory_space=pltpu.VMEM)
    there = pl.BlockSpec(memory_space=pl.ANY)
    return pl.pallas_call(
        functools.partial(second_kernel, plan),
        in_specs=[pl.BlockSpec(memory_space=pltpu.SMEM), there]
        + [whole] * 4
        + [there] * len(blocks),
        out_specs=[whole, there],
        out_shape=[
            jax.ShapeDtypeStruct((rows, cols), bf16),
            jax.ShapeDtypeStruct((rows, width), bf16),
        ],
        scratch_shapes=[
            pltpu.VMEM((n, rows, shard), bf16),
            pltpu.VMEM((n, shard, cols), bf16),
            pltpu.VMEM((n, rows, shard), f32),
            pltpu.VMEM((rows, cols), f32),
            pltpu.VMEM((n, rows, shard), bf16),
            pltpu.SemaphoreType.DMA((n,)),
            pltpu.SemaphoreType.DMA((n,)),
            pltpu.SemaphoreType.DMA((n,)),
        ],
        compiler_params=pltpu.CompilerParams(vmem_limit_bytes=48 * 2**20),
        cost_estimate=pl.CostEstimate(
            flops=4 * rows * width * cols,
            bytes_accessed=4 * rows * width + 2 * width * cols,
            transcendentals=0,
        ),
        name="project_and_input_grad",
    )(at, tokens_in, kv_grad, inv, cosine, sine, *blocks)


def replica_sum(value):
    replicas = lax.axis_size("replica")
    if replicas != 4:
        total = lax.psum(value, "replica")
        return total, total
    swap = lambda v, step: lax.ppermute(v, "replica", [(r, r ^ step) for r in range(4)])
    odd = lax.axis_index("replica") % 2
    half = value.shape[0] // 2
    mine = lax.dynamic_slice_in_dim(value, odd * half, half, 0)
    theirs = lax.dynamic_slice_in_dim(value, (1 - odd) * half, half, 0)
    came = swap(theirs, 1)
    mine = mine + came
    mine = mine + swap(mine, 2)
    theirs = swap(mine, 1)
    low, high = jnp.where(odd == 0, mine, theirs), jnp.where(odd == 0, theirs, mine)
    return (low, high), came


def exchange_ring(ring, own, far, near, pseudo):
    total, came = replica_sum(pseudo)
    cut = own[0].shape[0]
    own = jnp.concatenate(own)
    shard = own.shape[0]
    blocks = [own]
    from_left = from_right = own
    for d in range(1, ring.half):
        from_left, from_right = ring.to_right(from_left), ring.to_left(from_right)
        blocks += [from_left, from_right]
    from_left, from_right = after((from_left, from_right), total)
    blocks += [ring.to_right(from_left[:cut]), ring.to_left(from_right[cut:])]
    last = len(blocks) - 2
    plan = [((None, k, 0, shard),) for k in range(last)]
    plan.append(((None, last, 0, cut), (None, last + 1, cut, shard)))

    far = after(far, blocks[1], blocks[2])
    from_left, from_right = ring.to_right(far[:cut]), ring.to_left(far[cut:])
    for k in range(0, 2 * (ring.half - 1), 2):
        from_left, from_right = lax.optimization_barrier((from_left, from_right))
        if k == 0:
            from_left = jnp.pad(from_left, ((0, shard - cut), (0, 0)))
            from_right = jnp.pad(from_right, ((cut, 0), (0, 0)))
        from_left = ring.to_right((near[k] + from_left.astype(f32)).astype(bf16))
        from_right = ring.to_left((near[k + 1] + from_right.astype(f32)).astype(bf16))
    term = near[-1] + from_left.astype(f32) + from_right.astype(f32)
    return blocks, plan, jnp.zeros((1,), jnp.int32), term, total


def exchange_plane(plane, own, far, near, pseudo):
    shard = 2 * own[0].shape[0]
    at0, at1, at2, at3 = plane.at
    zero = jnp.zeros((), f32)
    pieces = [(0, shard // 2), (shard // 2, shard)]
    halves = range(2)
    wide = lambda v: v.astype(f32)
    pick = jnp.where
    sent, crossed = [own], [own]

    def part(value, h):
        return value[pieces[h][0] : pieces[h][1]]

    def later(*values):
        return after(values, sent[0])

    def links(to_right, to_left, chord=None):
        sent[0] = to_right, to_left
        came = [plane.to_right(to_right), plane.to_left(to_left)]
        if chord is not None:
            came.append(plane.over_chord(after(chord, sent[0], crossed[0])))
            crossed[0] = came[-1]
        return lax.optimization_barrier(came)

    one = [links(*later(own[h], own[h])) for h in halves]
    total, came = replica_sum(after(pseudo, sent[0]))
    one[0], far, came = lax.optimization_barrier((one[0], far, came))
    two = [links(*later(*one[h])) for h in halves]
    two[0], total = lax.optimization_barrier((two[0], total))
    three = []
    for h in halves:
        left, right = later(*two[h])
        terms = part(far, h)
        three.append(links(pick(at0, terms, left), pick(at3, terms, right), own[h]))
    four = []
    for h in halves:
        left, right, _ = later(*three[h])
        to_right = wide(part(near[0], h)) + pick(at1, wide(left), zero)
        to_left = wide(part(near[1], h)) + pick(at2, wide(right), zero)
        to_right = pick(at2, left, to_right.astype(bf16))
        to_left = pick(at1, right, to_left.astype(bf16))
        four.append(links(to_right, to_left, pick(at2, *one[h])))
    five = []
    for h in halves:
        left, right, _ = later(*four[h])
        to_right = part(near[2], h) + pick(at3, zero, wide(left))
        to_left = part(near[3], h) + pick(at0, zero, wide(right))
        five.append(links(to_right.astype(bf16), to_left.astype(bf16), part(far, h)))
    six = []
    for h in halves:
        left, right, chord = later(*five[h])
        to_right = part(near[4], h) + wide(left) + pick(at1, wide(chord), zero)
        to_left = part(near[5], h) + wide(right) + pick(at2, wide(chord), zero)
        for_partner = part(pick(at1, near[1], near[0]).astype(bf16), h)
        six.append(links(to_right.astype(bf16), to_left.astype(bf16), for_partner))
    term = [part(near[6], h) + sum(wide(came) for came in six[h]) for h in halves]

    blocks, plan = [], []

    def add(flag, arrays):
        entry = []
        for (start, stop), array in zip(pieces, arrays):
            entry.append((flag, len(blocks), start, stop))
            blocks.append(array)
        return entry

    plan.append(add(None, own))
    for step in (one, two):
        for way in range(2):
            plan.append(add(None, [step[h][way] for h in halves]))
    partner = add(0, [three[h][2] for h in halves])
    for way in range(2):
        entry = [(way, *rest) for _, *rest in partner]
        plan.append(entry + add(2 + way, [three[h][way] for h in halves]))
    plan.append(add(4, [four[h][2] for h in halves]))
    for way in range(2):
        plan[-1] += add(5 + way, [four[h][way] for h in halves])
    flags = [at1, at2, ~at1, ~at2, at1 | at2, at3, at0]
    plan = tuple(tuple(entry) for entry in plan)
    return blocks, plan, jnp.stack(flags), jnp.concatenate(term), total


def local(
    layer_input,
    norm_gain,
    kv_weight,
    kv_cotangent,
    pseudo_grad,
    outer_momentum,
    global_params,
    local_params,
):
    small = lax.axis_size("fsdp") == 8
    ring = Plane() if small else Ring()
    tokens_in = layer_input[0]
    gain_shard = norm_gain[0].astype(f32)[:, None]
    weight_shard = kv_weight[0]
    cotangent = kv_cotangent[0]
    rows, width = tokens_in.shape
    shard, cols = weight_shard.shape

    cut = shard // 2
    own = [
        (weight_shard[rows].astype(f32) * gain_shard[rows]).astype(bf16)
        for rows in (slice(0, cut), slice(cut, shard))
    ]
    positions = (ring.me * rows + jnp.arange(rows, dtype=jnp.int32)) % SEQ_LEN
    cosine, sine = rope_tables(positions)
    scale = 1.0 / math.sqrt(rows * ring.count)
    kv_grad, inv, far, near = first_part(
        ring, tokens_in, cotangent, cosine, sine, shard, scale
    )
    exchange = exchange_plane if small else exchange_ring
    blocks, plan, flags, term, total = exchange(ring, own, far, near, pseudo_grad[0])
    weight_grad = term * gain_shard
    gain_grad = jnp.sum(term * weight_shard.astype(f32), axis=1)

    if isinstance(total, tuple):
        total = jnp.concatenate(total)
    average = total / lax.axis_size("replica")
    momentum_new = momentum_rate * outer_momentum + average
    global_new = global_params - outer_rate * (average + momentum_rate * momentum_new)
    local_new = (
        mixing_rate * local_params[0].astype(f32) + (1.0 - mixing_rate) * global_new
    ).astype(bf16)

    kv_out, input_grad = second_part(
        ring, tokens_in, kv_grad, inv, cosine, sine, blocks, plan, flags, shard
    )
    return (
        kv_out[None],
        input_grad[None],
        weight_grad[None],
        gain_grad[None],
        momentum_new,
        global_new,
        local_new[None],
    )


def solution(mesh):
    in_specs = (
        P("replica", "fsdp", None),
        P("replica", "fsdp"),
        P("replica", "fsdp", None),
        P("replica", "fsdp", None),
        P("replica", "fsdp", None),
        P("fsdp", None),
        P("fsdp", None),
        P("replica", "fsdp", None),
    )
    out_specs = (
        P("replica", "fsdp", None),
        P("replica", "fsdp", None),
        P("replica", "fsdp", None),
        P("replica", "fsdp"),
        P("fsdp", None),
        P("fsdp", None),
        P("replica", "fsdp", None),
    )
    return jax.shard_map(local, mesh=mesh, in_specs=in_specs, out_specs=out_specs, check_vma=False)
```

```python
import functools
import math

import jax
import jax.numpy as jnp
from jax import lax
from jax.experimental import pallas as pl
from jax.experimental.pallas import tpu as pltpu
from jax.sharding import PartitionSpec as P

HEAD = 128
SEQ_LEN = 4096


epsilon = 1e-05
rope_base = 500000.0
momentum_rate = 0.9
outer_rate = 0.7
mixing_rate = 0.5

f32, bf16 = jnp.float32, jnp.bfloat16


class Ring:
    def __init__(self):
        self.count = lax.axis_size("fsdp")
        self.half = self.count // 2
        walk = list(range(0, self.count, 2)) + list(range(self.count - 1, 0, -2))
        after = walk[1:] + walk[:1]
        self.right = list(zip(walk, after))
        self.left = list(zip(after, walk))
        self.me = lax.axis_index("fsdp")
        self.spot = jnp.where(
            self.me % 2 == 0, self.me // 2, self.count - 1 - self.me // 2
        )

    def devices_at(self, distances):
        spot = (self.spot + self.count + jnp.array(distances, jnp.int32)) % self.count
        return jnp.where(spot < self.half, 2 * spot, 2 * (self.count - 1 - spot) + 1)

    def to_right(self, value):
        return lax.ppermute(value, "fsdp", self.right)

    def to_left(self, value):
        return lax.ppermute(value, "fsdp", self.left)


class Plane(Ring):
    def __init__(self):
        super().__init__()
        self.at = [self.spot % 4 == i for i in range(4)]

    def over_chord(self, value):
        return lax.ppermute(value, "fsdp", [(2, 3), (3, 2), (4, 5), (5, 4)])


def after(value, *others):
    return lax.optimization_barrier((value, others))[0]


def rope_tables(positions):
    half = HEAD // 2
    index_f = jnp.arange(half, dtype=f32)
    inverse = jnp.exp(index_f * (-2.0 * math.log(rope_base) / HEAD))
    angle = positions.astype(f32)[:, None] * inverse[None, :]
    cosine, sine = jnp.cos(angle), jnp.sin(angle)
    return jnp.concatenate([cosine, cosine], axis=1), jnp.concatenate([-sine, sine], axis=1)


def first_kernel(scale, at, x, cotangent, cosine, sine, kv_grad, inv, far, near):
    step = pl.program_id(0)
    width = x.shape[1]
    shard = far.shape[0]
    kvw = cotangent.shape[1] // 2

    @pl.when(step == 0)
    def _():
        total = jnp.zeros((x.shape[0], HEAD), f32)
        for c in range(0, width, HEAD):
            part = x[:, c : c + HEAD].astype(f32)
            total = total + part * part
        mean = jnp.sum(total, axis=1, keepdims=True) / width
        inv[...] = jnp.broadcast_to(lax.rsqrt(mean + epsilon), inv.shape)
        for c in range(0, kvw, HEAD):
            part = cotangent[:, c : c + HEAD].astype(f32)
            turned = pltpu.roll(part, HEAD // 2, 1)
            kv_grad[:, c : c + HEAD] = (part * cosine[...] - turned * sine[...]).astype(bf16)
        kv_grad[:, kvw:] = cotangent[:, kvw:]

    block = x[:, pl.ds(pl.multiple_of(at[step] * shard, shard), shard)]
    normed = (block.astype(f32) * inv[:, :1]).astype(bf16)
    term = (
        lax.dot_general(normed, kv_grad[...], (((0,), (0,)), ((), ())), preferred_element_type=f32)
        * scale
    )

    @pl.when(step == 0)
    def _():
        far[...] = term.astype(bf16)

    @pl.when(step > 0)
    def _():
        near[0] = term


def first_part(ring, tokens_in, cotangent, cosine, sine, shard, scale):
    rows, width = tokens_in.shape
    cols = cotangent.shape[1]
    order = [ring.half]
    for d in range(ring.half - 1, 0, -1):
        order += [d, -d]
    order.append(0)
    n = ring.count
    fixed = lambda k, at: (0, 0)
    return pl.pallas_call(
        functools.partial(first_kernel, scale),
        grid_spec=pltpu.PrefetchScalarGridSpec(
            num_scalar_prefetch=1,
            grid=(n,),
            in_specs=[
                pl.BlockSpec((rows, width), fixed),
                pl.BlockSpec((rows, cols), fixed),
                pl.BlockSpec((rows, HEAD), fixed),
                pl.BlockSpec((rows, HEAD), fixed),
            ],
            out_specs=[
                pl.BlockSpec((rows, cols), fixed),
                pl.BlockSpec((rows, HEAD), fixed),
                pl.BlockSpec((shard, cols), fixed),
                pl.BlockSpec((1, shard, cols), lambda k, at: (jnp.maximum(k - 1, 0), 0, 0)),
            ],
        ),
        out_shape=[
            jax.ShapeDtypeStruct((rows, cols), bf16),
            jax.ShapeDtypeStruct((rows, HEAD), f32),
            jax.ShapeDtypeStruct((shard, cols), bf16),
            jax.ShapeDtypeStruct((n - 1, shard, cols), f32),
        ],
        compiler_params=pltpu.CompilerParams(vmem_limit_bytes=40 * 2**20),
        cost_estimate=pl.CostEstimate(
            flops=2 * rows * width * cols,
            bytes_accessed=2 * rows * width + 4 * width * cols,
            transcendentals=0,
        ),
        name="norm_and_weight_terms",
    )(ring.devices_at(order), tokens_in, cotangent, cosine, sine)


def last_kernel(count, own, weight, gain, *refs):
    came, (weight_grad, gain_grad) = refs[:count], refs[-2:]
    term = own[0]
    for ref in came:
        term = term + ref[...].astype(f32)
    product = term * weight[...].astype(f32)
    rows, cols = product.shape
    lanes = product[:, :HEAD]
    for c in range(HEAD, cols, HEAD):
        lanes = lanes + product[:, c : c + HEAD]
    gain_grad[...] = jnp.sum(lanes.T, axis=0, keepdims=True)
    gains = jnp.broadcast_to(gain[...].astype(f32), (8, rows)).T
    weight_grad[0] = term * gains[:, :1]


def last_part(near, weight, gain, sums):
    shard, cols = weight.shape
    many = len(sums)
    tile = HEAD
    tiles = shard // many // tile
    outs = None
    for h, came in enumerate(sums):
        row = lambda i, h=h: h * tiles + i
        specs = [
            pl.BlockSpec((1, tile, cols), lambda i, row=row: (near.shape[0] - 1, row(i), 0)),
            pl.BlockSpec((tile, cols), lambda i, row=row: (row(i), 0)),
            pl.BlockSpec((1, tile), lambda i, row=row: (0, row(i))),
        ]
        specs += [pl.BlockSpec((tile, cols), lambda i: (i, 0))] * len(came)
        operands = [near, weight, gain, *came]
        if outs is not None:
            specs += [pl.BlockSpec(memory_space=pl.ANY)] * 2
        outs = pl.pallas_call(
            functools.partial(last_kernel, len(came)),
            grid=(tiles,),
            in_specs=specs,
            out_specs=[
                pl.BlockSpec((1, tile, cols), lambda i, row=row: (0, row(i), 0)),
                pl.BlockSpec((1, tile), lambda i, row=row: (0, row(i))),
            ],
            out_shape=[
                jax.ShapeDtypeStruct((1, shard, cols), f32),
                jax.ShapeDtypeStruct((1, shard), f32),
            ],
            input_output_aliases=(
                {} if outs is None else {len(operands): 0, len(operands) + 1: 1}
            ),
            compiler_params=pltpu.CompilerParams(vmem_limit_bytes=16 * 2**20),
            cost_estimate=pl.CostEstimate(
                flops=shard // many * cols * 8,
                bytes_accessed=shard // many * cols * 14,
                transcendentals=0,
            ),
            name="sum_of_terms",
        )(*operands, *(outs or ()))
    return outs


def second_kernel(plan, at, x, kv_grad, inv, cosine, sine, *refs):
    n = len(plan)
    blocks, refs = refs[:-10], refs[-10:]
    kv_out, input_grad, xs, ws, ng, pre, out, x_sem, w_sem, o_sem = refs
    rows, width = x.shape
    shard = xs.shape[2]
    kvw = pre.shape[1] // 2

    def columns(k):
        return pl.ds(pl.multiple_of(at[k] * shard, shard), shard)

    def x_copy(k):
        return pltpu.make_async_copy(x.at[:, columns(k)], xs.at[k], x_sem.at[k])

    def o_copy(k):
        return pltpu.make_async_copy(out.at[k], input_grad.at[:, columns(k)], o_sem.at[k])

    for k in range(n):
        x_copy(k).start()
        for flag, block, start, stop in plan[k]:
            copy = pltpu.make_async_copy(blocks[block], ws.at[k, start:stop], w_sem.at[k])
            if flag is None:
                copy.start()
            else:

                @pl.when(at[n + flag] == 1)
                def _(copy=copy):
                    copy.start()

    pre[...] = jnp.zeros_like(pre)

    def gather(k, total):
        x_copy(k).wait()
        pltpu.make_async_copy(ws.at[k], ws.at[k], w_sem.at[k]).wait()
        weight = ws[k]
        normed = xs[k].astype(f32) * inv[:, :1]
        pre[...] += jnp.dot(normed.astype(bf16), weight, preferred_element_type=f32)
        grad = lax.dot_general(
            kv_grad[...], weight, (((1,), (1,)), ((), ())), preferred_element_type=f32
        )
        ng[k] = grad
        product = grad * normed
        for c in range(0, shard, HEAD):
            total = total + product[:, c : c + HEAD]
        return total

    total = lax.fori_loop(0, n, gather, jnp.zeros((rows, HEAD), f32))
    mean = jnp.sum(total, axis=1, keepdims=True) / width

    def finish(k, carry):
        scale = inv[:, :1]
        normed = xs[k].astype(f32) * scale
        out[k] = (scale * (ng[k] - normed * mean)).astype(bf16)
        o_copy(k).start()
        return carry

    lax.fori_loop(0, n, finish, 0)
    for c in range(0, kvw, HEAD):
        part = pre[:, c : c + HEAD]
        turned = pltpu.roll(part, HEAD // 2, 1)
        kv_out[:, c : c + HEAD] = (part * cosine[...] + turned * sine[...]).astype(bf16)
    kv_out[:, kvw:] = pre[:, kvw:].astype(bf16)

    def drain(k, carry):
        o_copy(k).wait()
        return carry

    lax.fori_loop(0, n, drain, 0)


def second_part(ring, tokens_in, kv_grad, inv, cosine, sine, blocks, plan, flags, shard):
    rows, width = tokens_in.shape
    cols = kv_grad.shape[1]
    n = ring.count
    order = [0]
    for d in range(1, ring.half):
        order += [-d, d]
    order.append(ring.half)
    at = jnp.concatenate([ring.devices_at(order).astype(jnp.int32), flags.astype(jnp.int32)])
    whole = pl.BlockSpec(memory_space=pltpu.VMEM)
    there = pl.BlockSpec(memory_space=pl.ANY)
    return pl.pallas_call(
        functools.partial(second_kernel, plan),
        in_specs=[pl.BlockSpec(memory_space=pltpu.SMEM), there]
        + [whole] * 4
        + [there] * len(blocks),
        out_specs=[whole, there],
        out_shape=[
            jax.ShapeDtypeStruct((rows, cols), bf16),
            jax.ShapeDtypeStruct((rows, width), bf16),
        ],
        scratch_shapes=[
            pltpu.VMEM((n, rows, shard), bf16),
            pltpu.VMEM((n, shard, cols), bf16),
            pltpu.VMEM((n, rows, shard), f32),
            pltpu.VMEM((rows, cols), f32),
            pltpu.VMEM((n, rows, shard), bf16),
            pltpu.SemaphoreType.DMA((n,)),
            pltpu.SemaphoreType.DMA((n,)),
            pltpu.SemaphoreType.DMA((n,)),
        ],
        compiler_params=pltpu.CompilerParams(vmem_limit_bytes=48 * 2**20),
        cost_estimate=pl.CostEstimate(
            flops=4 * rows * width * cols,
            bytes_accessed=4 * rows * width + 2 * width * cols,
            transcendentals=0,
        ),
        name="project_and_input_grad",
    )(at, tokens_in, kv_grad, inv, cosine, sine, *blocks)


def replica_sum(value, other):
    replicas = lax.axis_size("replica")
    if replicas != 4:
        total = lax.psum(value, "replica")
        return total, total
    swap = lambda v, step: lax.ppermute(v, "replica", [(r, r ^ step) for r in range(4)])
    odd = lax.axis_index("replica") % 2
    half = value.shape[0] // 2
    mine = lax.dynamic_slice_in_dim(value, odd * half, half, 0)
    theirs = lax.dynamic_slice_in_dim(value, (1 - odd) * half, half, 0)
    came = swap(theirs, 1)
    mine = mine + came
    mine = mine + after(swap(mine, 2), other)
    theirs = swap(mine, 1)
    low, high = jnp.where(odd == 0, mine, theirs), jnp.where(odd == 0, theirs, mine)
    return (low, high), came


def exchange_ring(ring, own, far, near, pseudo):
    total, _ = replica_sum(pseudo, far)
    shard, cut = own.shape[0], own.shape[0] // 2
    blocks = [own]
    from_left = from_right = own
    for d in range(1, ring.half):
        from_left, from_right = ring.to_right(from_left), ring.to_left(from_right)
        blocks += [from_left, from_right]
    from_left, from_right = after((from_left, from_right), total)
    blocks += [ring.to_right(from_left[:cut]), ring.to_left(from_right[cut:])]
    last = len(blocks) - 2
    plan = [((None, k, 0, shard),) for k in range(last)]
    plan.append(((None, last, 0, cut), (None, last + 1, cut, shard)))

    far = after(far, blocks[1], blocks[2])
    from_left, from_right = ring.to_right(far[:cut]), ring.to_left(far[cut:])
    for k in range(0, 2 * (ring.half - 1), 2):
        from_left, from_right = lax.optimization_barrier((from_left, from_right))
        if k == 0:
            from_left = jnp.pad(from_left, ((0, shard - cut), (0, 0)))
            from_right = jnp.pad(from_right, ((cut, 0), (0, 0)))
        from_left = ring.to_right((near[k] + from_left.astype(f32)).astype(bf16))
        from_right = ring.to_left((near[k + 1] + from_right.astype(f32)).astype(bf16))
    sums = [(from_left, from_right)]
    return blocks, plan, jnp.zeros((1,), jnp.int32), sums, total


def exchange_plane(plane, own, far, near, pseudo):
    shard = own.shape[0]
    at0, at1, at2, at3 = plane.at
    zero = jnp.zeros((), f32)
    pieces = [(0, shard // 2), (shard // 2, shard)]
    halves = range(2)
    wide = lambda v: v.astype(f32)
    pick = jnp.where
    sent, crossed = [own], [own]

    def part(value, h):
        return value[pieces[h][0] : pieces[h][1]]

    def later(*values):
        return after(values, sent[0])

    def links(to_right, to_left, chord=None):
        sent[0] = to_right, to_left
        came = [plane.to_right(to_right), plane.to_left(to_left)]
        if chord is not None:
            came.append(plane.over_chord(after(chord, sent[0], crossed[0])))
            crossed[0] = came[-1]
        return lax.optimization_barrier(came)

    first = links(own, own)
    total, came = replica_sum(after(pseudo, own), far)
    first, far, came = lax.optimization_barrier((first, far, came))
    one = [[part(came, h) for came in first] for h in halves]
    two = [links(*later(*one[h])) for h in halves]
    two[0], total = lax.optimization_barrier((two[0], total))
    chords = [part(own, h) for h in halves] + [pick(at2, *one[h]) for h in halves] + [part(far, h) for h in halves]
    chords += [part(pick(at1, near[1], near[0]).astype(bf16), h) for h in halves]
    three = []
    for h in halves:
        left, right = later(*two[h])
        terms = part(far, h)
        three.append(links(pick(at0, terms, left), pick(at3, terms, right), chords[h]))
    four = []
    for h in halves:
        left, right = later(*three[h][:2])
        to_right = wide(part(near[0], h)) + pick(at1, wide(left), zero)
        to_left = wide(part(near[1], h)) + pick(at2, wide(right), zero)
        to_right = pick(at2, left, to_right.astype(bf16))
        to_left = pick(at1, right, to_left.astype(bf16))
        four.append(links(to_right, to_left, chords[2 + h]))
    five = []
    for h in halves:
        left, right = later(*four[h][:2])
        to_right = part(near[2], h) + pick(at3, zero, wide(left))
        to_left = part(near[3], h) + pick(at0, zero, wide(right))
        five.append(links(to_right.astype(bf16), to_left.astype(bf16), chords[4 + h]))
    six = []
    for h in halves:
        left, right, chord = later(*five[h])
        chord = wide(chord)
        to_right = part(near[4], h) + wide(left) + pick(at1, chord, zero)
        to_left = part(near[5], h) + wide(right) + pick(at2, chord, zero)
        six.append(links(to_right.astype(bf16), to_left.astype(bf16), chords[6 + h]))

    blocks, plan = [], []

    def add(flag, arrays):
        entry = []
        for (start, stop), array in zip(pieces, arrays):
            entry.append((flag, len(blocks), start, stop))
            blocks.append(array)
        return entry

    for array in (own, *first):
        plan.append([(None, len(blocks), 0, shard)])
        blocks.append(array)
    for way in range(2):
        plan.append(add(None, [two[h][way] for h in halves]))
    partner = add(0, [three[h][2] for h in halves])
    for way in range(2):
        entry = [(way, *rest) for _, *rest in partner]
        plan.append(entry + add(2 + way, [three[h][way] for h in halves]))
    plan.append(add(4, [four[h][2] for h in halves]))
    for way in range(2):
        plan[-1] += add(5 + way, [four[h][way] for h in halves])
    flags = [at1, at2, ~at1, ~at2, at1 | at2, at3, at0]
    plan = tuple(tuple(entry) for entry in plan)
    return blocks, plan, jnp.stack(flags), six, total


def local(
    layer_input,
    norm_gain,
    kv_weight,
    kv_cotangent,
    pseudo_grad,
    outer_momentum,
    global_params,
    local_params,
):
    small = lax.axis_size("fsdp") == 8
    ring = Plane() if small else Ring()
    tokens_in = layer_input[0]
    gain_shard = norm_gain[0].astype(f32)[:, None]
    weight_shard = kv_weight[0]
    cotangent = kv_cotangent[0]
    rows, width = tokens_in.shape
    shard, cols = weight_shard.shape

    own = (weight_shard.astype(f32) * gain_shard).astype(bf16)
    positions = (ring.me * rows + jnp.arange(rows, dtype=jnp.int32)) % SEQ_LEN
    cosine, sine = rope_tables(positions)
    scale = 1.0 / math.sqrt(rows * ring.count)
    kv_grad, inv, far, near = first_part(
        ring, tokens_in, cotangent, cosine, sine, shard, scale
    )
    exchange = exchange_plane if small else exchange_ring
    blocks, plan, flags, sums, total = exchange(
        ring, own, far, near, pseudo_grad[0]
    )
    weight_grad, gain_grad = last_part(near, weight_shard, norm_gain, sums)

    if isinstance(total, tuple):
        total = jnp.concatenate(total)
    average = total / lax.axis_size("replica")
    momentum_new = momentum_rate * outer_momentum + average
    global_new = global_params - outer_rate * (average + momentum_rate * momentum_new)
    local_new = (
        mixing_rate * local_params[0].astype(f32) + (1.0 - mixing_rate) * global_new
    ).astype(bf16)

    kv_out, input_grad = second_part(
        ring, tokens_in, kv_grad, inv, cosine, sine, blocks, plan, flags, shard
    )
    return (
        kv_out[None],
        input_grad[None],
        weight_grad,
        gain_grad,
        momentum_new,
        global_new,
        local_new[None],
    )


def solution(mesh):
    in_specs = (
        P("replica", "fsdp", None),
        P("replica", "fsdp"),
        P("replica", "fsdp", None),
        P("replica", "fsdp", None),
        P("replica", "fsdp", None),
        P("fsdp", None),
        P("fsdp", None),
        P("replica", "fsdp", None),
    )
    out_specs = (
        P("replica", "fsdp", None),
        P("replica", "fsdp", None),
        P("replica", "fsdp", None),
        P("replica", "fsdp"),
        P("fsdp", None),
        P("fsdp", None),
        P("replica", "fsdp", None),
    )
    return jax.shard_map(local, mesh=mesh, in_specs=in_specs, out_specs=out_specs, check_vma=False)
```

```python
import functools
import math

import jax
import jax.numpy as jnp
from jax import lax
from jax.experimental import pallas as pl
from jax.experimental.pallas import tpu as pltpu
from jax.sharding import PartitionSpec as P

HEAD = 128
SEQ_LEN = 4096


epsilon = 1e-05
rope_base = 500000.0
momentum_rate = 0.9
outer_rate = 0.7
mixing_rate = 0.5

f32, bf16 = jnp.float32, jnp.bfloat16


class Ring:
    def __init__(self):
        self.count = lax.axis_size("fsdp")
        self.half = self.count // 2
        walk = list(range(0, self.count, 2)) + list(range(self.count - 1, 0, -2))
        after = walk[1:] + walk[:1]
        self.right = list(zip(walk, after))
        self.left = list(zip(after, walk))
        self.me = lax.axis_index("fsdp")
        self.spot = jnp.where(
            self.me % 2 == 0, self.me // 2, self.count - 1 - self.me // 2
        )

    def devices_at(self, distances):
        spot = (self.spot + self.count + jnp.array(distances, jnp.int32)) % self.count
        return jnp.where(spot < self.half, 2 * spot, 2 * (self.count - 1 - spot) + 1)

    def to_right(self, value):
        return lax.ppermute(value, "fsdp", self.right)

    def to_left(self, value):
        return lax.ppermute(value, "fsdp", self.left)


class Plane(Ring):
    def __init__(self):
        super().__init__()
        self.at = [self.spot % 4 == i for i in range(4)]

    def over_chord(self, value):
        return lax.ppermute(value, "fsdp", [(2, 3), (3, 2), (4, 5), (5, 4)])


def after(value, *others):
    return lax.optimization_barrier((value, others))[0]


def rope_tables(positions):
    half = HEAD // 2
    index_f = jnp.arange(half, dtype=f32)
    inverse = jnp.exp(index_f * (-2.0 * math.log(rope_base) / HEAD))
    angle = positions.astype(f32)[:, None] * inverse[None, :]
    cosine, sine = jnp.cos(angle), jnp.sin(angle)
    return jnp.concatenate([cosine, cosine], axis=1), jnp.concatenate([-sine, sine], axis=1)


def first_kernel(scale, at, x, cotangent, cosine, sine, kv_grad, inv, far, near):
    step = pl.program_id(0)
    width = x.shape[1]
    shard = far.shape[0]
    kvw = cotangent.shape[1] // 2

    @pl.when(step == 0)
    def _():
        total = jnp.zeros((x.shape[0], HEAD), f32)
        for c in range(0, width, HEAD):
            part = x[:, c : c + HEAD].astype(f32)
            total = total + part * part
        mean = jnp.sum(total, axis=1, keepdims=True) / width
        inv[...] = jnp.broadcast_to(lax.rsqrt(mean + epsilon), inv.shape)
        for c in range(0, kvw, HEAD):
            part = cotangent[:, c : c + HEAD].astype(f32)
            turned = pltpu.roll(part, HEAD // 2, 1)
            kv_grad[:, c : c + HEAD] = (part * cosine[...] - turned * sine[...]).astype(bf16)
        kv_grad[:, kvw:] = cotangent[:, kvw:]

    block = x[:, pl.ds(pl.multiple_of(at[step] * shard, shard), shard)]
    normed = (block.astype(f32) * inv[:, :1]).astype(bf16)
    term = (
        lax.dot_general(normed, kv_grad[...], (((0,), (0,)), ((), ())), preferred_element_type=f32)
        * scale
    )

    @pl.when(step == 0)
    def _():
        far[...] = term.astype(bf16)

    @pl.when(step > 0)
    def _():
        near[0] = term


def first_part(ring, tokens_in, cotangent, cosine, sine, shard, scale):
    rows, width = tokens_in.shape
    cols = cotangent.shape[1]
    order = [ring.half]
    for d in range(ring.half - 1, 0, -1):
        order += [d, -d]
    order.append(0)
    n = ring.count
    fixed = lambda k, at: (0, 0)
    return pl.pallas_call(
        functools.partial(first_kernel, scale),
        grid_spec=pltpu.PrefetchScalarGridSpec(
            num_scalar_prefetch=1,
            grid=(n,),
            in_specs=[
                pl.BlockSpec((rows, width), fixed),
                pl.BlockSpec((rows, cols), fixed),
                pl.BlockSpec((rows, HEAD), fixed),
                pl.BlockSpec((rows, HEAD), fixed),
            ],
            out_specs=[
                pl.BlockSpec((rows, cols), fixed),
                pl.BlockSpec((rows, HEAD), fixed),
                pl.BlockSpec((shard, cols), fixed),
                pl.BlockSpec((1, shard, cols), lambda k, at: (jnp.maximum(k - 1, 0), 0, 0)),
            ],
        ),
        out_shape=[
            jax.ShapeDtypeStruct((rows, cols), bf16),
            jax.ShapeDtypeStruct((rows, HEAD), f32),
            jax.ShapeDtypeStruct((shard, cols), bf16),
            jax.ShapeDtypeStruct((n - 1, shard, cols), f32),
        ],
        compiler_params=pltpu.CompilerParams(vmem_limit_bytes=40 * 2**20),
        cost_estimate=pl.CostEstimate(
            flops=2 * rows * width * cols,
            bytes_accessed=2 * rows * width + 4 * width * cols,
            transcendentals=0,
        ),
        name="norm_and_weight_terms",
    )(ring.devices_at(order), tokens_in, cotangent, cosine, sine)


def last_kernel(count, own, weight, gain, *refs):
    came, (weight_grad, gain_grad) = refs[:count], refs[-2:]
    term = own[0]
    for ref in came:
        term = term + ref[...].astype(f32)
    product = term * weight[...].astype(f32)
    rows, cols = product.shape
    lanes = product[:, :HEAD]
    for c in range(HEAD, cols, HEAD):
        lanes = lanes + product[:, c : c + HEAD]
    gain_grad[...] = jnp.sum(lanes.T, axis=0, keepdims=True)
    gains = jnp.broadcast_to(gain[...].astype(f32), (8, rows)).T
    weight_grad[0] = term * gains[:, :1]


def last_part(near, weight, gain, sums):
    shard, cols = weight.shape
    many = len(sums)
    tile = HEAD
    tiles = shard // many // tile
    outs = None
    for h, came in enumerate(sums):
        row = lambda i, h=h: h * tiles + i
        specs = [
            pl.BlockSpec((1, tile, cols), lambda i, row=row: (near.shape[0] - 1, row(i), 0)),
            pl.BlockSpec((tile, cols), lambda i, row=row: (row(i), 0)),
            pl.BlockSpec((1, tile), lambda i, row=row: (0, row(i))),
        ]
        specs += [pl.BlockSpec((tile, cols), lambda i: (i, 0))] * len(came)
        operands = [near, weight, gain, *came]
        if outs is not None:
            specs += [pl.BlockSpec(memory_space=pl.ANY)] * 2
        outs = pl.pallas_call(
            functools.partial(last_kernel, len(came)),
            grid=(tiles,),
            in_specs=specs,
            out_specs=[
                pl.BlockSpec((1, tile, cols), lambda i, row=row: (0, row(i), 0)),
                pl.BlockSpec((1, tile), lambda i, row=row: (0, row(i))),
            ],
            out_shape=[
                jax.ShapeDtypeStruct((1, shard, cols), f32),
                jax.ShapeDtypeStruct((1, shard), f32),
            ],
            input_output_aliases=(
                {} if outs is None else {len(operands): 0, len(operands) + 1: 1}
            ),
            compiler_params=pltpu.CompilerParams(vmem_limit_bytes=16 * 2**20),
            cost_estimate=pl.CostEstimate(
                flops=shard // many * cols * 8,
                bytes_accessed=shard // many * cols * 14,
                transcendentals=0,
            ),
            name="sum_of_terms",
        )(*operands, *(outs or ()))
    return outs


def second_kernel(plan, at, x, kv_grad, inv, cosine, sine, *refs):
    n = len(plan)
    blocks, refs = refs[:-10], refs[-10:]
    kv_out, input_grad, xs, ws, ng, pre, out, x_sem, w_sem, o_sem = refs
    rows, width = x.shape
    shard = xs.shape[2]
    kvw = pre.shape[1] // 2

    def columns(k):
        return pl.ds(pl.multiple_of(at[k] * shard, shard), shard)

    def x_copy(k):
        return pltpu.make_async_copy(x.at[:, columns(k)], xs.at[k], x_sem.at[k])

    def o_copy(k):
        return pltpu.make_async_copy(out.at[k], input_grad.at[:, columns(k)], o_sem.at[k])

    for k in range(n):
        x_copy(k).start()
        for flag, block, start, stop in plan[k]:
            copy = pltpu.make_async_copy(blocks[block], ws.at[k, start:stop], w_sem.at[k])
            if flag is None:
                copy.start()
            else:

                @pl.when(at[n + flag] == 1)
                def _(copy=copy):
                    copy.start()

    pre[...] = jnp.zeros_like(pre)

    def gather(k, total):
        x_copy(k).wait()
        pltpu.make_async_copy(ws.at[k], ws.at[k], w_sem.at[k]).wait()
        weight = ws[k]
        normed = xs[k].astype(f32) * inv[:, :1]
        pre[...] += jnp.dot(normed.astype(bf16), weight, preferred_element_type=f32)
        grad = lax.dot_general(
            kv_grad[...], weight, (((1,), (1,)), ((), ())), preferred_element_type=f32
        )
        ng[k] = grad
        product = grad * normed
        for c in range(0, shard, HEAD):
            total = total + product[:, c : c + HEAD]
        return total

    total = lax.fori_loop(0, n, gather, jnp.zeros((rows, HEAD), f32))
    mean = jnp.sum(total, axis=1, keepdims=True) / width

    def finish(k, carry):
        scale = inv[:, :1]
        normed = xs[k].astype(f32) * scale
        out[k] = (scale * (ng[k] - normed * mean)).astype(bf16)
        o_copy(k).start()
        return carry

    lax.fori_loop(0, n, finish, 0)
    for c in range(0, kvw, HEAD):
        part = pre[:, c : c + HEAD]
        turned = pltpu.roll(part, HEAD // 2, 1)
        kv_out[:, c : c + HEAD] = (part * cosine[...] + turned * sine[...]).astype(bf16)
    kv_out[:, kvw:] = pre[:, kvw:].astype(bf16)

    def drain(k, carry):
        o_copy(k).wait()
        return carry

    lax.fori_loop(0, n, drain, 0)


def second_part(ring, tokens_in, kv_grad, inv, cosine, sine, blocks, plan, flags, shard):
    rows, width = tokens_in.shape
    cols = kv_grad.shape[1]
    n = ring.count
    order = [0]
    for d in range(1, ring.half):
        order += [-d, d]
    order.append(ring.half)
    at = jnp.concatenate([ring.devices_at(order).astype(jnp.int32), flags.astype(jnp.int32)])
    whole = pl.BlockSpec(memory_space=pltpu.VMEM)
    there = pl.BlockSpec(memory_space=pl.ANY)
    return pl.pallas_call(
        functools.partial(second_kernel, plan),
        in_specs=[pl.BlockSpec(memory_space=pltpu.SMEM), there]
        + [whole] * 4
        + [there] * len(blocks),
        out_specs=[whole, there],
        out_shape=[
            jax.ShapeDtypeStruct((rows, cols), bf16),
            jax.ShapeDtypeStruct((rows, width), bf16),
        ],
        scratch_shapes=[
            pltpu.VMEM((n, rows, shard), bf16),
            pltpu.VMEM((n, shard, cols), bf16),
            pltpu.VMEM((n, rows, shard), f32),
            pltpu.VMEM((rows, cols), f32),
            pltpu.VMEM((n, rows, shard), bf16),
            pltpu.SemaphoreType.DMA((n,)),
            pltpu.SemaphoreType.DMA((n,)),
            pltpu.SemaphoreType.DMA((n,)),
        ],
        compiler_params=pltpu.CompilerParams(vmem_limit_bytes=48 * 2**20),
        cost_estimate=pl.CostEstimate(
            flops=4 * rows * width * cols,
            bytes_accessed=4 * rows * width + 2 * width * cols,
            transcendentals=0,
        ),
        name="project_and_input_grad",
    )(at, tokens_in, kv_grad, inv, cosine, sine, *blocks)


def replica_pairs(value, odd):
    swap = lambda v, step: lax.ppermute(v, "replica", [(r, r ^ step) for r in range(4)])
    half = value.shape[0] // 2
    mine = lax.dynamic_slice_in_dim(value, odd * half, half, 0)
    theirs = lax.dynamic_slice_in_dim(value, (1 - odd) * half, half, 0)
    mine = mine + swap(theirs, 1)
    return mine, swap(mine, 2)


def replica_halves(mine, odd):
    theirs = lax.ppermute(mine, "replica", [(r, r ^ 1) for r in range(4)])
    return jnp.where(odd, theirs, mine), jnp.where(odd, mine, theirs)


def exchange_ring(ring, own, far, near, pseudo):
    total = lax.psum(pseudo, "replica")
    shard, cut = own.shape[0], own.shape[0] // 2
    blocks = [own]
    from_left = from_right = own
    for d in range(1, ring.half):
        from_left, from_right = ring.to_right(from_left), ring.to_left(from_right)
        blocks += [from_left, from_right]
    from_left, from_right = after((from_left, from_right), total)
    blocks += [ring.to_right(from_left[:cut]), ring.to_left(from_right[cut:])]
    last = len(blocks) - 2
    plan = [((None, k, 0, shard),) for k in range(last)]
    plan.append(((None, last, 0, cut), (None, last + 1, cut, shard)))

    far = after(far, blocks[1], blocks[2])
    from_left, from_right = ring.to_right(far[:cut]), ring.to_left(far[cut:])
    for k in range(0, 2 * (ring.half - 1), 2):
        from_left, from_right = lax.optimization_barrier((from_left, from_right))
        if k == 0:
            from_left = jnp.pad(from_left, ((0, shard - cut), (0, 0)))
            from_right = jnp.pad(from_right, ((cut, 0), (0, 0)))
        from_left = ring.to_right((near[k] + from_left.astype(f32)).astype(bf16))
        from_right = ring.to_left((near[k + 1] + from_right.astype(f32)).astype(bf16))
    sums = [(from_left, from_right)]
    return blocks, plan, jnp.zeros((1,), jnp.int32), sums, total


def exchange_plane(plane, own, far, near, pseudo):
    shard = own.shape[0]
    at0, at1, at2, at3 = plane.at
    zero = jnp.zeros((), f32)
    pieces = [(0, shard // 2), (shard // 2, shard)]
    halves = range(2)
    wide = lambda v: v.astype(f32)
    pick = jnp.where
    sent = [own]

    def part(value, h):
        return value[pieces[h][0] : pieces[h][1]]

    def later(*values):
        return after(values, sent[0])

    def ring(to_right, to_left):
        sent[0] = to_right, to_left
        return lax.optimization_barrier([plane.to_right(to_right), plane.to_left(to_left)])

    def chord(value, *others):
        return plane.over_chord(after(value, sent[0], *others))

    first = ring(own, own)
    partner = chord(own)
    odd = lax.axis_index("replica") % 2 == 1
    sum_over = lax.axis_size("replica") == 4
    if sum_over:
        mine, came = replica_pairs(after(pseudo, own), odd.astype(jnp.int32))
    else:
        came = total = lax.psum(pseudo, "replica")
    first, partner, far, came = lax.optimization_barrier((first, partner, far, came))
    one = [[part(side, h) for side in first] for h in halves]
    two = [ring(*later(*one[0]))]
    if sum_over:
        total = replica_halves(mine + came, odd)
    one[1], total = lax.optimization_barrier((one[1], total))
    two.append(ring(*later(*one[1])))
    from_inner = chord(far, total)
    three = []
    for h in halves:
        left, right = later(*two[h])
        terms = part(far, h)
        three.append(ring(pick(at0, terms, left), pick(at3, terms, right)))
    three[0], from_inner = lax.optimization_barrier((three[0], from_inner))
    four = []
    for h in halves:
        left, right = later(*three[h])
        to_right = wide(part(near[0], h)) + pick(at1, wide(left), zero)
        to_left = wide(part(near[1], h)) + pick(at2, wide(right), zero)
        to_right = pick(at2, left, to_right.astype(bf16))
        to_left = pick(at1, right, to_left.astype(bf16))
        four.append(ring(to_right, to_left))
        if h == 0:
            join = jnp.concatenate([pick(at2, *one[g]) for g in halves])
            far_inner = chord(join, from_inner)
    five = []
    for h in halves:
        if h == 1:
            four[1], far_inner = lax.optimization_barrier((four[1], far_inner))
        left, right = later(*four[h])
        to_right = part(near[2], h) + pick(at3, zero, wide(left))
        to_left = part(near[3], h) + pick(at0, zero, wide(right))
        five.append(ring(to_right.astype(bf16), to_left.astype(bf16)))
    six, from_partner = [], []
    for h in halves:
        for_partner = pick(at1, part(near[1], h), part(near[0], h)).astype(bf16)
        from_partner.append(chord(for_partner, far_inner, *from_partner))
        left, right = later(*five[h])
        over = wide(part(from_inner, h))
        to_right = part(near[4], h) + wide(left) + pick(at1, over, zero)
        to_left = part(near[5], h) + wide(right) + pick(at2, over, zero)
        six.append(ring(to_right.astype(bf16), to_left.astype(bf16)))
    sums = [(*six[h], from_partner[h]) for h in halves]

    blocks, plan = [], []

    def add(flag, arrays):
        entry = []
        for (start, stop), array in zip(pieces, arrays):
            entry.append((flag, len(blocks), start, stop))
            blocks.append(array)
        return entry

    for array in (own, *first, partner):
        plan.append([(None, len(blocks), 0, shard)])
        blocks.append(array)
    plan.pop()
    for way in range(2):
        plan.append(add(None, [two[h][way] for h in halves]))
    for way in range(2):
        plan.append([(way, 3, 0, shard)] + add(2 + way, [three[h][way] for h in halves]))
    plan.append([(4, len(blocks), 0, shard)])
    blocks.append(far_inner)
    for way in range(2):
        plan[-1] += add(5 + way, [four[h][way] for h in halves])
    flags = [at1, at2, ~at1, ~at2, at1 | at2, at3, at0]
    plan = tuple(tuple(entry) for entry in plan)
    return blocks, plan, jnp.stack(flags), sums, total


def local(
    layer_input,
    norm_gain,
    kv_weight,
    kv_cotangent,
    pseudo_grad,
    outer_momentum,
    global_params,
    local_params,
):
    small = lax.axis_size("fsdp") == 8
    ring = Plane() if small else Ring()
    tokens_in = layer_input[0]
    gain_shard = norm_gain[0].astype(f32)[:, None]
    weight_shard = kv_weight[0]
    cotangent = kv_cotangent[0]
    rows, width = tokens_in.shape
    shard, cols = weight_shard.shape

    own = (weight_shard.astype(f32) * gain_shard).astype(bf16)
    positions = (ring.me * rows + jnp.arange(rows, dtype=jnp.int32)) % SEQ_LEN
    cosine, sine = rope_tables(positions)
    scale = 1.0 / math.sqrt(rows * ring.count)
    kv_grad, inv, far, near = first_part(
        ring, tokens_in, cotangent, cosine, sine, shard, scale
    )
    exchange = exchange_plane if small else exchange_ring
    blocks, plan, flags, sums, total = exchange(
        ring, own, far, near, pseudo_grad[0]
    )
    weight_grad, gain_grad = last_part(near, weight_shard, norm_gain, sums)

    if isinstance(total, tuple):
        total = jnp.concatenate(total)
    average = total / lax.axis_size("replica")
    momentum_new = momentum_rate * outer_momentum + average
    global_new = global_params - outer_rate * (average + momentum_rate * momentum_new)
    local_new = (
        mixing_rate * local_params[0].astype(f32) + (1.0 - mixing_rate) * global_new
    ).astype(bf16)

    kv_out, input_grad = second_part(
        ring, tokens_in, kv_grad, inv, cosine, sine, blocks, plan, flags, shard
    )
    return (
        kv_out[None],
        input_grad[None],
        weight_grad,
        gain_grad,
        momentum_new,
        global_new,
        local_new[None],
    )


def solution(mesh):
    in_specs = (
        P("replica", "fsdp", None),
        P("replica", "fsdp"),
        P("replica", "fsdp", None),
        P("replica", "fsdp", None),
        P("replica", "fsdp", None),
        P("fsdp", None),
        P("fsdp", None),
        P("replica", "fsdp", None),
    )
    out_specs = (
        P("replica", "fsdp", None),
        P("replica", "fsdp", None),
        P("replica", "fsdp", None),
        P("replica", "fsdp"),
        P("fsdp", None),
        P("fsdp", None),
        P("replica", "fsdp", None),
    )
    return jax.shard_map(local, mesh=mesh, in_specs=in_specs, out_specs=out_specs, check_vma=False)
```

```python
import functools
import math

import jax
import jax.numpy as jnp
from jax import lax
from jax.experimental import pallas as pl
from jax.experimental.pallas import tpu as pltpu
from jax.sharding import PartitionSpec as P

HEAD = 128
SEQ_LEN = 4096


FLAGS = 7

epsilon = 1e-05
rope_base = 500000.0
momentum_rate = 0.9
outer_rate = 0.7
mixing_rate = 0.5

f32, bf16 = jnp.float32, jnp.bfloat16


class Ring:
    def __init__(self):
        self.count = lax.axis_size("fsdp")
        self.half = self.count // 2
        walk = list(range(0, self.count, 2)) + list(range(self.count - 1, 0, -2))
        after = walk[1:] + walk[:1]
        self.right = list(zip(walk, after))
        self.left = list(zip(after, walk))
        self.me = lax.axis_index("fsdp")
        self.spot = jnp.where(
            self.me % 2 == 0, self.me // 2, self.count - 1 - self.me // 2
        )

    def devices_at(self, distances):
        spot = (self.spot + self.count + jnp.array(distances, jnp.int32)) % self.count
        return jnp.where(spot < self.half, 2 * spot, 2 * (self.count - 1 - spot) + 1)

    def to_right(self, value):
        return lax.ppermute(value, "fsdp", self.right)

    def to_left(self, value):
        return lax.ppermute(value, "fsdp", self.left)


class Plane(Ring):
    def __init__(self):
        super().__init__()
        self.at = [self.spot % 4 == i for i in range(4)]

    def over_chord(self, value):
        return lax.ppermute(value, "fsdp", [(2, 3), (3, 2), (4, 5), (5, 4)])


def after(value, *others):
    return lax.optimization_barrier((value, others))[0]


def rope_tables(positions):
    half = HEAD // 2
    index_f = jnp.arange(half, dtype=f32)
    inverse = jnp.exp(index_f * (-2.0 * math.log(rope_base) / HEAD))
    angle = positions.astype(f32)[:, None] * inverse[None, :]
    cosine, sine = jnp.cos(angle), jnp.sin(angle)
    return jnp.concatenate([cosine, cosine], axis=1), jnp.concatenate([-sine, sine], axis=1)


def first_kernel(scale, at, x, cotangent, cosine, sine, kv_grad, inv, far, near, last):
    step = pl.program_id(0)
    width = x.shape[1]
    shard = far.shape[0]
    kvw = cotangent.shape[1] // 2

    @pl.when(step == 0)
    def _():
        total = jnp.zeros((x.shape[0], HEAD), f32)
        for c in range(0, width, HEAD):
            part = x[:, c : c + HEAD].astype(f32)
            total = total + part * part
        mean = jnp.sum(total, axis=1, keepdims=True) / width
        inv[...] = jnp.broadcast_to(lax.rsqrt(mean + epsilon), inv.shape)
        for c in range(0, kvw, HEAD):
            part = cotangent[:, c : c + HEAD].astype(f32)
            turned = pltpu.roll(part, HEAD // 2, 1)
            kv_grad[:, c : c + HEAD] = (part * cosine[...] - turned * sine[...]).astype(bf16)
        kv_grad[:, kvw:] = cotangent[:, kvw:]

    block = x[:, pl.ds(pl.multiple_of(at[step] * shard, shard), shard)]
    normed = (block.astype(f32) * inv[:, :1]).astype(bf16)
    term = (
        lax.dot_general(normed, kv_grad[...], (((0,), (0,)), ((), ())), preferred_element_type=f32)
        * scale
    )

    @pl.when(step == 0)
    def _():
        far[...] = term.astype(bf16)

    @pl.when((step > 0) & (step < pl.num_programs(0) - 1))
    def _():
        near[0] = term

    @pl.when(step == pl.num_programs(0) - 1)
    def _():
        last[...] = term


def first_part(ring, tokens_in, cotangent, cosine, sine, shard, scale):
    rows, width = tokens_in.shape
    cols = cotangent.shape[1]
    order = [ring.half]
    for d in range(ring.half - 1, 0, -1):
        order += [d, -d]
    order.append(0)
    n = ring.count
    fixed = lambda k, at: (0, 0)
    return pl.pallas_call(
        functools.partial(first_kernel, scale),
        grid_spec=pltpu.PrefetchScalarGridSpec(
            num_scalar_prefetch=1,
            grid=(n,),
            in_specs=[
                pl.BlockSpec((rows, width), fixed),
                pl.BlockSpec((rows, cols), fixed),
                pl.BlockSpec((rows, HEAD), fixed),
                pl.BlockSpec((rows, HEAD), fixed),
            ],
            out_specs=[
                pl.BlockSpec((rows, cols), fixed),
                pl.BlockSpec((rows, HEAD), fixed),
                pl.BlockSpec((shard, cols), fixed),
                pl.BlockSpec((1, shard, cols), lambda k, at: (jnp.clip(k - 1, 0, n - 3), 0, 0)),
                pl.BlockSpec((shard, cols), fixed),
            ],
        ),
        out_shape=[
            jax.ShapeDtypeStruct((rows, cols), bf16),
            jax.ShapeDtypeStruct((rows, HEAD), f32),
            jax.ShapeDtypeStruct((shard, cols), bf16),
            jax.ShapeDtypeStruct((n - 2, shard, cols), f32),
            jax.ShapeDtypeStruct((shard, cols), f32),
        ],
        compiler_params=pltpu.CompilerParams(vmem_limit_bytes=40 * 2**20),
        cost_estimate=pl.CostEstimate(
            flops=2 * rows * width * cols,
            bytes_accessed=2 * rows * width + 4 * width * cols,
            transcendentals=0,
        ),
        name="norm_and_weight_terms",
    )(ring.devices_at(order), tokens_in, cotangent, cosine, sine)


def last_kernel(count, own, weight, gain, *refs):
    came, (weight_grad, gain_grad) = refs[:count], refs[-2:]
    term = own[...]
    for ref in came:
        term = term + ref[...].astype(f32)
    product = term * weight[...].astype(f32)
    rows, cols = product.shape
    lanes = product[:, :HEAD]
    for c in range(HEAD, cols, HEAD):
        lanes = lanes + product[:, c : c + HEAD]
    gain_grad[...] = jnp.sum(lanes.T, axis=0, keepdims=True)
    gains = jnp.broadcast_to(gain[...].astype(f32), (8, rows)).T
    weight_grad[0] = term * gains[:, :1]


def last_part(own, weight, gain, sums):
    shard, cols = weight.shape
    many = len(sums)
    tile = HEAD
    tiles = shard // many // tile
    outs = None
    for h, came in enumerate(sums):
        row = lambda i, h=h: h * tiles + i
        specs = [
            pl.BlockSpec((tile, cols), lambda i, row=row: (row(i), 0)),
            pl.BlockSpec((tile, cols), lambda i, row=row: (row(i), 0)),
            pl.BlockSpec((1, tile), lambda i, row=row: (0, row(i))),
        ]
        specs += [pl.BlockSpec((tile, cols), lambda i: (i, 0))] * len(came)
        operands = [own, weight, gain, *came]
        if outs is not None:
            specs += [pl.BlockSpec(memory_space=pl.ANY)] * 2
        outs = pl.pallas_call(
            functools.partial(last_kernel, len(came)),
            grid=(tiles,),
            in_specs=specs,
            out_specs=[
                pl.BlockSpec((1, tile, cols), lambda i, row=row: (0, row(i), 0)),
                pl.BlockSpec((1, tile), lambda i, row=row: (0, row(i))),
            ],
            out_shape=[
                jax.ShapeDtypeStruct((1, shard, cols), f32),
                jax.ShapeDtypeStruct((1, shard), f32),
            ],
            input_output_aliases=(
                {} if outs is None else {len(operands): 0, len(operands) + 1: 1}
            ),
            compiler_params=pltpu.CompilerParams(vmem_limit_bytes=16 * 2**20),
            cost_estimate=pl.CostEstimate(
                flops=shard // many * cols * 8,
                bytes_accessed=shard // many * cols * 14,
                transcendentals=0,
            ),
            name="sum_of_terms",
        )(*operands, *(outs or ()))
    return outs


def part_kernel(plan, before, finish, at, x, kv_grad, inv, cosine, sine, *refs):
    here = len(plan)
    done = sum(before)
    n = done + here
    total_at = len(refs) - (8 if not finish else 9)
    blocks, refs = refs[:total_at], refs[total_at:]
    if before:
        pre0, sums0, *grads0 = blocks[: 2 + len(before)]
        blocks = blocks[2 + len(before) :]
    if finish:
        kv_out, input_grad, xs, ws, ng, pre, x_sem, w_sem, g_sem = refs
    else:
        pre, sums, grads, xs, ws, x_sem, w_sem, g_sem = refs
    rows, width = x.shape
    shard = xs.shape[2]
    kvw = pre.shape[1] // 2
    held = range(n) if finish else range(done, n)
    base = held[0]

    def columns(k):
        return pl.ds(pl.multiple_of(at[k] * shard, shard), shard)

    def x_copy(k):
        return pltpu.make_async_copy(x.at[:, columns(k)], xs.at[k - base], x_sem.at[k - base])

    def o_copy(k):
        return pltpu.make_async_copy(xs.at[k], input_grad.at[:, columns(k)], x_sem.at[k])

    for k in range(done, n):
        x_copy(k).start()
        for flag, block, start, stop in plan[k - done]:
            slot = k - done
            copy = pltpu.make_async_copy(blocks[block], ws.at[slot, start:stop], w_sem.at[slot])
            if flag is None:
                copy.start()
            else:

                @pl.when(at[at.shape[0] - FLAGS + flag] == 1)
                def _(copy=copy):
                    copy.start()

    if before:
        pre[...] = pre0[...]
        start = sums0[...]
    else:
        pre[...] = jnp.zeros_like(pre)
        start = jnp.zeros((rows, HEAD), f32)
    loads = []
    if finish:
        slot = 0
        for j, count in enumerate(before):
            loads.append(
                pltpu.make_async_copy(grads0[j], ng.at[slot : slot + count], g_sem.at[j])
            )
            slot += count
        for load in loads:
            load.start()
        for k in range(done):
            x_copy(k).start()

    def gather(i, total):
        k = done + i
        x_copy(k).wait()
        pltpu.make_async_copy(ws.at[i], ws.at[i], w_sem.at[i]).wait()
        weight = ws[i]
        normed = xs[k - base].astype(f32) * inv[:, :1]
        pre[...] += jnp.dot(normed.astype(bf16), weight, preferred_element_type=f32)
        grad = lax.dot_general(
            kv_grad[...], weight, (((1,), (1,)), ((), ())), preferred_element_type=f32
        )
        if finish:
            ng[k] = grad
        else:
            grads[i] = grad
        product = grad * normed
        for c in range(0, shard, HEAD):
            total = total + product[:, c : c + HEAD]
        return total

    total = lax.fori_loop(0, here, gather, start)
    if not finish:
        sums[...] = total
        return
    mean = jnp.sum(total, axis=1, keepdims=True) / width
    for load in loads:
        load.wait()

    def write(k, carry):
        @pl.when(k < done)
        def _():
            x_copy(k).wait()

        scale = inv[:, :1]
        normed = xs[k].astype(f32) * scale
        xs[k] = (scale * (ng[k] - normed * mean)).astype(bf16)
        o_copy(k).start()
        return carry

    lax.fori_loop(0, n, write, 0)
    for c in range(0, kvw, HEAD):
        part = pre[:, c : c + HEAD]
        turned = pltpu.roll(part, HEAD // 2, 1)
        kv_out[:, c : c + HEAD] = (part * cosine[...] + turned * sine[...]).astype(bf16)
    kv_out[:, kvw:] = pre[:, kvw:].astype(bf16)

    def drain(k, carry):
        o_copy(k).wait()
        return carry

    lax.fori_loop(0, n, drain, 0)


def project_part(at, tokens_in, kv_grad, inv, cosine, sine, blocks, plan, carry, before, finish):
    rows, width = tokens_in.shape
    cols = kv_grad.shape[1]
    here = len(plan)
    n = sum(before) + here
    used = sorted({entry[1] for entries in plan for entry in entries})
    plan = tuple(
        tuple((flag, used.index(block), *rest) for flag, block, *rest in entries)
        for entries in plan
    )
    blocks = [blocks[i] for i in used]
    shard = plan[0][0][3] if len(plan[0]) == 1 else max(entry[3] for entry in plan[0])
    whole = pl.BlockSpec(memory_space=pltpu.VMEM)
    there = pl.BlockSpec(memory_space=pl.ANY)
    in_specs = [pl.BlockSpec(memory_space=pltpu.SMEM), there] + [whole] * 4
    in_specs += [whole, whole][: 2 if before else 0] + [there] * (len(before) + len(blocks))
    slots = n if finish else here
    scratch = [
        pltpu.VMEM((slots, rows, shard), bf16),
        pltpu.VMEM((here, shard, cols), bf16),
    ]
    if finish:
        scratch += [pltpu.VMEM((n, rows, shard), f32), pltpu.VMEM((rows, cols), f32)]
        out_specs = [whole, there]
        out_shape = [
            jax.ShapeDtypeStruct((rows, cols), bf16),
            jax.ShapeDtypeStruct((rows, width), bf16),
        ]
    else:
        out_specs = [whole] * 3
        out_shape = [
            jax.ShapeDtypeStruct((rows, cols), f32),
            jax.ShapeDtypeStruct((rows, HEAD), f32),
            jax.ShapeDtypeStruct((here, rows, shard), f32),
        ]
    scratch += [pltpu.SemaphoreType.DMA((slots,)), pltpu.SemaphoreType.DMA((here,))]
    scratch += [pltpu.SemaphoreType.DMA((max(len(before), 1),))]
    return pl.pallas_call(
        functools.partial(part_kernel, plan, tuple(before), finish),
        in_specs=in_specs,
        out_specs=out_specs,
        out_shape=out_shape,
        scratch_shapes=scratch,
        compiler_params=pltpu.CompilerParams(vmem_limit_bytes=48 * 2**20),
        cost_estimate=pl.CostEstimate(
            flops=4 * rows * shard * here * cols,
            bytes_accessed=4 * rows * width + 2 * shard * here * cols,
            transcendentals=0,
        ),
        name="project_last" if finish else "project_first",
    )(at, tokens_in, kv_grad, inv, cosine, sine, *carry, *blocks)


def replica_pairs(value, odd):
    swap = lambda v, step: lax.ppermute(v, "replica", [(r, r ^ step) for r in range(4)])
    half = value.shape[0] // 2
    mine = lax.dynamic_slice_in_dim(value, odd * half, half, 0)
    theirs = lax.dynamic_slice_in_dim(value, (1 - odd) * half, half, 0)
    mine = mine + swap(theirs, 1)
    return mine, swap(mine, 2)


def replica_halves(mine, odd):
    theirs = lax.ppermute(mine, "replica", [(r, r ^ 1) for r in range(4)])
    return jnp.where(odd, theirs, mine), jnp.where(odd, mine, theirs)


def exchange_ring(ring, own, far, near, pseudo, project):
    total = lax.psum(pseudo, "replica")
    shard, cut = own.shape[0], own.shape[0] // 2
    blocks = [own]
    from_left = from_right = own
    for d in range(1, ring.half):
        from_left, from_right = ring.to_right(from_left), ring.to_left(from_right)
        blocks += [from_left, from_right]
    from_left, from_right = after((from_left, from_right), total)
    blocks += [ring.to_right(from_left[:cut]), ring.to_left(from_right[cut:])]
    last = len(blocks) - 2
    plan = [((None, k, 0, shard),) for k in range(last)]
    plan.append(((None, last, 0, cut), (None, last + 1, cut, shard)))

    far = after(far, blocks[1], blocks[2])
    from_left, from_right = ring.to_right(far[:cut]), ring.to_left(far[cut:])
    for k in range(0, 2 * (ring.half - 1), 2):
        from_left, from_right = lax.optimization_barrier((from_left, from_right))
        if k == 0:
            from_left = jnp.pad(from_left, ((0, shard - cut), (0, 0)))
            from_right = jnp.pad(from_right, ((cut, 0), (0, 0)))
        from_left = ring.to_right((near[k] + from_left.astype(f32)).astype(bf16))
        from_right = ring.to_left((near[k + 1] + from_right.astype(f32)).astype(bf16))
    sums = [(from_left, from_right)]
    return project(blocks, tuple(plan), (), (), True), sums, total


ORDER = {"sum": (0, 1), "inner": (3, 8), "far": (0, 5), "partner0": (4, None), "partner1": (6, None), "first": (2, 4)}
CHAIN = True


def exchange_plane(plane, own, far, near, pseudo, project):
    shard = own.shape[0]
    at0, at1, at2, at3 = plane.at
    zero = jnp.zeros((), f32)
    pieces = [(0, shard // 2), (shard // 2, shard)]
    halves = range(2)
    wide = lambda v: v.astype(f32)
    pick = jnp.where
    sent, crossed, beside = [own], [own], {}

    def part(value, h):
        return value[pieces[h][0] : pieces[h][1]]

    def chord(value):
        crossed[0] = plane.over_chord(after(value, sent[0], crossed[0] if CHAIN else own))
        return crossed[0]

    def ring(step, to_right, to_left):
        sent[0] = to_right, to_left
        came = lax.optimization_barrier([plane.to_right(to_right), plane.to_left(to_left)])
        for name, (begin, _) in ORDER.items():
            if begin == step:
                beside[name] = tasks[name]()
        return came

    def later(step, *values):
        names = [name for name, (_, end) in ORDER.items() if end == step]
        awaited = [beside[name] for name in names]
        values, awaited = lax.optimization_barrier((after(values, sent[0]), awaited))
        beside.update(zip(names, awaited))
        return values

    def for_partner(h):
        return pick(at1, part(near[1], h), part(near[0], h)).astype(bf16)

    def first_blocks():
        gated = after(blocks[0], sent[0])
        return project([gated, *blocks[1:]], plan[:5], (), (), False)

    tasks = {
        "sum": lambda: replica_halves(after(mine, sent[0]) + came, odd),
        "far": lambda: chord(pick(at2, *first)),
        "inner": lambda: chord(far),
        "partner0": lambda: chord(for_partner(0)),
        "partner1": lambda: chord(for_partner(1)),
        "first": first_blocks,
    }

    first = ring(None, own, own)
    partner = chord(own)
    odd = lax.axis_index("replica") % 2 == 1
    if lax.axis_size("replica") == 4:
        mine, came = replica_pairs(after(pseudo, own), odd.astype(jnp.int32))
    else:
        came = lax.psum(pseudo, "replica")
        tasks["sum"] = lambda: came
    first, partner, far, came = lax.optimization_barrier((first, partner, far, came))
    two = [ring(0, *(part(side, 0) for side in first))]
    two.append(ring(1, *(part(side, 1) for side in later(1, *first))))
    blocks = [own, *first, *(two[h][way] for way in range(2) for h in halves)]
    plan = [((None, k, 0, shard),) for k in range(3)]
    plan += [tuple((None, 3 + 2 * way + h, *pieces[h]) for h in halves) for way in range(2)]
    three = []
    for h in halves:
        left, right = later(2 + h, *two[h])
        terms = part(far, h)
        three.append(ring(2 + h, pick(at0, terms, left), pick(at3, terms, right)))
    four = []
    for h in halves:
        left, right = later(4 + h, *three[h])
        to_right = wide(part(near[0], h)) + pick(at1, wide(left), zero)
        to_left = wide(part(near[1], h)) + pick(at2, wide(right), zero)
        to_right = pick(at2, left, to_right.astype(bf16))
        to_left = pick(at1, right, to_left.astype(bf16))
        four.append(ring(4 + h, to_right, to_left))
    five = []
    for h in halves:
        left, right = later(6 + h, *four[h])
        to_right = part(near[2], h) + pick(at3, zero, wide(left))
        to_left = part(near[3], h) + pick(at0, zero, wide(right))
        five.append(ring(6 + h, to_right.astype(bf16), to_left.astype(bf16)))
    six = []
    for h in halves:
        left, right = later(8 + h, *five[h])
        over = wide(part(beside["inner"], h))
        to_right = part(near[4], h) + wide(left) + pick(at1, over, zero)
        to_left = part(near[5], h) + wide(right) + pick(at2, over, zero)
        six.append(ring(8 + h, to_right.astype(bf16), to_left.astype(bf16)))
    sums = [(*six[h], beside["partner%d" % h]) for h in halves]

    blocks = [partner, beside["far"]] + [
        steps[h][way] for steps in (three, four) for way in range(2) for h in halves
    ]
    ways = lambda flag, at: tuple((flag, at + h, *pieces[h]) for h in halves)
    plan = (
        ((0, 0, 0, shard), *ways(2, 2)),
        ((1, 0, 0, shard), *ways(3, 4)),
        ((4, 1, 0, shard), *ways(5, 6), *ways(6, 8)),
    )
    outs = project(blocks, plan, beside["first"], (5,), True)
    return outs, sums, beside["sum"]


def local(
    layer_input,
    norm_gain,
    kv_weight,
    kv_cotangent,
    pseudo_grad,
    outer_momentum,
    global_params,
    local_params,
):
    small = lax.axis_size("fsdp") == 8
    ring = Plane() if small else Ring()
    tokens_in = layer_input[0]
    gain_shard = norm_gain[0].astype(f32)[:, None]
    weight_shard = kv_weight[0]
    cotangent = kv_cotangent[0]
    rows, width = tokens_in.shape
    shard, cols = weight_shard.shape

    own = (weight_shard.astype(f32) * gain_shard).astype(bf16)
    positions = (ring.me * rows + jnp.arange(rows, dtype=jnp.int32)) % SEQ_LEN
    cosine, sine = rope_tables(positions)
    scale = 1.0 / math.sqrt(rows * ring.count)
    kv_grad, inv, far, near, last = first_part(
        ring, tokens_in, cotangent, cosine, sine, shard, scale
    )
    order = [0]
    for d in range(1, ring.half):
        order += [-d, d]
    order.append(ring.half)
    at = [ring.devices_at(order).astype(jnp.int32)]
    if small:
        at0, at1, at2, at3 = ring.at
        flags = [at1, at2, ~at1, ~at2, at1 | at2, at3, at0]
        at.append(jnp.stack(flags).astype(jnp.int32))
    at = jnp.concatenate(at)

    def project(*args):
        return project_part(at, tokens_in, kv_grad, inv, cosine, sine, *args)

    exchange = exchange_plane if small else exchange_ring
    (kv_out, input_grad), sums, total = exchange(ring, own, far, near, pseudo_grad[0], project)
    weight_grad, gain_grad = last_part(last, weight_shard, norm_gain, sums)

    if isinstance(total, tuple):
        total = jnp.concatenate(total)
    average = total / lax.axis_size("replica")
    momentum_new = momentum_rate * outer_momentum + average
    global_new = global_params - outer_rate * (average + momentum_rate * momentum_new)
    local_new = (
        mixing_rate * local_params[0].astype(f32) + (1.0 - mixing_rate) * global_new
    ).astype(bf16)

    return (
        kv_out[None],
        input_grad[None],
        weight_grad,
        gain_grad,
        momentum_new,
        global_new,
        local_new[None],
    )


def solution(mesh):
    in_specs = (
        P("replica", "fsdp", None),
        P("replica", "fsdp"),
        P("replica", "fsdp", None),
        P("replica", "fsdp", None),
        P("replica", "fsdp", None),
        P("fsdp", None),
        P("fsdp", None),
        P("replica", "fsdp", None),
    )
    out_specs = (
        P("replica", "fsdp", None),
        P("replica", "fsdp", None),
        P("replica", "fsdp", None),
        P("replica", "fsdp"),
        P("fsdp", None),
        P("fsdp", None),
        P("replica", "fsdp", None),
    )
    return jax.shard_map(local, mesh=mesh, in_specs=in_specs, out_specs=out_specs, check_vma=False)
```

```python
import functools
import math

import jax
import jax.numpy as jnp
from jax import lax
from jax.experimental import pallas as pl
from jax.experimental.pallas import tpu as pltpu
from jax.sharding import PartitionSpec as P

HEAD = 128
SEQ_LEN = 4096


FLAGS = 7

epsilon = 1e-05
rope_base = 500000.0
momentum_rate = 0.9
outer_rate = 0.7
mixing_rate = 0.5

f32, bf16 = jnp.float32, jnp.bfloat16


class Ring:
    def __init__(self):
        self.count = lax.axis_size("fsdp")
        self.half = self.count // 2
        walk = list(range(0, self.count, 2)) + list(range(self.count - 1, 0, -2))
        after = walk[1:] + walk[:1]
        self.right = list(zip(walk, after))
        self.left = list(zip(after, walk))
        self.me = lax.axis_index("fsdp")
        self.spot = jnp.where(
            self.me % 2 == 0, self.me // 2, self.count - 1 - self.me // 2
        )

    def devices_at(self, distances):
        spot = (self.spot + self.count + jnp.array(distances, jnp.int32)) % self.count
        return jnp.where(spot < self.half, 2 * spot, 2 * (self.count - 1 - spot) + 1)

    def to_right(self, value):
        return lax.ppermute(value, "fsdp", self.right)

    def to_left(self, value):
        return lax.ppermute(value, "fsdp", self.left)


class Plane(Ring):
    def __init__(self):
        super().__init__()
        self.at = [self.spot % 4 == i for i in range(4)]

    def over_chord(self, value):
        return lax.ppermute(value, "fsdp", [(2, 3), (3, 2), (4, 5), (5, 4)])


def after(value, *others):
    return lax.optimization_barrier((value, others))[0]


def rope_tables(positions):
    half = HEAD // 2
    index_f = jnp.arange(half, dtype=f32)
    inverse = jnp.exp(index_f * (-2.0 * math.log(rope_base) / HEAD))
    angle = positions.astype(f32)[:, None] * inverse[None, :]
    cosine, sine = jnp.cos(angle), jnp.sin(angle)
    return jnp.concatenate([cosine, cosine], axis=1), jnp.concatenate([-sine, sine], axis=1)


def scale_kernel(weight, gain, out):
    gains = jnp.broadcast_to(gain[...].astype(f32), (8, weight.shape[0])).T
    out[...] = (weight[...].astype(f32) * gains[:, :1]).astype(bf16)


def scale_rows(weight, gain):
    shard, cols = weight.shape
    return pl.pallas_call(
        scale_kernel,
        grid=(shard // HEAD,),
        in_specs=[
            pl.BlockSpec((HEAD, cols), lambda i: (i, 0)),
            pl.BlockSpec((1, HEAD), lambda i: (0, i)),
        ],
        out_specs=pl.BlockSpec((HEAD, cols), lambda i: (i, 0)),
        out_shape=jax.ShapeDtypeStruct((shard, cols), bf16),
        compiler_params=pltpu.CompilerParams(vmem_limit_bytes=16 * 2**20),
        cost_estimate=pl.CostEstimate(
            flops=shard * cols, bytes_accessed=4 * shard * cols, transcendentals=0
        ),
        name="scale_rows",
    )(weight, gain)


def first_kernel(scale, at, x, cotangent, cosine, sine, kv_grad, inv, far, near, last):
    step = pl.program_id(0)
    width = x.shape[1]
    shard = far.shape[0]
    kvw = cotangent.shape[1] // 2

    @pl.when(step == 0)
    def _():
        total = jnp.zeros((x.shape[0], HEAD), f32)
        for c in range(0, width, HEAD):
            part = x[:, c : c + HEAD].astype(f32)
            total = total + part * part
        mean = jnp.sum(total, axis=1, keepdims=True) / width
        inv[...] = jnp.broadcast_to(lax.rsqrt(mean + epsilon), inv.shape)
        for c in range(0, kvw, HEAD):
            part = cotangent[:, c : c + HEAD].astype(f32)
            turned = pltpu.roll(part, HEAD // 2, 1)
            kv_grad[:, c : c + HEAD] = (part * cosine[...] - turned * sine[...]).astype(bf16)
        kv_grad[:, kvw:] = cotangent[:, kvw:]

    block = x[:, pl.ds(pl.multiple_of(at[step] * shard, shard), shard)]
    normed = (block.astype(f32) * inv[:, :1]).astype(bf16)
    term = (
        lax.dot_general(normed, kv_grad[...], (((0,), (0,)), ((), ())), preferred_element_type=f32)
        * scale
    )

    @pl.when(step == 0)
    def _():
        far[...] = term.astype(bf16)

    @pl.when((step > 0) & (step < pl.num_programs(0) - 1))
    def _():
        near[0] = term

    @pl.when(step == pl.num_programs(0) - 1)
    def _():
        last[...] = term


def first_part(ring, tokens_in, cotangent, cosine, sine, shard, scale):
    rows, width = tokens_in.shape
    cols = cotangent.shape[1]
    order = [ring.half]
    for d in range(ring.half - 1, 0, -1):
        order += [d, -d]
    order.append(0)
    n = ring.count
    fixed = lambda k, at: (0, 0)
    return pl.pallas_call(
        functools.partial(first_kernel, scale),
        grid_spec=pltpu.PrefetchScalarGridSpec(
            num_scalar_prefetch=1,
            grid=(n,),
            in_specs=[
                pl.BlockSpec((rows, width), fixed),
                pl.BlockSpec((rows, cols), fixed),
                pl.BlockSpec((rows, HEAD), fixed),
                pl.BlockSpec((rows, HEAD), fixed),
            ],
            out_specs=[
                pl.BlockSpec((rows, cols), fixed),
                pl.BlockSpec((rows, HEAD), fixed),
                pl.BlockSpec((shard, cols), fixed),
                pl.BlockSpec((1, shard, cols), lambda k, at: (jnp.clip(k - 1, 0, n - 3), 0, 0)),
                pl.BlockSpec((shard, cols), fixed),
            ],
        ),
        out_shape=[
            jax.ShapeDtypeStruct((rows, cols), bf16),
            jax.ShapeDtypeStruct((rows, HEAD), f32),
            jax.ShapeDtypeStruct((shard, cols), bf16),
            jax.ShapeDtypeStruct((n - 2, shard, cols), f32),
            jax.ShapeDtypeStruct((shard, cols), f32),
        ],
        compiler_params=pltpu.CompilerParams(vmem_limit_bytes=40 * 2**20),
        cost_estimate=pl.CostEstimate(
            flops=2 * rows * width * cols,
            bytes_accessed=2 * rows * width + 4 * width * cols,
            transcendentals=0,
        ),
        name="norm_and_weight_terms",
    )(ring.devices_at(order), tokens_in, cotangent, cosine, sine)


def last_kernel(count, own, weight, gain, *refs):
    came, (weight_grad, gain_grad) = refs[:count], refs[-2:]
    term = own[...]
    for ref in came:
        term = term + ref[...].astype(f32)
    product = term * weight[...].astype(f32)
    rows, cols = product.shape
    lanes = product[:, :HEAD]
    for c in range(HEAD, cols, HEAD):
        lanes = lanes + product[:, c : c + HEAD]
    gain_grad[...] = jnp.sum(lanes.T, axis=0, keepdims=True)
    gains = jnp.broadcast_to(gain[...].astype(f32), (8, rows)).T
    weight_grad[0] = term * gains[:, :1]


def last_part(own, weight, gain, sums):
    shard, cols = weight.shape
    many = len(sums)
    tile = HEAD
    tiles = shard // many // tile
    outs = None
    for h, came in enumerate(sums):
        row = lambda i, h=h: h * tiles + i
        specs = [
            pl.BlockSpec((tile, cols), lambda i, row=row: (row(i), 0)),
            pl.BlockSpec((tile, cols), lambda i, row=row: (row(i), 0)),
            pl.BlockSpec((1, tile), lambda i, row=row: (0, row(i))),
        ]
        specs += [pl.BlockSpec((tile, cols), lambda i: (i, 0))] * len(came)
        operands = [own, weight, gain, *came]
        if outs is not None:
            specs += [pl.BlockSpec(memory_space=pl.ANY)] * 2
        outs = pl.pallas_call(
            functools.partial(last_kernel, len(came)),
            grid=(tiles,),
            in_specs=specs,
            out_specs=[
                pl.BlockSpec((1, tile, cols), lambda i, row=row: (0, row(i), 0)),
                pl.BlockSpec((1, tile), lambda i, row=row: (0, row(i))),
            ],
            out_shape=[
                jax.ShapeDtypeStruct((1, shard, cols), f32),
                jax.ShapeDtypeStruct((1, shard), f32),
            ],
            input_output_aliases=(
                {} if outs is None else {len(operands): 0, len(operands) + 1: 1}
            ),
            compiler_params=pltpu.CompilerParams(vmem_limit_bytes=16 * 2**20),
            cost_estimate=pl.CostEstimate(
                flops=shard // many * cols * 8,
                bytes_accessed=shard // many * cols * 14,
                transcendentals=0,
            ),
            name="sum_of_terms",
        )(*operands, *(outs or ()))
    return outs


def part_kernel(plan, before, finish, at, x, kv_grad, inv, cosine, sine, *refs):
    here = len(plan)
    done = sum(before)
    n = done + here
    total_at = len(refs) - 9
    blocks, refs = refs[:total_at], refs[total_at:]
    if before:
        pre0, sums0, *grads0 = blocks[: 2 + len(before)]
        blocks = blocks[2 + len(before) :]
    if finish:
        kv_out, input_grad, xs, ws, ng, pre, x_sem, w_sem, g_sem = refs
    else:
        pre, sums, grads, xs, ws, ng, x_sem, w_sem, g_sem = refs
    rows, width = x.shape
    shard = xs.shape[2]
    kvw = pre.shape[1] // 2
    held = range(n) if finish else range(done, n)
    base = held[0]

    def columns(k):
        return pl.ds(pl.multiple_of(at[k] * shard, shard), shard)

    def x_copy(k):
        return pltpu.make_async_copy(x.at[:, columns(k)], xs.at[k - base], x_sem.at[k - base])

    def o_copy(k):
        return pltpu.make_async_copy(xs.at[k], input_grad.at[:, columns(k)], x_sem.at[k])

    for k in range(done, n):
        x_copy(k).start()
        for flag, block, start, stop in plan[k - done]:
            slot = k - done
            copy = pltpu.make_async_copy(blocks[block], ws.at[slot, start:stop], w_sem.at[slot])
            if flag is None:
                copy.start()
            else:

                @pl.when(at[at.shape[0] - FLAGS + flag] == 1)
                def _(copy=copy):
                    copy.start()

    if before:
        pre[...] = pre0[...]
        start = sums0[...]
    else:
        pre[...] = jnp.zeros_like(pre)
        start = jnp.zeros((rows, HEAD), f32)
    loads = []
    if finish:
        slot = 0
        for j, count in enumerate(before):
            loads.append(
                pltpu.make_async_copy(grads0[j], ng.at[slot : slot + count], g_sem.at[j])
            )
            slot += count
        for load in loads:
            load.start()
        for k in range(done):
            x_copy(k).start()

    def gather(i, total):
        k = done + i
        x_copy(k).wait()
        pltpu.make_async_copy(ws.at[i], ws.at[i], w_sem.at[i]).wait()
        weight = ws[i]
        normed = xs[k - base].astype(f32) * inv[:, :1]
        pre[...] += jnp.dot(normed.astype(bf16), weight, preferred_element_type=f32)
        grad = lax.dot_general(
            kv_grad[...], weight, (((1,), (1,)), ((), ())), preferred_element_type=f32
        )
        ng[k - base] = grad
        if not finish:
            pltpu.make_async_copy(ng.at[i], grads.at[i], g_sem.at[i]).start()
        product = grad * normed
        for c in range(0, shard, HEAD):
            total = total + product[:, c : c + HEAD]
        return total

    total = lax.fori_loop(0, here, gather, start)
    if not finish:
        sums[...] = total
        for i in range(here):
            pltpu.make_async_copy(ng.at[i], grads.at[i], g_sem.at[i]).wait()
        return
    mean = jnp.sum(total, axis=1, keepdims=True) / width
    for load in loads:
        load.wait()

    def write(k, carry):
        @pl.when(k < done)
        def _():
            x_copy(k).wait()

        scale = inv[:, :1]
        normed = xs[k].astype(f32) * scale
        xs[k] = (scale * (ng[k] - normed * mean)).astype(bf16)
        o_copy(k).start()
        return carry

    lax.fori_loop(0, n, write, 0)
    for c in range(0, kvw, HEAD):
        part = pre[:, c : c + HEAD]
        turned = pltpu.roll(part, HEAD // 2, 1)
        kv_out[:, c : c + HEAD] = (part * cosine[...] + turned * sine[...]).astype(bf16)
    kv_out[:, kvw:] = pre[:, kvw:].astype(bf16)

    def drain(k, carry):
        o_copy(k).wait()
        return carry

    lax.fori_loop(0, n, drain, 0)


def project_part(at, tokens_in, kv_grad, inv, cosine, sine, blocks, plan, carry, before, finish):
    rows, width = tokens_in.shape
    cols = kv_grad.shape[1]
    here = len(plan)
    n = sum(before) + here
    used = sorted({entry[1] for entries in plan for entry in entries})
    plan = tuple(
        tuple((flag, used.index(block), *rest) for flag, block, *rest in entries)
        for entries in plan
    )
    blocks = [blocks[i] for i in used]
    shard = plan[0][0][3] if len(plan[0]) == 1 else max(entry[3] for entry in plan[0])
    whole = pl.BlockSpec(memory_space=pltpu.VMEM)
    there = pl.BlockSpec(memory_space=pl.ANY)
    in_specs = [pl.BlockSpec(memory_space=pltpu.SMEM), there] + [whole] * 4
    in_specs += [whole, whole][: 2 if before else 0] + [there] * (len(before) + len(blocks))
    slots = n if finish else here
    scratch = [
        pltpu.VMEM((slots, rows, shard), bf16),
        pltpu.VMEM((here, shard, cols), bf16),
    ]
    if finish:
        scratch += [pltpu.VMEM((n, rows, shard), f32), pltpu.VMEM((rows, cols), f32)]
        out_specs = [whole, there]
        out_shape = [
            jax.ShapeDtypeStruct((rows, cols), bf16),
            jax.ShapeDtypeStruct((rows, width), bf16),
        ]
    else:
        scratch.append(pltpu.VMEM((here, rows, shard), f32))
        out_specs = [whole, whole, there]
        out_shape = [
            jax.ShapeDtypeStruct((rows, cols), f32),
            jax.ShapeDtypeStruct((rows, HEAD), f32),
            jax.ShapeDtypeStruct((here, rows, shard), f32),
        ]
    scratch += [pltpu.SemaphoreType.DMA((slots,)), pltpu.SemaphoreType.DMA((here,))]
    scratch += [pltpu.SemaphoreType.DMA((max(len(before), here),))]
    return pl.pallas_call(
        functools.partial(part_kernel, plan, tuple(before), finish),
        in_specs=in_specs,
        out_specs=out_specs,
        out_shape=out_shape,
        scratch_shapes=scratch,
        compiler_params=pltpu.CompilerParams(vmem_limit_bytes=48 * 2**20),
        cost_estimate=pl.CostEstimate(
            flops=4 * rows * shard * here * cols,
            bytes_accessed=4 * rows * width + 2 * shard * here * cols,
            transcendentals=0,
        ),
        name="project_last" if finish else "project_first",
    )(at, tokens_in, kv_grad, inv, cosine, sine, *carry, *blocks)


def replica_pairs(value, odd):
    swap = lambda v, step: lax.ppermute(v, "replica", [(r, r ^ step) for r in range(4)])
    half = value.shape[0] // 2
    mine = lax.dynamic_slice_in_dim(value, odd * half, half, 0)
    theirs = lax.dynamic_slice_in_dim(value, (1 - odd) * half, half, 0)
    mine = mine + swap(theirs, 1)
    return mine, swap(mine, 2)


def replica_halves(mine, odd):
    theirs = lax.ppermute(mine, "replica", [(r, r ^ 1) for r in range(4)])
    return jnp.where(odd, theirs, mine), jnp.where(odd, mine, theirs)


def exchange_ring(ring, own, far, near, pseudo, project, update):
    total = lax.psum(pseudo, "replica")
    shard, cut = own.shape[0], own.shape[0] // 2
    blocks = [own]
    from_left = from_right = own
    for d in range(1, ring.half):
        from_left, from_right = ring.to_right(from_left), ring.to_left(from_right)
        blocks += [from_left, from_right]
    from_left, from_right = after((from_left, from_right), total)
    blocks += [ring.to_right(from_left[:cut]), ring.to_left(from_right[cut:])]
    last = len(blocks) - 2
    plan = [((None, k, 0, shard),) for k in range(last)]
    plan.append(((None, last, 0, cut), (None, last + 1, cut, shard)))

    far = after(far, blocks[1], blocks[2])
    from_left, from_right = ring.to_right(far[:cut]), ring.to_left(far[cut:])
    for k in range(0, 2 * (ring.half - 1), 2):
        from_left, from_right = lax.optimization_barrier((from_left, from_right))
        if k == 0:
            from_left = jnp.pad(from_left, ((0, shard - cut), (0, 0)))
            from_right = jnp.pad(from_right, ((cut, 0), (0, 0)))
        from_left = ring.to_right((near[k] + from_left.astype(f32)).astype(bf16))
        from_right = ring.to_left((near[k + 1] + from_right.astype(f32)).astype(bf16))
    sums = [(from_left, from_right)]
    return project(blocks, tuple(plan), (), (), True), sums, update(total)


ORDER = {"sum": (0, 2), "inner": (3, 8), "far": (0, 3), "partner0": (4, None), "partner1": (6, None), "part0": (1, 3), "part1": (2, 5), "part2": (5, 9), "update": (3, 7)}
CHAIN = True
PAIR = 4


def exchange_plane(plane, own, far, near, pseudo, project, update):
    shard = own.shape[0]
    at0, at1, at2, at3 = plane.at
    zero = jnp.zeros((), f32)
    pieces = [(0, shard // 2), (shard // 2, shard)]
    halves = range(2)
    wide = lambda v: v.astype(f32)
    pick = jnp.where
    sent, crossed, beside = [own], [own], {}

    def part(value, h):
        return value[pieces[h][0] : pieces[h][1]]

    def chord(value):
        crossed[0] = plane.over_chord(after(value, sent[0], crossed[0] if CHAIN else own))
        return crossed[0]

    def ring(step, to_right, to_left):
        sent[0] = to_right, to_left
        came = lax.optimization_barrier([plane.to_right(to_right), plane.to_left(to_left)])
        for name, (begin, _) in ORDER.items():
            if begin == step:
                beside[name] = tasks[name]()
        return came

    def later(step, *values):
        names = [name for name, (_, end) in ORDER.items() if end == step]
        awaited = [beside[name] for name in names]
        if step == PAIR:
            awaited.append(partner[0])
        values, awaited = lax.optimization_barrier((after(values, sent[0]), awaited))
        beside.update(zip(names, awaited))
        if step == PAIR:
            partner[0] = awaited[-1]
        return values

    def for_partner(h):
        return pick(at1, part(near[1], h), part(near[0], h)).astype(bf16)

    ways = lambda flag, at: tuple((flag, at + h, *pieces[h]) for h in halves)
    carry, before = [()], []

    def part_of(plan, blocks, last=False):
        blocks = [after(blocks[0], sent[0]), *blocks[1:]]
        outs = project(blocks, plan, carry[0], tuple(before), last)
        if not last:
            carry[0] = (*outs[:2], *carry[0][2:], outs[2])
            before.append(len(plan))
        return outs

    tasks = {
        "sum": lambda: replica_halves(after(mine, sent[0]) + came, odd),
        "far": lambda: chord(pick(at2, *first)),
        "inner": lambda: chord(far),
        "partner0": lambda: chord(for_partner(0)),
        "partner1": lambda: chord(for_partner(1)),
        "part0": lambda: part_of(
            tuple(((None, k, 0, shard),) for k in range(3)), [own, *first]
        ),
        "part1": lambda: part_of((ways(None, 0), ways(None, 2)), by_way(two)),
        "part2": lambda: part_of(
            (((0, 0, 0, shard), *ways(2, 1)), ((1, 0, 0, shard), *ways(3, 3))),
            [partner[0], *by_way(three)],
        ),
        "update": lambda: update(after(beside["sum"], sent[0])),
    }
    by_way = lambda steps: [steps[h][way] for way in range(2) for h in halves]

    first = ring(None, own, own)
    partner = [chord(own)]
    odd = lax.axis_index("replica") % 2 == 1
    if lax.axis_size("replica") == 4:
        mine, came = replica_pairs(after(pseudo, own), odd.astype(jnp.int32))
    else:
        came = lax.psum(pseudo, "replica")
        tasks["sum"] = lambda: came
    first, far, came = lax.optimization_barrier((first, far, came))
    two = [ring(0, *(part(side, 0) for side in first))]
    two.append(ring(1, *(part(side, 1) for side in later(1, *first))))
    three = []
    for h in halves:
        left, right = later(2 + h, *two[h])
        terms = part(far, h)
        three.append(ring(2 + h, pick(at0, terms, left), pick(at3, terms, right)))
    four = []
    for h in halves:
        left, right = later(4 + h, *three[h])
        to_right = wide(part(near[0], h)) + pick(at1, wide(left), zero)
        to_left = wide(part(near[1], h)) + pick(at2, wide(right), zero)
        to_right = pick(at2, left, to_right.astype(bf16))
        to_left = pick(at1, right, to_left.astype(bf16))
        four.append(ring(4 + h, to_right, to_left))
    five = []
    for h in halves:
        left, right = later(6 + h, *four[h])
        to_right = part(near[2], h) + pick(at3, zero, wide(left))
        to_left = part(near[3], h) + pick(at0, zero, wide(right))
        five.append(ring(6 + h, to_right.astype(bf16), to_left.astype(bf16)))
    six = []
    for h in halves:
        left, right = later(8 + h, *five[h])
        over = wide(part(beside["inner"], h))
        to_right = part(near[4], h) + wide(left) + pick(at1, over, zero)
        to_left = part(near[5], h) + wide(right) + pick(at2, over, zero)
        six.append(ring(8 + h, to_right.astype(bf16), to_left.astype(bf16)))
    sums = [(*six[h], beside["partner%d" % h]) for h in halves]

    outs = part_of(
        (((4, 0, 0, shard), *ways(5, 1), *ways(6, 3)),), [beside["far"], *by_way(four)], True
    )
    return outs, sums, beside["update"]


def local(
    layer_input,
    norm_gain,
    kv_weight,
    kv_cotangent,
    pseudo_grad,
    outer_momentum,
    global_params,
    local_params,
):
    small = lax.axis_size("fsdp") == 8
    ring = Plane() if small else Ring()
    tokens_in = layer_input[0]
    weight_shard = kv_weight[0]
    cotangent = kv_cotangent[0]
    rows, width = tokens_in.shape
    shard, cols = weight_shard.shape

    own = scale_rows(weight_shard, norm_gain)
    positions = (ring.me * rows + jnp.arange(rows, dtype=jnp.int32)) % SEQ_LEN
    cosine, sine = rope_tables(positions)
    scale = 1.0 / math.sqrt(rows * ring.count)
    kv_grad, inv, far, near, last = first_part(
        ring, tokens_in, cotangent, cosine, sine, shard, scale
    )
    order = [0]
    for d in range(1, ring.half):
        order += [-d, d]
    order.append(ring.half)
    at = [ring.devices_at(order).astype(jnp.int32)]
    if small:
        at0, at1, at2, at3 = ring.at
        flags = [at1, at2, ~at1, ~at2, at1 | at2, at3, at0]
        at.append(jnp.stack(flags).astype(jnp.int32))
    at = jnp.concatenate(at)

    def project(*args):
        return project_part(at, tokens_in, kv_grad, inv, cosine, sine, *args)

    def update(total):
        if isinstance(total, tuple):
            total = jnp.concatenate(total)
        average = total / lax.axis_size("replica")
        momentum_new = momentum_rate * outer_momentum + average
        global_new = global_params - outer_rate * (average + momentum_rate * momentum_new)
        local_new = (
            mixing_rate * local_params[0].astype(f32) + (1.0 - mixing_rate) * global_new
        ).astype(bf16)
        return momentum_new, global_new, local_new

    exchange = exchange_plane if small else exchange_ring
    (kv_out, input_grad), sums, updated = exchange(
        ring, own, far, near, pseudo_grad[0], project, update
    )
    momentum_new, global_new, local_new = updated
    weight_grad, gain_grad = last_part(last, weight_shard, norm_gain, sums)

    return (
        kv_out[None],
        input_grad[None],
        weight_grad,
        gain_grad,
        momentum_new,
        global_new,
        local_new[None],
    )


def solution(mesh):
    in_specs = (
        P("replica", "fsdp", None),
        P("replica", "fsdp"),
        P("replica", "fsdp", None),
        P("replica", "fsdp", None),
        P("replica", "fsdp", None),
        P("fsdp", None),
        P("fsdp", None),
        P("replica", "fsdp", None),
    )
    out_specs = (
        P("replica", "fsdp", None),
        P("replica", "fsdp", None),
        P("replica", "fsdp", None),
        P("replica", "fsdp"),
        P("fsdp", None),
        P("fsdp", None),
        P("replica", "fsdp", None),
    )
    return jax.shard_map(local, mesh=mesh, in_specs=in_specs, out_specs=out_specs, check_vma=False)
```

```python
import functools
import math

import jax
import jax.numpy as jnp
from jax import lax
from jax.experimental import pallas as pl
from jax.experimental.pallas import tpu as pltpu
from jax.sharding import PartitionSpec as P

HEAD = 128
SEQ_LEN = 4096


FLAGS = 7

epsilon = 1e-05
rope_base = 500000.0
momentum_rate = 0.9
outer_rate = 0.7
mixing_rate = 0.5

f32, bf16 = jnp.float32, jnp.bfloat16


class Ring:
    def __init__(self):
        self.count = lax.axis_size("fsdp")
        self.half = self.count // 2
        walk = list(range(0, self.count, 2)) + list(range(self.count - 1, 0, -2))
        after = walk[1:] + walk[:1]
        self.right = list(zip(walk, after))
        self.left = list(zip(after, walk))
        self.me = lax.axis_index("fsdp")
        self.spot = jnp.where(
            self.me % 2 == 0, self.me // 2, self.count - 1 - self.me // 2
        )

    def devices_at(self, distances):
        spot = (self.spot + self.count + jnp.array(distances, jnp.int32)) % self.count
        return jnp.where(spot < self.half, 2 * spot, 2 * (self.count - 1 - spot) + 1)

    def to_right(self, value):
        return lax.ppermute(value, "fsdp", self.right)

    def to_left(self, value):
        return lax.ppermute(value, "fsdp", self.left)


class Plane(Ring):
    def __init__(self):
        super().__init__()
        self.at = [self.spot % 4 == i for i in range(4)]

    def over_chord(self, value):
        return lax.ppermute(value, "fsdp", [(2, 3), (3, 2), (4, 5), (5, 4)])


def after(value, *others):
    return lax.optimization_barrier((value, others))[0]


def rope_tables(positions):
    half = HEAD // 2
    index_f = jnp.arange(half, dtype=f32)
    inverse = jnp.exp(index_f * (-2.0 * math.log(rope_base) / HEAD))
    angle = positions.astype(f32)[:, None] * inverse[None, :]
    cosine, sine = jnp.cos(angle), jnp.sin(angle)
    return jnp.concatenate([cosine, cosine], axis=1), jnp.concatenate([-sine, sine], axis=1)


def scale_kernel(weight, gain, out):
    gains = jnp.broadcast_to(gain[...].astype(f32), (8, weight.shape[0])).T
    out[...] = (weight[...].astype(f32) * gains[:, :1]).astype(bf16)


def scale_rows(weight, gain):
    shard, cols = weight.shape
    return pl.pallas_call(
        scale_kernel,
        grid=(shard // HEAD,),
        in_specs=[
            pl.BlockSpec((HEAD, cols), lambda i: (i, 0)),
            pl.BlockSpec((1, HEAD), lambda i: (0, i)),
        ],
        out_specs=pl.BlockSpec((HEAD, cols), lambda i: (i, 0)),
        out_shape=jax.ShapeDtypeStruct((shard, cols), bf16),
        compiler_params=pltpu.CompilerParams(vmem_limit_bytes=16 * 2**20),
        cost_estimate=pl.CostEstimate(
            flops=shard * cols, bytes_accessed=4 * shard * cols, transcendentals=0
        ),
        name="scale_rows",
    )(weight, gain)


def first_kernel(scale, at, x, cotangent, cosine, sine, kv_grad, inv, far, near, last):
    step = pl.program_id(0)
    width = x.shape[1]
    shard = far.shape[0]
    kvw = cotangent.shape[1] // 2

    @pl.when(step == 0)
    def _():
        total = jnp.zeros((x.shape[0], HEAD), f32)
        for c in range(0, width, HEAD):
            part = x[:, c : c + HEAD].astype(f32)
            total = total + part * part
        mean = jnp.sum(total, axis=1, keepdims=True) / width
        inv[...] = jnp.broadcast_to(lax.rsqrt(mean + epsilon), inv.shape)
        for c in range(0, kvw, HEAD):
            part = cotangent[:, c : c + HEAD].astype(f32)
            turned = pltpu.roll(part, HEAD // 2, 1)
            kv_grad[:, c : c + HEAD] = (part * cosine[...] - turned * sine[...]).astype(bf16)
        kv_grad[:, kvw:] = cotangent[:, kvw:]

    block = x[:, pl.ds(pl.multiple_of(at[step] * shard, shard), shard)]
    normed = (block.astype(f32) * inv[:, :1]).astype(bf16)
    term = (
        lax.dot_general(normed, kv_grad[...], (((0,), (0,)), ((), ())), preferred_element_type=f32)
        * scale
    )

    @pl.when(step == 0)
    def _():
        far[...] = term.astype(bf16)

    @pl.when((step > 0) & (step < pl.num_programs(0) - 1))
    def _():
        near[0] = term

    @pl.when(step == pl.num_programs(0) - 1)
    def _():
        last[...] = term


def first_part(ring, tokens_in, cotangent, cosine, sine, shard, scale):
    rows, width = tokens_in.shape
    cols = cotangent.shape[1]
    order = [ring.half]
    for d in range(ring.half - 1, 0, -1):
        order += [d, -d]
    order.append(0)
    n = ring.count
    fixed = lambda k, at: (0, 0)
    return pl.pallas_call(
        functools.partial(first_kernel, scale),
        grid_spec=pltpu.PrefetchScalarGridSpec(
            num_scalar_prefetch=1,
            grid=(n,),
            in_specs=[
                pl.BlockSpec((rows, width), fixed),
                pl.BlockSpec((rows, cols), fixed),
                pl.BlockSpec((rows, HEAD), fixed),
                pl.BlockSpec((rows, HEAD), fixed),
            ],
            out_specs=[
                pl.BlockSpec((rows, cols), fixed),
                pl.BlockSpec((rows, HEAD), fixed),
                pl.BlockSpec((shard, cols), fixed),
                pl.BlockSpec((1, shard, cols), lambda k, at: (jnp.clip(k - 1, 0, n - 3), 0, 0)),
                pl.BlockSpec((shard, cols), fixed),
            ],
        ),
        out_shape=[
            jax.ShapeDtypeStruct((rows, cols), bf16),
            jax.ShapeDtypeStruct((rows, HEAD), f32),
            jax.ShapeDtypeStruct((shard, cols), bf16),
            jax.ShapeDtypeStruct((n - 2, shard, cols), f32),
            jax.ShapeDtypeStruct((shard, cols), f32),
        ],
        compiler_params=pltpu.CompilerParams(vmem_limit_bytes=40 * 2**20),
        cost_estimate=pl.CostEstimate(
            flops=2 * rows * width * cols,
            bytes_accessed=2 * rows * width + 4 * width * cols,
            transcendentals=0,
        ),
        name="norm_and_weight_terms",
    )(ring.devices_at(order), tokens_in, cotangent, cosine, sine)


def last_kernel(count, own, weight, gain, *refs):
    came, (weight_grad, gain_grad) = refs[:count], refs[-2:]
    term = own[...]
    for ref in came:
        term = term + ref[...].astype(f32)
    product = term * weight[...].astype(f32)
    rows, cols = product.shape
    lanes = product[:, :HEAD]
    for c in range(HEAD, cols, HEAD):
        lanes = lanes + product[:, c : c + HEAD]
    gain_grad[...] = jnp.sum(lanes.T, axis=0, keepdims=True)
    gains = jnp.broadcast_to(gain[...].astype(f32), (8, rows)).T
    weight_grad[0] = term * gains[:, :1]


def last_part(own, weight, gain, sums):
    shard, cols = weight.shape
    many = len(sums)
    tile = HEAD
    tiles = shard // many // tile
    outs = None
    for h, came in enumerate(sums):
        row = lambda i, h=h: h * tiles + i
        specs = [
            pl.BlockSpec((tile, cols), lambda i, row=row: (row(i), 0)),
            pl.BlockSpec((tile, cols), lambda i, row=row: (row(i), 0)),
            pl.BlockSpec((1, tile), lambda i, row=row: (0, row(i))),
        ]
        for ref in came:
            whole = ref.shape[0] == shard
            at = row if whole else lambda i: i
            specs.append(pl.BlockSpec((tile, cols), lambda i, at=at: (at(i), 0)))
        operands = [own, weight, gain, *came]
        if outs is not None:
            specs += [pl.BlockSpec(memory_space=pl.ANY)] * 2
        outs = pl.pallas_call(
            functools.partial(last_kernel, len(came)),
            grid=(tiles,),
            in_specs=specs,
            out_specs=[
                pl.BlockSpec((1, tile, cols), lambda i, row=row: (0, row(i), 0)),
                pl.BlockSpec((1, tile), lambda i, row=row: (0, row(i))),
            ],
            out_shape=[
                jax.ShapeDtypeStruct((1, shard, cols), f32),
                jax.ShapeDtypeStruct((1, shard), f32),
            ],
            input_output_aliases=(
                {} if outs is None else {len(operands): 0, len(operands) + 1: 1}
            ),
            compiler_params=pltpu.CompilerParams(vmem_limit_bytes=16 * 2**20),
            cost_estimate=pl.CostEstimate(
                flops=shard // many * cols * 8,
                bytes_accessed=shard // many * cols * 14,
                transcendentals=0,
            ),
            name="sum_of_terms",
        )(*operands, *(outs or ()))
    return outs


def start_blocks(plan, at, blocks, ws, w_sem, ks):
    shard = ws.shape[0] // len(plan)
    for k in ks:
        for flag, block, start, stop in plan[k]:
            there = ws.at[k * shard + start : k * shard + stop]
            copy = pltpu.make_async_copy(blocks[block], there, w_sem.at[k])
            if flag is None:
                copy.start()
            else:

                @pl.when(at[at.shape[0] - FLAGS + flag] == 1)
                def _(copy=copy):
                    copy.start()


def wait_block(ws, w_sem, k, shard):
    there = ws.at[k * shard : (k + 1) * shard]
    pltpu.make_async_copy(there, there, w_sem.at[k]).wait()


def columns(at, k, shard):
    return pl.ds(pl.multiple_of(at[k] * shard, shard), shard)


def lane_sums(product):
    total = product[:, :HEAD]
    for c in range(HEAD, product.shape[1], HEAD):
        total = total + product[:, c : c + HEAD]
    return total


def grad_of(kv_grad, weight):
    return lax.dot_general(
        kv_grad[...], weight, (((1,), (1,)), ((), ())), preferred_element_type=f32
    )


def early_kernel(plan, at, x, kv_grad, inv, *refs):
    blocks, (sums, grads, xs, ws, ng, x_sem, w_sem, g_sem) = refs[:-8], refs[-8:]
    n = len(plan)
    shard = xs.shape[2]

    def x_copy(k):
        return pltpu.make_async_copy(x.at[:, columns(at, k, shard)], xs.at[k], x_sem.at[k])

    def g_copy(k):
        return pltpu.make_async_copy(ng.at[k], grads.at[k], g_sem.at[k])

    for k in range(n):
        x_copy(k).start()
        start_blocks(plan, at, blocks, ws, w_sem, [k])
    total = None
    for k in range(n):
        x_copy(k).wait()
        wait_block(ws, w_sem, k, shard)
        grad = grad_of(kv_grad, ws[k * shard : (k + 1) * shard, :])
        ng[k] = grad
        g_copy(k).start()
        product = lane_sums(grad * (xs[k].astype(f32) * inv[:, :1]))
        total = product if total is None else total + product
    sums[...] = total
    for k in range(n):
        g_copy(k).wait()


def late_kernel(plan, done, at, x, kv_grad, inv, cosine, sine, *refs):
    own = 9
    blocks, refs = refs[:-own], refs[-own:]
    if done:
        sums0, grads0, *blocks = blocks
    kv_out, input_grad, xs, hs, ws, ng, x_sem, w_sem, g_sem = refs
    n = len(plan)
    rows, width = x.shape
    shard = xs.shape[2]
    cols = ws.shape[1]
    kvw = cols // 2

    def x_copy(k):
        return pltpu.make_async_copy(x.at[:, columns(at, k, shard)], xs.at[k], x_sem.at[k])

    def o_copy(k):
        return pltpu.make_async_copy(xs.at[k], input_grad.at[:, columns(at, k, shard)], x_sem.at[k])

    order = [*range(done, n), *range(done)]
    for k in order:
        x_copy(k).start()
        start_blocks(plan, at, blocks, ws, w_sem, [k])
    if done:
        load = pltpu.make_async_copy(grads0, ng.at[:done], g_sem.at[0])
        load.start()
        total = sums0[...]
    else:
        total = jnp.zeros((rows, HEAD), f32)
    for k in order:
        x_copy(k).wait()
        normed = xs[k].astype(f32) * inv[:, :1]
        hs[:, k * shard : (k + 1) * shard] = normed.astype(bf16)
        if k >= done:
            wait_block(ws, w_sem, k, shard)
            grad = grad_of(kv_grad, ws[k * shard : (k + 1) * shard, :])
            ng[k] = grad
            total = total + lane_sums(grad * normed)
    mean = jnp.sum(total, axis=1, keepdims=True) / width
    if done:
        load.wait()
    for k in range(done):
        wait_block(ws, w_sem, k, shard)

    def project(i, keys):
        tile = 2 * HEAD
        at_column = pl.ds(pl.multiple_of(i * tile, tile), tile)
        pre = jnp.dot(hs[...], ws[:, at_column], preferred_element_type=f32)
        if keys:
            turned = [pltpu.roll(pre[:, c : c + HEAD], HEAD // 2, 1) for c in (0, HEAD)]
            pre = jnp.concatenate(
                [
                    pre[:, c : c + HEAD] * cosine[...] + part * sine[...]
                    for c, part in zip((0, HEAD), turned)
                ],
                axis=1,
            )
        kv_out[:, at_column] = pre.astype(bf16)

    def finish(k):
        scale = inv[:, :1]
        normed = xs[k].astype(f32) * scale
        xs[k] = (scale * (ng[k] - normed * mean)).astype(bf16)
        o_copy(k).start()

    lax.fori_loop(0, n, lambda k, c: (finish(k), c)[1], 0)
    tiles = kvw // (2 * HEAD)
    lax.fori_loop(0, tiles, lambda i, c: (project(i, True), c)[1], 0)
    lax.fori_loop(tiles, 2 * tiles, lambda i, c: (project(i, False), c)[1], 0)
    lax.fori_loop(0, n, lambda k, c: (o_copy(k).wait(), c)[1], 0)


def pick_blocks(blocks, plan):
    used = sorted({entry[1] for entries in plan for entry in entries})
    plan = tuple(
        tuple((flag, used.index(block), *rest) for flag, block, *rest in entries)
        for entries in plan
    )
    return [blocks[i] for i in used], plan


def early_part(at, tokens_in, kv_grad, inv, blocks, plan, shard):
    rows, width = tokens_in.shape
    cols = kv_grad.shape[1]
    n = len(plan)
    blocks, plan = pick_blocks(blocks, plan)
    whole = pl.BlockSpec(memory_space=pltpu.VMEM)
    there = pl.BlockSpec(memory_space=pl.ANY)
    return pl.pallas_call(
        functools.partial(early_kernel, plan),
        in_specs=[pl.BlockSpec(memory_space=pltpu.SMEM), there, whole, whole]
        + [there] * len(blocks),
        out_specs=[whole, there],
        out_shape=[
            jax.ShapeDtypeStruct((rows, HEAD), f32),
            jax.ShapeDtypeStruct((n, rows, shard), f32),
        ],
        scratch_shapes=[
            pltpu.VMEM((n, rows, shard), bf16),
            pltpu.VMEM((n * shard, cols), bf16),
            pltpu.VMEM((n, rows, shard), f32),
        ]
        + [pltpu.SemaphoreType.DMA((n,))] * 3,
        compiler_params=pltpu.CompilerParams(vmem_limit_bytes=40 * 2**20),
        cost_estimate=pl.CostEstimate(
            flops=2 * rows * shard * n * cols,
            bytes_accessed=shard * n * (6 * rows + 2 * cols),
            transcendentals=0,
        ),
        name="project_first",
    )(at, tokens_in, kv_grad, inv, *blocks)


def late_part(at, tokens_in, kv_grad, inv, cosine, sine, blocks, plan, shard, carry=()):
    rows, width = tokens_in.shape
    cols = kv_grad.shape[1]
    n = len(plan)
    done = carry[1].shape[0] if carry else 0
    blocks, plan = pick_blocks(blocks, plan)
    whole = pl.BlockSpec(memory_space=pltpu.VMEM)
    there = pl.BlockSpec(memory_space=pl.ANY)
    return pl.pallas_call(
        functools.partial(late_kernel, plan, done),
        in_specs=[pl.BlockSpec(memory_space=pltpu.SMEM), there]
        + [whole] * 4
        + [whole, there][: len(carry)]
        + [there] * len(blocks),
        out_specs=[whole, there],
        out_shape=[
            jax.ShapeDtypeStruct((rows, cols), bf16),
            jax.ShapeDtypeStruct((rows, width), bf16),
        ],
        scratch_shapes=[
            pltpu.VMEM((n, rows, shard), bf16),
            pltpu.VMEM((rows, n * shard), bf16),
            pltpu.VMEM((n * shard, cols), bf16),
            pltpu.VMEM((n, rows, shard), f32),
        ]
        + [pltpu.SemaphoreType.DMA((n,))] * 3,
        compiler_params=pltpu.CompilerParams(vmem_limit_bytes=48 * 2**20),
        cost_estimate=pl.CostEstimate(
            flops=4 * rows * width * cols,
            bytes_accessed=4 * rows * width + 2 * width * cols,
            transcendentals=0,
        ),
        name="project_last",
    )(at, tokens_in, kv_grad, inv, cosine, sine, *carry, *blocks)


def replica_swap(value, step):
    return lax.ppermute(value, "replica", [(r, r ^ step) for r in range(4)])


def exchange_ring(ring, own, far, near, pseudo, early, late, update):
    total = lax.psum(pseudo, "replica")
    shard, cut = own.shape[0], own.shape[0] // 2
    blocks = [own]
    from_left = from_right = own
    for d in range(1, ring.half):
        from_left, from_right = ring.to_right(from_left), ring.to_left(from_right)
        blocks += [from_left, from_right]
    from_left, from_right = after((from_left, from_right), total)
    blocks += [ring.to_right(from_left[:cut]), ring.to_left(from_right[cut:])]
    last = len(blocks) - 2
    plan = [((None, k, 0, shard),) for k in range(last)]
    plan.append(((None, last, 0, cut), (None, last + 1, cut, shard)))

    far = after(far, blocks[1], blocks[2])
    from_left, from_right = ring.to_right(far[:cut]), ring.to_left(far[cut:])
    for k in range(0, 2 * (ring.half - 1), 2):
        from_left, from_right = lax.optimization_barrier((from_left, from_right))
        if k == 0:
            from_left = jnp.pad(from_left, ((0, shard - cut), (0, 0)))
            from_right = jnp.pad(from_right, ((cut, 0), (0, 0)))
        from_left = ring.to_right((near[k] + from_left.astype(f32)).astype(bf16))
        from_right = ring.to_left((near[k + 1] + from_right.astype(f32)).astype(bf16))
    sums = [(from_left, from_right)]
    return late(blocks, plan), sums, update(total)


ORDER = {"sum": (-1, 3), "pair": (-1, 3), "inner": (2, 7), "far": (1, 5), "partner": (7, None), "first": (2, 4), "update": (4, 7)}
CHAIN = True


def exchange_plane(plane, own, far, near, pseudo, early, late, update):
    shard = own.shape[0]
    at0, at1, at2, at3 = plane.at
    zero = jnp.zeros((), f32)
    pieces = [(0, shard // 2), (shard // 2, shard)]
    halves = range(2)
    wide = lambda v: v.astype(f32)
    pick = jnp.where
    sent, crossed, beside = [own], [own], {}

    def part(value, h):
        return value[pieces[h][0] : pieces[h][1]]

    def chord(value):
        crossed[0] = plane.over_chord(after(value, sent[0], crossed[0] if CHAIN else own))
        return crossed[0]

    def ring(step, to_right, to_left):
        sent[0] = to_right, to_left
        came = lax.optimization_barrier([plane.to_right(to_right), plane.to_left(to_left)])
        for name, (begin, _) in ORDER.items():
            if begin == step:
                beside[name] = tasks[name]()
        return came

    def later(step, *values):
        names = [name for name, (_, end) in ORDER.items() if end == step]
        awaited = [beside[name] for name in names]
        values, awaited = lax.optimization_barrier((after(values, sent[0]), awaited))
        beside.update(zip(names, awaited))
        return values

    ways = lambda flag, at: tuple((flag, at + h, *pieces[h]) for h in halves)
    by_way = lambda steps: [steps[h][way] for way in range(2) for h in halves]
    near_plan = [((None, k, 0, shard),) for k in range(3)] + [ways(None, 3), ways(None, 5)]
    tasks = {
        "far": lambda: chord(pick(at2, *first)),
        "inner": lambda: chord(far),
        "partner": lambda: chord(pick(at1, near[1], near[0]).astype(bf16)),
        "first": lambda: early([after(own, sent[0]), *first, *by_way(two)], near_plan),
        "update": lambda: update(after((pairs, beside["sum"]), sent[0])),
    }

    first = ring(None, own, own)
    beside["pair"] = chord(own)
    if lax.axis_size("replica") == 4:
        pairs = after(pseudo, own)
        pairs = (pairs + replica_swap(pairs, 1)).astype(bf16)
        came = replica_swap(pairs, 2)
    else:
        pairs, came = lax.psum(pseudo, "replica"), jnp.zeros((), f32)
    first, far, pairs = lax.optimization_barrier((first, far, pairs))
    beside["sum"] = came
    two = [ring(0, *(part(side, 0) for side in first))]
    two.append(ring(1, *(part(side, 1) for side in later(1, *first))))
    three = []
    for h in halves:
        left, right = later(2 + h, *two[h])
        terms = part(far, h)
        three.append(ring(2 + h, pick(at0, terms, left), pick(at3, terms, right)))
    four = []
    for h in halves:
        left, right = later(4 + h, *three[h])
        to_right = wide(part(near[0], h)) + pick(at1, wide(left), zero)
        to_left = wide(part(near[1], h)) + pick(at2, wide(right), zero)
        to_right = pick(at2, left, to_right.astype(bf16))
        to_left = pick(at1, right, to_left.astype(bf16))
        four.append(ring(4 + h, to_right, to_left))
    five = []
    for h in halves:
        left, right = later(6 + h, *four[h])
        to_right = part(near[2], h) + pick(at3, zero, wide(left))
        to_left = part(near[3], h) + pick(at0, zero, wide(right))
        five.append(ring(6 + h, to_right.astype(bf16), to_left.astype(bf16)))
    six = []
    for h in halves:
        left, right = later(8 + h, *five[h])
        over = wide(part(beside["inner"], h))
        to_right = part(near[4], h) + wide(left) + pick(at1, over, zero)
        to_left = part(near[5], h) + wide(right) + pick(at2, over, zero)
        six.append(ring(8 + h, to_right.astype(bf16), to_left.astype(bf16)))
    sums = [(*six[h], beside["partner"]) for h in halves]

    blocks = [own, *first, *by_way(two), beside["pair"], *by_way(three), beside["far"], *by_way(four)]
    plan = near_plan + [
        ((0, 7, 0, shard), *ways(2, 8)),
        ((1, 7, 0, shard), *ways(3, 10)),
        ((4, 12, 0, shard), *ways(5, 13), *ways(6, 15)),
    ]
    return late(blocks, plan, beside["first"]), sums, beside["update"]


def local(
    layer_input,
    norm_gain,
    kv_weight,
    kv_cotangent,
    pseudo_grad,
    outer_momentum,
    global_params,
    local_params,
):
    small = lax.axis_size("fsdp") == 8
    ring = Plane() if small else Ring()
    tokens_in = layer_input[0]
    weight_shard = kv_weight[0]
    cotangent = kv_cotangent[0]
    rows, width = tokens_in.shape
    shard, cols = weight_shard.shape

    own = scale_rows(weight_shard, norm_gain)
    positions = (ring.me * rows + jnp.arange(rows, dtype=jnp.int32)) % SEQ_LEN
    cosine, sine = rope_tables(positions)
    scale = 1.0 / math.sqrt(rows * ring.count)
    kv_grad, inv, far, near, last = first_part(
        ring, tokens_in, cotangent, cosine, sine, shard, scale
    )
    order = [0]
    for d in range(1, ring.half):
        order += [-d, d]
    order.append(ring.half)
    at = [ring.devices_at(order).astype(jnp.int32)]
    if small:
        at0, at1, at2, at3 = ring.at
        flags = [at1, at2, ~at1, ~at2, at1 | at2, at3, at0]
        at.append(jnp.stack(flags).astype(jnp.int32))
    at = jnp.concatenate(at)

    def early(blocks, plan):
        return early_part(at, tokens_in, kv_grad, inv, blocks, plan, shard)

    def late(blocks, plan, carry=()):
        return late_part(at, tokens_in, kv_grad, inv, cosine, sine, blocks, plan, shard, carry)

    def update(total):
        if isinstance(total, tuple):
            total = total[0].astype(f32) + total[1].astype(f32)
        average = total / lax.axis_size("replica")
        momentum_new = momentum_rate * outer_momentum + average
        global_new = global_params - outer_rate * (average + momentum_rate * momentum_new)
        local_new = (
            mixing_rate * local_params[0].astype(f32) + (1.0 - mixing_rate) * global_new
        ).astype(bf16)
        return momentum_new, global_new, local_new

    exchange = exchange_plane if small else exchange_ring
    (kv_out, input_grad), sums, updated = exchange(
        ring, own, far, near, pseudo_grad[0], early, late, update
    )
    momentum_new, global_new, local_new = updated
    weight_grad, gain_grad = last_part(last, weight_shard, norm_gain, sums)

    return (
        kv_out[None],
        input_grad[None],
        weight_grad,
        gain_grad,
        momentum_new,
        global_new,
        local_new[None],
    )


def solution(mesh):
    in_specs = (
        P("replica", "fsdp", None),
        P("replica", "fsdp"),
        P("replica", "fsdp", None),
        P("replica", "fsdp", None),
        P("replica", "fsdp", None),
        P("fsdp", None),
        P("fsdp", None),
        P("replica", "fsdp", None),
    )
    out_specs = (
        P("replica", "fsdp", None),
        P("replica", "fsdp", None),
        P("replica", "fsdp", None),
        P("replica", "fsdp"),
        P("fsdp", None),
        P("fsdp", None),
        P("replica", "fsdp", None),
    )
    return jax.shard_map(local, mesh=mesh, in_specs=in_specs, out_specs=out_specs, check_vma=False)
```

```python
import functools
import math

import jax
import jax.numpy as jnp
from jax import lax
from jax.experimental import pallas as pl
from jax.experimental.pallas import tpu as pltpu
from jax.sharding import PartitionSpec as P

HEAD = 128
SEQ_LEN = 4096


FLAGS = 7

epsilon = 1e-05
rope_base = 500000.0
momentum_rate = 0.9
outer_rate = 0.7
mixing_rate = 0.5

f32, bf16 = jnp.float32, jnp.bfloat16


class Ring:
    def __init__(self):
        self.count = lax.axis_size("fsdp")
        self.half = self.count // 2
        walk = list(range(0, self.count, 2)) + list(range(self.count - 1, 0, -2))
        after = walk[1:] + walk[:1]
        self.right = list(zip(walk, after))
        self.left = list(zip(after, walk))
        self.me = lax.axis_index("fsdp")
        self.spot = jnp.where(
            self.me % 2 == 0, self.me // 2, self.count - 1 - self.me // 2
        )

    def devices_at(self, distances):
        spot = (self.spot + self.count + jnp.array(distances, jnp.int32)) % self.count
        return jnp.where(spot < self.half, 2 * spot, 2 * (self.count - 1 - spot) + 1)

    def to_right(self, value):
        return lax.ppermute(value, "fsdp", self.right)

    def to_left(self, value):
        return lax.ppermute(value, "fsdp", self.left)


class Plane(Ring):
    def __init__(self):
        super().__init__()
        self.at = [self.spot % 4 == i for i in range(4)]

    def over_chord(self, value):
        return lax.ppermute(value, "fsdp", [(2, 3), (3, 2), (4, 5), (5, 4)])


def after(value, *others):
    return lax.optimization_barrier((value, others))[0]


def rope_tables(positions):
    half = HEAD // 2
    index_f = jnp.arange(half, dtype=f32)
    inverse = jnp.exp(index_f * (-2.0 * math.log(rope_base) / HEAD))
    angle = positions.astype(f32)[:, None] * inverse[None, :]
    cosine, sine = jnp.cos(angle), jnp.sin(angle)
    return jnp.concatenate([cosine, cosine], axis=1), jnp.concatenate([-sine, sine], axis=1)


def scale_kernel(weight, gain, out):
    gains = jnp.broadcast_to(gain[...].astype(f32), (8, weight.shape[0])).T
    out[...] = (weight[...].astype(f32) * gains[:, :1]).astype(bf16)


def scale_rows(weight, gain):
    shard, cols = weight.shape
    return pl.pallas_call(
        scale_kernel,
        grid=(shard // HEAD,),
        in_specs=[
            pl.BlockSpec((HEAD, cols), lambda i: (i, 0)),
            pl.BlockSpec((1, HEAD), lambda i: (0, i)),
        ],
        out_specs=pl.BlockSpec((HEAD, cols), lambda i: (i, 0)),
        out_shape=jax.ShapeDtypeStruct((shard, cols), bf16),
        compiler_params=pltpu.CompilerParams(vmem_limit_bytes=16 * 2**20),
        cost_estimate=pl.CostEstimate(
            flops=shard * cols, bytes_accessed=4 * shard * cols, transcendentals=0
        ),
        name="scale_rows",
    )(weight, gain)


def first_kernel(scale, at, x, cotangent, cosine, sine, kv_grad, inv, far, near, last):
    step = pl.program_id(0)
    width = x.shape[1]
    shard = far.shape[0]
    kvw = cotangent.shape[1] // 2

    @pl.when(step == 0)
    def _():
        total = jnp.zeros((x.shape[0], HEAD), f32)
        for c in range(0, width, HEAD):
            part = x[:, c : c + HEAD].astype(f32)
            total = total + part * part
        mean = jnp.sum(total, axis=1, keepdims=True) / width
        inv[...] = jnp.broadcast_to(lax.rsqrt(mean + epsilon), inv.shape)
        for c in range(0, kvw, HEAD):
            part = cotangent[:, c : c + HEAD].astype(f32)
            turned = pltpu.roll(part, HEAD // 2, 1)
            kv_grad[:, c : c + HEAD] = (part * cosine[...] - turned * sine[...]).astype(bf16)
        kv_grad[:, kvw:] = cotangent[:, kvw:]

    block = x[:, pl.ds(pl.multiple_of(at[step] * shard, shard), shard)]
    normed = (block.astype(f32) * inv[:, :1]).astype(bf16)
    term = (
        lax.dot_general(normed, kv_grad[...], (((0,), (0,)), ((), ())), preferred_element_type=f32)
        * scale
    )

    @pl.when(step == 0)
    def _():
        far[...] = term.astype(bf16)

    @pl.when((step > 0) & (step < pl.num_programs(0) - 1))
    def _():
        near[0] = term

    @pl.when(step == pl.num_programs(0) - 1)
    def _():
        last[...] = term


def first_part(ring, tokens_in, cotangent, cosine, sine, shard, scale):
    rows, width = tokens_in.shape
    cols = cotangent.shape[1]
    order = [ring.half]
    for d in range(ring.half - 1, 0, -1):
        order += [d, -d]
    order.append(0)
    n = ring.count
    fixed = lambda k, at: (0, 0)
    return pl.pallas_call(
        functools.partial(first_kernel, scale),
        grid_spec=pltpu.PrefetchScalarGridSpec(
            num_scalar_prefetch=1,
            grid=(n,),
            in_specs=[
                pl.BlockSpec((rows, width), fixed),
                pl.BlockSpec((rows, cols), fixed),
                pl.BlockSpec((rows, HEAD), fixed),
                pl.BlockSpec((rows, HEAD), fixed),
            ],
            out_specs=[
                pl.BlockSpec((rows, cols), fixed),
                pl.BlockSpec((rows, HEAD), fixed),
                pl.BlockSpec((shard, cols), fixed),
                pl.BlockSpec((1, shard, cols), lambda k, at: (jnp.clip(k - 1, 0, n - 3), 0, 0)),
                pl.BlockSpec((shard, cols), fixed),
            ],
        ),
        out_shape=[
            jax.ShapeDtypeStruct((rows, cols), bf16),
            jax.ShapeDtypeStruct((rows, HEAD), f32),
            jax.ShapeDtypeStruct((shard, cols), bf16),
            jax.ShapeDtypeStruct((n - 2, shard, cols), f32),
            jax.ShapeDtypeStruct((shard, cols), f32),
        ],
        compiler_params=pltpu.CompilerParams(vmem_limit_bytes=40 * 2**20),
        cost_estimate=pl.CostEstimate(
            flops=2 * rows * width * cols,
            bytes_accessed=2 * rows * width + 4 * width * cols,
            transcendentals=0,
        ),
        name="norm_and_weight_terms",
    )(ring.devices_at(order), tokens_in, cotangent, cosine, sine)


def last_kernel(count, own, weight, gain, *refs):
    came, (weight_grad, gain_grad) = refs[:count], refs[-2:]
    term = own[...]
    for ref in came:
        term = term + ref[...].astype(f32)
    product = term * weight[...].astype(f32)
    rows, cols = product.shape
    lanes = product[:, :HEAD]
    for c in range(HEAD, cols, HEAD):
        lanes = lanes + product[:, c : c + HEAD]
    gain_grad[...] = jnp.sum(lanes.T, axis=0, keepdims=True)
    gains = jnp.broadcast_to(gain[...].astype(f32), (8, rows)).T
    weight_grad[0] = term * gains[:, :1]


def last_part(own, weight, gain, sums):
    shard, cols = weight.shape
    many = len(sums)
    tile = HEAD
    tiles = shard // many // tile
    outs = None
    for h, came in enumerate(sums):
        row = lambda i, h=h: h * tiles + i
        specs = [
            pl.BlockSpec((tile, cols), lambda i, row=row: (row(i), 0)),
            pl.BlockSpec((tile, cols), lambda i, row=row: (row(i), 0)),
            pl.BlockSpec((1, tile), lambda i, row=row: (0, row(i))),
        ]
        for ref in came:
            whole = ref.shape[0] == shard
            at = row if whole else lambda i: i
            specs.append(pl.BlockSpec((tile, cols), lambda i, at=at: (at(i), 0)))
        operands = [own, weight, gain, *came]
        if outs is not None:
            specs += [pl.BlockSpec(memory_space=pl.ANY)] * 2
        outs = pl.pallas_call(
            functools.partial(last_kernel, len(came)),
            grid=(tiles,),
            in_specs=specs,
            out_specs=[
                pl.BlockSpec((1, tile, cols), lambda i, row=row: (0, row(i), 0)),
                pl.BlockSpec((1, tile), lambda i, row=row: (0, row(i))),
            ],
            out_shape=[
                jax.ShapeDtypeStruct((1, shard, cols), f32),
                jax.ShapeDtypeStruct((1, shard), f32),
            ],
            input_output_aliases=(
                {} if outs is None else {len(operands): 0, len(operands) + 1: 1}
            ),
            compiler_params=pltpu.CompilerParams(vmem_limit_bytes=16 * 2**20),
            cost_estimate=pl.CostEstimate(
                flops=shard // many * cols * 8,
                bytes_accessed=shard // many * cols * 14,
                transcendentals=0,
            ),
            name="sum_of_terms",
        )(*operands, *(outs or ()))
    return outs


def start_blocks(plan, at, blocks, ws, w_sem, ks):
    shard = ws.shape[0] // len(plan)
    for k in ks:
        for flag, block, start, stop in plan[k]:
            there = ws.at[k * shard + start : k * shard + stop]
            copy = pltpu.make_async_copy(blocks[block], there, w_sem.at[k])
            if flag is None:
                copy.start()
            else:

                @pl.when(at[at.shape[0] - FLAGS + flag] == 1)
                def _(copy=copy):
                    copy.start()


def wait_block(ws, w_sem, k, shard):
    there = ws.at[k * shard : (k + 1) * shard]
    pltpu.make_async_copy(there, there, w_sem.at[k]).wait()


def columns(at, k, shard):
    return pl.ds(pl.multiple_of(at[k] * shard, shard), shard)


def lane_sums(product):
    total = product[:, :HEAD]
    for c in range(HEAD, product.shape[1], HEAD):
        total = total + product[:, c : c + HEAD]
    return total


def grad_of(kv_grad, weight):
    return lax.dot_general(
        kv_grad[...], weight, (((1,), (1,)), ((), ())), preferred_element_type=f32
    )


def early_kernel(plan, at, x, kv_grad, inv, *refs):
    blocks, (sums, grads, xs, ws, ng, x_sem, w_sem, g_sem) = refs[:-8], refs[-8:]
    n = len(plan)
    shard = xs.shape[2]

    def x_copy(k):
        return pltpu.make_async_copy(x.at[:, columns(at, k, shard)], xs.at[k], x_sem.at[k])

    def g_copy(k):
        return pltpu.make_async_copy(ng.at[k], grads.at[k], g_sem.at[k])

    for k in range(n):
        x_copy(k).start()
        start_blocks(plan, at, blocks, ws, w_sem, [k])
    total = None
    for k in range(n):
        x_copy(k).wait()
        wait_block(ws, w_sem, k, shard)
        grad = grad_of(kv_grad, ws[k * shard : (k + 1) * shard, :])
        ng[k] = grad
        g_copy(k).start()
        product = lane_sums(grad * (xs[k].astype(f32) * inv[:, :1]))
        total = product if total is None else total + product
    sums[...] = total
    for k in range(n):
        g_copy(k).wait()


def late_kernel(plan, done, at, x, kv_grad, inv, cosine, sine, *refs):
    own = 9
    blocks, refs = refs[:-own], refs[-own:]
    if done:
        sums0, grads0, *blocks = blocks
    kv_out, input_grad, xs, hs, ws, ng, x_sem, w_sem, g_sem = refs
    n = len(plan)
    rows, width = x.shape
    shard = xs.shape[2]
    cols = ws.shape[1]
    kvw = cols // 2

    def x_copy(k):
        return pltpu.make_async_copy(x.at[:, columns(at, k, shard)], xs.at[k], x_sem.at[k])

    def o_copy(k):
        return pltpu.make_async_copy(xs.at[k], input_grad.at[:, columns(at, k, shard)], x_sem.at[k])

    order = [*range(done, n), *range(done)]
    for k in order:
        x_copy(k).start()
        start_blocks(plan, at, blocks, ws, w_sem, [k])
    if done:
        load = pltpu.make_async_copy(grads0, ng.at[:done], g_sem.at[0])
        load.start()
        total = sums0[...]
    else:
        total = jnp.zeros((rows, HEAD), f32)
    for k in order:
        x_copy(k).wait()
        normed = xs[k].astype(f32) * inv[:, :1]
        hs[:, k * shard : (k + 1) * shard] = normed.astype(bf16)
        if k >= done:
            wait_block(ws, w_sem, k, shard)
            grad = grad_of(kv_grad, ws[k * shard : (k + 1) * shard, :])
            ng[k] = grad
            total = total + lane_sums(grad * normed)
    mean = jnp.sum(total, axis=1, keepdims=True) / width
    if done:
        load.wait()
    for k in range(done):
        wait_block(ws, w_sem, k, shard)

    def project(i, keys):
        tile = 2 * HEAD
        at_column = pl.ds(pl.multiple_of(i * tile, tile), tile)
        pre = jnp.dot(hs[...], ws[:, at_column], preferred_element_type=f32)
        if keys:
            turned = [pltpu.roll(pre[:, c : c + HEAD], HEAD // 2, 1) for c in (0, HEAD)]
            pre = jnp.concatenate(
                [
                    pre[:, c : c + HEAD] * cosine[...] + part * sine[...]
                    for c, part in zip((0, HEAD), turned)
                ],
                axis=1,
            )
        kv_out[:, at_column] = pre.astype(bf16)

    def finish(k):
        scale = inv[:, :1]
        normed = xs[k].astype(f32) * scale
        xs[k] = (scale * (ng[k] - normed * mean)).astype(bf16)
        o_copy(k).start()

    lax.fori_loop(0, n, lambda k, c: (finish(k), c)[1], 0)
    tiles = kvw // (2 * HEAD)
    lax.fori_loop(0, tiles, lambda i, c: (project(i, True), c)[1], 0)
    lax.fori_loop(tiles, 2 * tiles, lambda i, c: (project(i, False), c)[1], 0)
    lax.fori_loop(0, n, lambda k, c: (o_copy(k).wait(), c)[1], 0)


def pick_blocks(blocks, plan):
    used = sorted({entry[1] for entries in plan for entry in entries})
    plan = tuple(
        tuple((flag, used.index(block), *rest) for flag, block, *rest in entries)
        for entries in plan
    )
    return [blocks[i] for i in used], plan


def early_part(at, tokens_in, kv_grad, inv, blocks, plan, shard):
    rows, width = tokens_in.shape
    cols = kv_grad.shape[1]
    n = len(plan)
    blocks, plan = pick_blocks(blocks, plan)
    whole = pl.BlockSpec(memory_space=pltpu.VMEM)
    there = pl.BlockSpec(memory_space=pl.ANY)
    return pl.pallas_call(
        functools.partial(early_kernel, plan),
        in_specs=[pl.BlockSpec(memory_space=pltpu.SMEM), there, whole, whole]
        + [there] * len(blocks),
        out_specs=[whole, there],
        out_shape=[
            jax.ShapeDtypeStruct((rows, HEAD), f32),
            jax.ShapeDtypeStruct((n, rows, shard), f32),
        ],
        scratch_shapes=[
            pltpu.VMEM((n, rows, shard), bf16),
            pltpu.VMEM((n * shard, cols), bf16),
            pltpu.VMEM((n, rows, shard), f32),
        ]
        + [pltpu.SemaphoreType.DMA((n,))] * 3,
        compiler_params=pltpu.CompilerParams(vmem_limit_bytes=40 * 2**20),
        cost_estimate=pl.CostEstimate(
            flops=2 * rows * shard * n * cols,
            bytes_accessed=shard * n * (6 * rows + 2 * cols),
            transcendentals=0,
        ),
        name="project_first",
    )(at, tokens_in, kv_grad, inv, *blocks)


def late_part(at, tokens_in, kv_grad, inv, cosine, sine, blocks, plan, shard, carry=()):
    rows, width = tokens_in.shape
    cols = kv_grad.shape[1]
    n = len(plan)
    done = carry[1].shape[0] if carry else 0
    blocks, plan = pick_blocks(blocks, plan)
    whole = pl.BlockSpec(memory_space=pltpu.VMEM)
    there = pl.BlockSpec(memory_space=pl.ANY)
    return pl.pallas_call(
        functools.partial(late_kernel, plan, done),
        in_specs=[pl.BlockSpec(memory_space=pltpu.SMEM), there]
        + [whole] * 4
        + [whole, there][: len(carry)]
        + [there] * len(blocks),
        out_specs=[whole, there],
        out_shape=[
            jax.ShapeDtypeStruct((rows, cols), bf16),
            jax.ShapeDtypeStruct((rows, width), bf16),
        ],
        scratch_shapes=[
            pltpu.VMEM((n, rows, shard), bf16),
            pltpu.VMEM((rows, n * shard), bf16),
            pltpu.VMEM((n * shard, cols), bf16),
            pltpu.VMEM((n, rows, shard), f32),
        ]
        + [pltpu.SemaphoreType.DMA((n,))] * 3,
        compiler_params=pltpu.CompilerParams(vmem_limit_bytes=48 * 2**20),
        cost_estimate=pl.CostEstimate(
            flops=4 * rows * width * cols,
            bytes_accessed=4 * rows * width + 2 * width * cols,
            transcendentals=0,
        ),
        name="project_last",
    )(at, tokens_in, kv_grad, inv, cosine, sine, *carry, *blocks)


def replica_pairs(value):
    if lax.axis_size("replica") != 4:
        return lax.psum(value, "replica"), False
    value = value.astype(bf16)
    return (value.astype(f32) + replica_swap(value, 1).astype(f32)).astype(bf16), True


def replica_swap(value, step):
    return lax.ppermute(value, "replica", [(r, r ^ step) for r in range(4)])


def exchange_ring(ring, own, far, near, pseudo, early, late, update):
    pairs, halved = pseudo
    total = (pairs, replica_swap(pairs, 2) if halved else jnp.zeros((), f32))
    shard, cut = own.shape[0], own.shape[0] // 2
    blocks = [own]
    from_left = from_right = own
    for d in range(1, ring.half):
        from_left, from_right = ring.to_right(from_left), ring.to_left(from_right)
        blocks += [from_left, from_right]
    from_left, from_right = after((from_left, from_right), total)
    blocks += [ring.to_right(from_left[:cut]), ring.to_left(from_right[cut:])]
    last = len(blocks) - 2
    plan = [((None, k, 0, shard),) for k in range(last)]
    plan.append(((None, last, 0, cut), (None, last + 1, cut, shard)))

    far = after(far, blocks[1], blocks[2])
    from_left, from_right = ring.to_right(far[:cut]), ring.to_left(far[cut:])
    for k in range(0, 2 * (ring.half - 1), 2):
        from_left, from_right = lax.optimization_barrier((from_left, from_right))
        if k == 0:
            from_left = jnp.pad(from_left, ((0, shard - cut), (0, 0)))
            from_right = jnp.pad(from_right, ((cut, 0), (0, 0)))
        from_left = ring.to_right((near[k] + from_left.astype(f32)).astype(bf16))
        from_right = ring.to_left((near[k + 1] + from_right.astype(f32)).astype(bf16))
    sums = [(from_left, from_right)]
    return late(blocks, plan), sums, update(total)


ORDER = {"sum": (-1, 3), "pair": (-1, 4), "inner": (4, None), "far": (1, 5), "partner": (7, None), "first": (6, 7), "update": (4, 7)}
CHAIN = True


def exchange_plane(plane, own, far, near, pseudo, early, late, update):
    shard = own.shape[0]
    at0, at1, at2, at3 = plane.at
    zero = jnp.zeros((), f32)
    pieces = [(0, shard // 2), (shard // 2, shard)]
    halves = range(2)
    wide = lambda v: v.astype(f32)
    pick = jnp.where
    sent, crossed, beside = [own], [own], {}

    def part(value, h):
        return value[pieces[h][0] : pieces[h][1]]

    def chord(value):
        crossed[0] = plane.over_chord(after(value, sent[0], crossed[0] if CHAIN else own))
        return crossed[0]

    def ring(step, to_right, to_left):
        sent[0] = to_right, to_left
        came = lax.optimization_barrier([plane.to_right(to_right), plane.to_left(to_left)])
        for name, (begin, _) in ORDER.items():
            if begin == step:
                beside[name] = tasks[name]()
        return came

    def later(step, *values):
        names = [name for name, (_, end) in ORDER.items() if end == step]
        awaited = [beside[name] for name in names]
        values, awaited = lax.optimization_barrier((after(values, sent[0]), awaited))
        beside.update(zip(names, awaited))
        return values

    ways = lambda flag, at: tuple((flag, at + h, *pieces[h]) for h in halves)
    by_way = lambda steps: [steps[h][way] for way in range(2) for h in halves]
    near_plan = [((None, k, 0, shard),) for k in range(3)] + [ways(None, 3), ways(None, 5)]
    tasks = {
        "far": lambda: chord(pick(at2, *first)),
        "inner": lambda: chord(far),
        "partner": lambda: chord(pick(at1, near[1], near[0]).astype(bf16)),
        "first": lambda: early([after(own, sent[0]), *first, *by_way(two)], near_plan),
        "update": lambda: update(after((pairs, beside["sum"]), sent[0])),
    }

    first = ring(None, own, own)
    beside["pair"] = chord(own)
    pairs, first_swap = pseudo
    came = replica_swap(pairs, 2) if first_swap else jnp.zeros((), f32)
    first, far = lax.optimization_barrier((first, far))
    beside["sum"] = came
    two = [ring(0, *(part(side, 0) for side in first))]
    two.append(ring(1, *(part(side, 1) for side in later(1, *first))))
    three = []
    for h in halves:
        left, right = later(2 + h, *two[h])
        terms = part(far, h)
        three.append(ring(2 + h, pick(at0, terms, left), pick(at3, terms, right)))
    four = []
    for h in halves:
        left, right = later(4 + h, *three[h])
        to_right = wide(part(near[0], h)) + pick(at1, wide(left), zero)
        to_left = wide(part(near[1], h)) + pick(at2, wide(right), zero)
        to_right = pick(at2, left, to_right.astype(bf16))
        to_left = pick(at1, right, to_left.astype(bf16))
        four.append(ring(4 + h, to_right, to_left))
    five = []
    for h in halves:
        left, right = later(6 + h, *four[h])
        to_right = part(near[2], h) + pick(at3, zero, wide(left))
        to_left = part(near[3], h) + pick(at0, zero, wide(right))
        five.append(ring(6 + h, to_right.astype(bf16), to_left.astype(bf16)))
    six = []
    for h in halves:
        left, right = later(8 + h, *five[h])
        over = wide(part(beside["inner"], h))
        to_right = part(near[4], h) + wide(left) + pick(at1, over, zero)
        to_left = part(near[5], h) + wide(right) + pick(at2, over, zero)
        six.append(ring(8 + h, to_right.astype(bf16), to_left.astype(bf16)))
    sums = [(*six[h], beside["partner"]) for h in halves]

    blocks = [own, *first, *by_way(two), beside["pair"], *by_way(three), beside["far"], *by_way(four)]
    plan = near_plan + [
        ((0, 7, 0, shard), *ways(2, 8)),
        ((1, 7, 0, shard), *ways(3, 10)),
        ((4, 12, 0, shard), *ways(5, 13), *ways(6, 15)),
    ]
    return late(blocks, plan, beside["first"]), sums, beside["update"]


def local(
    layer_input,
    norm_gain,
    kv_weight,
    kv_cotangent,
    pseudo_grad,
    outer_momentum,
    global_params,
    local_params,
):
    small = lax.axis_size("fsdp") == 8
    ring = Plane() if small else Ring()
    tokens_in = layer_input[0]
    weight_shard = kv_weight[0]
    cotangent = kv_cotangent[0]
    rows, width = tokens_in.shape
    shard, cols = weight_shard.shape

    own = scale_rows(weight_shard, norm_gain)
    positions = (ring.me * rows + jnp.arange(rows, dtype=jnp.int32)) % SEQ_LEN
    cosine, sine = rope_tables(positions)
    scale = 1.0 / math.sqrt(rows * ring.count)
    pairs, halved = replica_pairs(after(pseudo_grad[0], own))
    kv_grad, inv, far, near, last = first_part(
        ring, tokens_in, after(cotangent, pairs), cosine, sine, shard, scale
    )
    order = [0]
    for d in range(1, ring.half):
        order += [-d, d]
    order.append(ring.half)
    at = [ring.devices_at(order).astype(jnp.int32)]
    if small:
        at0, at1, at2, at3 = ring.at
        flags = [at1, at2, ~at1, ~at2, at1 | at2, at3, at0]
        at.append(jnp.stack(flags).astype(jnp.int32))
    at = jnp.concatenate(at)

    def early(blocks, plan):
        return early_part(at, tokens_in, kv_grad, inv, blocks, plan, shard)

    def late(blocks, plan, carry=()):
        return late_part(at, tokens_in, kv_grad, inv, cosine, sine, blocks, plan, shard, carry)

    def update(total):
        if isinstance(total, tuple):
            total = total[0].astype(f32) + total[1].astype(f32)
        average = total / lax.axis_size("replica")
        momentum_new = momentum_rate * outer_momentum + average
        global_new = global_params - outer_rate * (average + momentum_rate * momentum_new)
        local_new = (
            mixing_rate * local_params[0].astype(f32) + (1.0 - mixing_rate) * global_new
        ).astype(bf16)
        return momentum_new, global_new, local_new

    exchange = exchange_plane if small else exchange_ring
    (kv_out, input_grad), sums, updated = exchange(
        ring, own, far, near, (pairs, halved), early, late, update
    )
    momentum_new, global_new, local_new = updated
    weight_grad, gain_grad = last_part(last, weight_shard, norm_gain, sums)

    return (
        kv_out[None],
        input_grad[None],
        weight_grad,
        gain_grad,
        momentum_new,
        global_new,
        local_new[None],
    )


def solution(mesh):
    in_specs = (
        P("replica", "fsdp", None),
        P("replica", "fsdp"),
        P("replica", "fsdp", None),
        P("replica", "fsdp", None),
        P("replica", "fsdp", None),
        P("fsdp", None),
        P("fsdp", None),
        P("replica", "fsdp", None),
    )
    out_specs = (
        P("replica", "fsdp", None),
        P("replica", "fsdp", None),
        P("replica", "fsdp", None),
        P("replica", "fsdp"),
        P("fsdp", None),
        P("fsdp", None),
        P("replica", "fsdp", None),
    )
    return jax.shard_map(local, mesh=mesh, in_specs=in_specs, out_specs=out_specs, check_vma=False)
```

```python
import functools
import math

import jax
import jax.numpy as jnp
from jax import lax
from jax.experimental import pallas as pl
from jax.experimental.pallas import tpu as pltpu
from jax.sharding import PartitionSpec as P

HEAD = 128
SEQ_LEN = 4096


FLAGS = 7

epsilon = 1e-05
rope_base = 500000.0
momentum_rate = 0.9
outer_rate = 0.7
mixing_rate = 0.5

f32, bf16 = jnp.float32, jnp.bfloat16


class Ring:
    def __init__(self):
        self.count = lax.axis_size("fsdp")
        self.half = self.count // 2
        walk = list(range(0, self.count, 2)) + list(range(self.count - 1, 0, -2))
        after = walk[1:] + walk[:1]
        self.right = list(zip(walk, after))
        self.left = list(zip(after, walk))
        self.me = lax.axis_index("fsdp")
        self.spot = jnp.where(
            self.me % 2 == 0, self.me // 2, self.count - 1 - self.me // 2
        )

    def devices_at(self, distances):
        spot = (self.spot + self.count + jnp.array(distances, jnp.int32)) % self.count
        return jnp.where(spot < self.half, 2 * spot, 2 * (self.count - 1 - spot) + 1)

    def to_right(self, value):
        return lax.ppermute(value, "fsdp", self.right)

    def to_left(self, value):
        return lax.ppermute(value, "fsdp", self.left)


class Plane(Ring):
    def __init__(self):
        super().__init__()
        self.at = [self.spot % 4 == i for i in range(4)]

    def over_chord(self, value):
        return lax.ppermute(value, "fsdp", [(2, 3), (3, 2), (4, 5), (5, 4)])


def after(value, *others):
    return lax.optimization_barrier((value, others))[0]


def rope_tables(positions):
    half = HEAD // 2
    index_f = jnp.arange(half, dtype=f32)
    inverse = jnp.exp(index_f * (-2.0 * math.log(rope_base) / HEAD))
    angle = positions.astype(f32)[:, None] * inverse[None, :]
    cosine, sine = jnp.cos(angle), jnp.sin(angle)
    return jnp.concatenate([cosine, cosine], axis=1), jnp.concatenate([-sine, sine], axis=1)


def scale_kernel(weight, gain, out):
    gains = jnp.broadcast_to(gain[...].astype(f32), (8, weight.shape[0])).T
    out[...] = (weight[...].astype(f32) * gains[:, :1]).astype(bf16)


def scale_rows(weight, gain):
    shard, cols = weight.shape
    return pl.pallas_call(
        scale_kernel,
        grid=(shard // HEAD,),
        in_specs=[
            pl.BlockSpec((HEAD, cols), lambda i: (i, 0)),
            pl.BlockSpec((1, HEAD), lambda i: (0, i)),
        ],
        out_specs=pl.BlockSpec((HEAD, cols), lambda i: (i, 0)),
        out_shape=jax.ShapeDtypeStruct((shard, cols), bf16),
        compiler_params=pltpu.CompilerParams(vmem_limit_bytes=16 * 2**20),
        cost_estimate=pl.CostEstimate(
            flops=shard * cols, bytes_accessed=4 * shard * cols, transcendentals=0
        ),
        name="scale_rows",
    )(weight, gain)


def first_kernel(scale, at, x, cotangent, cosine, sine, kv_grad, inv, far, near, last):
    step = pl.program_id(0)
    width = x.shape[1]
    shard = far.shape[0]
    kvw = cotangent.shape[1] // 2

    @pl.when(step == 0)
    def _():
        total = jnp.zeros((x.shape[0], HEAD), f32)
        for c in range(0, width, HEAD):
            part = x[:, c : c + HEAD].astype(f32)
            total = total + part * part
        mean = jnp.sum(total, axis=1, keepdims=True) / width
        inv[...] = jnp.broadcast_to(lax.rsqrt(mean + epsilon), inv.shape)
        for c in range(0, kvw, HEAD):
            part = cotangent[:, c : c + HEAD].astype(f32)
            turned = pltpu.roll(part, HEAD // 2, 1)
            kv_grad[:, c : c + HEAD] = (part * cosine[...] - turned * sine[...]).astype(bf16)
        kv_grad[:, kvw:] = cotangent[:, kvw:]

    block = x[:, pl.ds(pl.multiple_of(at[step] * shard, shard), shard)]
    normed = (block.astype(f32) * inv[:, :1]).astype(bf16)
    term = (
        lax.dot_general(normed, kv_grad[...], (((0,), (0,)), ((), ())), preferred_element_type=f32)
        * scale
    )

    @pl.when(step == 0)
    def _():
        far[...] = term.astype(bf16)

    @pl.when((step > 0) & (step < pl.num_programs(0) - 1))
    def _():
        near[0] = term

    @pl.when(step == pl.num_programs(0) - 1)
    def _():
        last[...] = term


def first_part(ring, tokens_in, cotangent, cosine, sine, shard, scale):
    rows, width = tokens_in.shape
    cols = cotangent.shape[1]
    order = [ring.half]
    for d in range(ring.half - 1, 0, -1):
        order += [d, -d]
    order.append(0)
    n = ring.count
    fixed = lambda k, at: (0, 0)
    return pl.pallas_call(
        functools.partial(first_kernel, scale),
        grid_spec=pltpu.PrefetchScalarGridSpec(
            num_scalar_prefetch=1,
            grid=(n,),
            in_specs=[
                pl.BlockSpec((rows, width), fixed),
                pl.BlockSpec((rows, cols), fixed),
                pl.BlockSpec((rows, HEAD), fixed),
                pl.BlockSpec((rows, HEAD), fixed),
            ],
            out_specs=[
                pl.BlockSpec((rows, cols), fixed),
                pl.BlockSpec((rows, HEAD), fixed),
                pl.BlockSpec((shard, cols), fixed),
                pl.BlockSpec((1, shard, cols), lambda k, at: (jnp.clip(k - 1, 0, n - 3), 0, 0)),
                pl.BlockSpec((shard, cols), fixed),
            ],
        ),
        out_shape=[
            jax.ShapeDtypeStruct((rows, cols), bf16),
            jax.ShapeDtypeStruct((rows, HEAD), f32),
            jax.ShapeDtypeStruct((shard, cols), bf16),
            jax.ShapeDtypeStruct((n - 2, shard, cols), f32),
            jax.ShapeDtypeStruct((shard, cols), f32),
        ],
        compiler_params=pltpu.CompilerParams(vmem_limit_bytes=60 * 2**20),
        cost_estimate=pl.CostEstimate(
            flops=2 * rows * width * cols,
            bytes_accessed=2 * rows * width + 4 * width * cols,
            transcendentals=0,
        ),
        name="norm_and_weight_terms",
    )(ring.devices_at(order), tokens_in, cotangent, cosine, sine)


def last_kernel(count, own, weight, gain, *refs):
    came, (weight_grad, gain_grad) = refs[:count], refs[-2:]
    term = own[...]
    for ref in came:
        term = term + ref[...].astype(f32)
    product = term * weight[...].astype(f32)
    rows, cols = product.shape
    lanes = product[:, :HEAD]
    for c in range(HEAD, cols, HEAD):
        lanes = lanes + product[:, c : c + HEAD]
    gain_grad[...] = jnp.sum(lanes.T, axis=0, keepdims=True)
    gains = jnp.broadcast_to(gain[...].astype(f32), (8, rows)).T
    weight_grad[0] = term * gains[:, :1]


def last_part(own, weight, gain, sums):
    shard, cols = weight.shape
    many = len(sums)
    tile = HEAD
    tiles = shard // many // tile
    outs = None
    for h, came in enumerate(sums):
        row = lambda i, h=h: h * tiles + i
        specs = [
            pl.BlockSpec((tile, cols), lambda i, row=row: (row(i), 0)),
            pl.BlockSpec((tile, cols), lambda i, row=row: (row(i), 0)),
            pl.BlockSpec((1, tile), lambda i, row=row: (0, row(i))),
        ]
        for ref in came:
            whole = ref.shape[0] == shard
            at = row if whole else lambda i: i
            specs.append(pl.BlockSpec((tile, cols), lambda i, at=at: (at(i), 0)))
        operands = [own, weight, gain, *came]
        if outs is not None:
            specs += [pl.BlockSpec(memory_space=pl.ANY)] * 2
        outs = pl.pallas_call(
            functools.partial(last_kernel, len(came)),
            grid=(tiles,),
            in_specs=specs,
            out_specs=[
                pl.BlockSpec((1, tile, cols), lambda i, row=row: (0, row(i), 0)),
                pl.BlockSpec((1, tile), lambda i, row=row: (0, row(i))),
            ],
            out_shape=[
                jax.ShapeDtypeStruct((1, shard, cols), f32),
                jax.ShapeDtypeStruct((1, shard), f32),
            ],
            input_output_aliases=(
                {} if outs is None else {len(operands): 0, len(operands) + 1: 1}
            ),
            compiler_params=pltpu.CompilerParams(vmem_limit_bytes=16 * 2**20),
            cost_estimate=pl.CostEstimate(
                flops=shard // many * cols * 8,
                bytes_accessed=shard // many * cols * 14,
                transcendentals=0,
            ),
            name="sum_of_terms",
        )(*operands, *(outs or ()))
    return outs


def start_blocks(plan, at, blocks, ws, w_sem, ks):
    shard = ws.shape[0] // len(plan)
    for k in ks:
        for flag, block, start, stop in plan[k]:
            there = ws.at[k * shard + start : k * shard + stop]
            copy = pltpu.make_async_copy(blocks[block], there, w_sem.at[k])
            if flag is None:
                copy.start()
            else:

                @pl.when(at[at.shape[0] - FLAGS + flag] == 1)
                def _(copy=copy):
                    copy.start()


def wait_block(ws, w_sem, k, shard):
    there = ws.at[k * shard : (k + 1) * shard]
    pltpu.make_async_copy(there, there, w_sem.at[k]).wait()


def columns(at, k, shard):
    return pl.ds(pl.multiple_of(at[k] * shard, shard), shard)


def lane_sums(product):
    total = product[:, :HEAD]
    for c in range(HEAD, product.shape[1], HEAD):
        total = total + product[:, c : c + HEAD]
    return total


def grad_of(kv_grad, weight):
    return lax.dot_general(
        kv_grad[...], weight, (((1,), (1,)), ((), ())), preferred_element_type=f32
    )


def early_kernel(plan, at, x, kv_grad, inv, *refs):
    blocks, (sums, grads, xs, ws, ng, x_sem, w_sem, g_sem) = refs[:-8], refs[-8:]
    n = len(plan)
    shard = xs.shape[2]

    def x_copy(k):
        return pltpu.make_async_copy(x.at[:, columns(at, k, shard)], xs.at[k], x_sem.at[k])

    def g_copy(k):
        return pltpu.make_async_copy(ng.at[k], grads.at[k], g_sem.at[k])

    for k in range(n):
        x_copy(k).start()
        start_blocks(plan, at, blocks, ws, w_sem, [k])
    total = None
    for k in range(n):
        x_copy(k).wait()
        wait_block(ws, w_sem, k, shard)
        grad = grad_of(kv_grad, ws[k * shard : (k + 1) * shard, :])
        ng[k] = grad
        g_copy(k).start()
        product = lane_sums(grad * (xs[k].astype(f32) * inv[:, :1]))
        total = product if total is None else total + product
    sums[...] = total
    for k in range(n):
        g_copy(k).wait()


def late_kernel(plan, done, at, x, kv_grad, inv, cosine, sine, *refs):
    own = 9
    blocks, refs = refs[:-own], refs[-own:]
    if done:
        sums0, grads0, *blocks = blocks
    kv_out, input_grad, xs, hs, ws, ng, x_sem, w_sem, g_sem = refs
    n = len(plan)
    rows, width = x.shape
    shard = xs.shape[2]
    cols = ws.shape[1]
    kvw = cols // 2

    def x_copy(k):
        return pltpu.make_async_copy(x.at[:, columns(at, k, shard)], xs.at[k], x_sem.at[k])

    def o_copy(k):
        return pltpu.make_async_copy(xs.at[k], input_grad.at[:, columns(at, k, shard)], x_sem.at[k])

    order = [*range(done, n), *range(done)]
    for k in order:
        x_copy(k).start()
        start_blocks(plan, at, blocks, ws, w_sem, [k])
    if done:
        load = pltpu.make_async_copy(grads0, ng.at[:done], g_sem.at[0])
        load.start()
        total = sums0[...]
    else:
        total = jnp.zeros((rows, HEAD), f32)
    for k in order:
        x_copy(k).wait()
        normed = xs[k].astype(f32) * inv[:, :1]
        hs[:, k * shard : (k + 1) * shard] = normed.astype(bf16)
        if k >= done:
            wait_block(ws, w_sem, k, shard)
            grad = grad_of(kv_grad, ws[k * shard : (k + 1) * shard, :])
            ng[k] = grad
            total = total + lane_sums(grad * normed)
    mean = jnp.sum(total, axis=1, keepdims=True) / width
    if done:
        load.wait()
    for k in range(done):
        wait_block(ws, w_sem, k, shard)

    def project(i, keys):
        tile = 2 * HEAD
        at_column = pl.ds(pl.multiple_of(i * tile, tile), tile)
        pre = jnp.dot(hs[...], ws[:, at_column], preferred_element_type=f32)
        if keys:
            turned = [pltpu.roll(pre[:, c : c + HEAD], HEAD // 2, 1) for c in (0, HEAD)]
            pre = jnp.concatenate(
                [
                    pre[:, c : c + HEAD] * cosine[...] + part * sine[...]
                    for c, part in zip((0, HEAD), turned)
                ],
                axis=1,
            )
        kv_out[:, at_column] = pre.astype(bf16)

    def finish(k):
        scale = inv[:, :1]
        normed = xs[k].astype(f32) * scale
        xs[k] = (scale * (ng[k] - normed * mean)).astype(bf16)
        o_copy(k).start()

    lax.fori_loop(0, n, lambda k, c: (finish(k), c)[1], 0)
    tiles = kvw // (2 * HEAD)
    lax.fori_loop(0, tiles, lambda i, c: (project(i, True), c)[1], 0)
    lax.fori_loop(tiles, 2 * tiles, lambda i, c: (project(i, False), c)[1], 0)
    lax.fori_loop(0, n, lambda k, c: (o_copy(k).wait(), c)[1], 0)


def pick_blocks(blocks, plan):
    used = sorted({entry[1] for entries in plan for entry in entries})
    plan = tuple(
        tuple((flag, used.index(block), *rest) for flag, block, *rest in entries)
        for entries in plan
    )
    return [blocks[i] for i in used], plan


def early_part(at, tokens_in, kv_grad, inv, blocks, plan, shard):
    rows, width = tokens_in.shape
    cols = kv_grad.shape[1]
    n = len(plan)
    blocks, plan = pick_blocks(blocks, plan)
    whole = pl.BlockSpec(memory_space=pltpu.VMEM)
    there = pl.BlockSpec(memory_space=pl.ANY)
    return pl.pallas_call(
        functools.partial(early_kernel, plan),
        in_specs=[pl.BlockSpec(memory_space=pltpu.SMEM), there, whole, whole]
        + [there] * len(blocks),
        out_specs=[whole, there],
        out_shape=[
            jax.ShapeDtypeStruct((rows, HEAD), f32),
            jax.ShapeDtypeStruct((n, rows, shard), f32),
        ],
        scratch_shapes=[
            pltpu.VMEM((n, rows, shard), bf16),
            pltpu.VMEM((n * shard, cols), bf16),
            pltpu.VMEM((n, rows, shard), f32),
        ]
        + [pltpu.SemaphoreType.DMA((n,))] * 3,
        compiler_params=pltpu.CompilerParams(vmem_limit_bytes=40 * 2**20),
        cost_estimate=pl.CostEstimate(
            flops=2 * rows * shard * n * cols,
            bytes_accessed=shard * n * (6 * rows + 2 * cols),
            transcendentals=0,
        ),
        name="project_first",
    )(at, tokens_in, kv_grad, inv, *blocks)


def late_part(at, tokens_in, kv_grad, inv, cosine, sine, blocks, plan, shard, carry=()):
    rows, width = tokens_in.shape
    cols = kv_grad.shape[1]
    n = len(plan)
    done = carry[1].shape[0] if carry else 0
    blocks, plan = pick_blocks(blocks, plan)
    whole = pl.BlockSpec(memory_space=pltpu.VMEM)
    there = pl.BlockSpec(memory_space=pl.ANY)
    return pl.pallas_call(
        functools.partial(late_kernel, plan, done),
        in_specs=[pl.BlockSpec(memory_space=pltpu.SMEM), there]
        + [whole] * 4
        + [whole, there][: len(carry)]
        + [there] * len(blocks),
        out_specs=[whole, there],
        out_shape=[
            jax.ShapeDtypeStruct((rows, cols), bf16),
            jax.ShapeDtypeStruct((rows, width), bf16),
        ],
        scratch_shapes=[
            pltpu.VMEM((n, rows, shard), bf16),
            pltpu.VMEM((rows, n * shard), bf16),
            pltpu.VMEM((n * shard, cols), bf16),
            pltpu.VMEM((n, rows, shard), f32),
        ]
        + [pltpu.SemaphoreType.DMA((n,))] * 3,
        compiler_params=pltpu.CompilerParams(vmem_limit_bytes=48 * 2**20),
        cost_estimate=pl.CostEstimate(
            flops=4 * rows * width * cols,
            bytes_accessed=4 * rows * width + 2 * width * cols,
            transcendentals=0,
        ),
        name="project_last",
    )(at, tokens_in, kv_grad, inv, cosine, sine, *carry, *blocks)


def replica_pairs(value):
    if lax.axis_size("replica") != 4:
        return lax.psum(value, "replica"), False
    value = value.astype(bf16)
    return (value.astype(f32) + replica_swap(value, 1).astype(f32)).astype(bf16), True


def replica_swap(value, step):
    return lax.ppermute(value, "replica", [(r, r ^ step) for r in range(4)])


def exchange_ring(ring, own, far, near, pseudo, early, late, update):
    pairs, halved = pseudo
    total = (pairs, replica_swap(pairs, 2) if halved else jnp.zeros((), f32))
    shard, cut = own.shape[0], own.shape[0] // 2
    blocks = [own]
    from_left = from_right = own
    for d in range(1, ring.half):
        from_left, from_right = ring.to_right(from_left), ring.to_left(from_right)
        blocks += [from_left, from_right]
    from_left, from_right = after((from_left, from_right), total)
    blocks += [ring.to_right(from_left[:cut]), ring.to_left(from_right[cut:])]
    last = len(blocks) - 2
    plan = [((None, k, 0, shard),) for k in range(last)]
    plan.append(((None, last, 0, cut), (None, last + 1, cut, shard)))

    far = after(far, blocks[1], blocks[2])
    from_left, from_right = ring.to_right(far[:cut]), ring.to_left(far[cut:])
    for k in range(0, 2 * (ring.half - 1), 2):
        from_left, from_right = lax.optimization_barrier((from_left, from_right))
        if k == 0:
            from_left = jnp.pad(from_left, ((0, shard - cut), (0, 0)))
            from_right = jnp.pad(from_right, ((cut, 0), (0, 0)))
        from_left = ring.to_right((near[k] + from_left.astype(f32)).astype(bf16))
        from_right = ring.to_left((near[k + 1] + from_right.astype(f32)).astype(bf16))
    sums = [(from_left, from_right)]
    return late(blocks, plan), sums, update(total)


ORDER = {"sum": (-1, 3), "pair": (-1, 4), "inner": (4, None), "far": (1, 5), "partner": (7, None), "first": (6, 7), "update": (4, 7)}
CHAIN = True


def exchange_plane(plane, own, far, near, pseudo, early, late, update):
    shard = own.shape[0]
    at0, at1, at2, at3 = plane.at
    zero = jnp.zeros((), f32)
    pieces = [(0, shard // 2), (shard // 2, shard)]
    halves = range(2)
    wide = lambda v: v.astype(f32)
    pick = jnp.where
    sent, crossed, beside = [own], [own], {}

    def part(value, h):
        return value[pieces[h][0] : pieces[h][1]]

    def chord(value):
        crossed[0] = plane.over_chord(after(value, sent[0], crossed[0] if CHAIN else own))
        return crossed[0]

    def ring(step, to_right, to_left):
        sent[0] = to_right, to_left
        came = lax.optimization_barrier([plane.to_right(to_right), plane.to_left(to_left)])
        for name, (begin, _) in ORDER.items():
            if begin == step:
                beside[name] = tasks[name]()
        return came

    def later(step, *values):
        names = [name for name, (_, end) in ORDER.items() if end == step]
        awaited = [beside[name] for name in names]
        values, awaited = lax.optimization_barrier((after(values, sent[0]), awaited))
        beside.update(zip(names, awaited))
        return values

    ways = lambda flag, at: tuple((flag, at + h, *pieces[h]) for h in halves)
    by_way = lambda steps: [steps[h][way] for way in range(2) for h in halves]
    near_plan = [((None, k, 0, shard),) for k in range(3)] + [ways(None, 3), ways(None, 5)]
    tasks = {
        "far": lambda: chord(pick(at2, *first)),
        "inner": lambda: chord(far),
        "partner": lambda: chord(pick(at1, near[1], near[0]).astype(bf16)),
        "first": lambda: early([after(own, sent[0]), *first, *by_way(two)], near_plan),
        "update": lambda: update(after((pairs, beside["sum"]), sent[0])),
    }

    first = ring(None, own, own)
    beside["pair"] = chord(own)
    pairs, first_swap = pseudo
    came = replica_swap(pairs, 2) if first_swap else jnp.zeros((), f32)
    first, far = lax.optimization_barrier((first, far))
    beside["sum"] = came
    two = [ring(0, *(part(side, 0) for side in first))]
    two.append(ring(1, *(part(side, 1) for side in later(1, *first))))
    three = []
    for h in halves:
        left, right = later(2 + h, *two[h])
        terms = part(far, h)
        three.append(ring(2 + h, pick(at0, terms, left), pick(at3, terms, right)))
    four = []
    for h in halves:
        left, right = later(4 + h, *three[h])
        to_right = wide(part(near[0], h)) + pick(at1, wide(left), zero)
        to_left = wide(part(near[1], h)) + pick(at2, wide(right), zero)
        to_right = pick(at2, left, to_right.astype(bf16))
        to_left = pick(at1, right, to_left.astype(bf16))
        four.append(ring(4 + h, to_right, to_left))
    five = []
    for h in halves:
        left, right = later(6 + h, *four[h])
        to_right = part(near[2], h) + pick(at3, zero, wide(left))
        to_left = part(near[3], h) + pick(at0, zero, wide(right))
        five.append(ring(6 + h, to_right.astype(bf16), to_left.astype(bf16)))
    six = []
    for h in halves:
        left, right = later(8 + h, *five[h])
        over = wide(part(beside["inner"], h))
        to_right = part(near[4], h) + wide(left) + pick(at1, over, zero)
        to_left = part(near[5], h) + wide(right) + pick(at2, over, zero)
        six.append(ring(8 + h, to_right.astype(bf16), to_left.astype(bf16)))
    sums = [(*six[h], beside["partner"]) for h in halves]

    blocks = [own, *first, *by_way(two), beside["pair"], *by_way(three), beside["far"], *by_way(four)]
    plan = near_plan + [
        ((0, 7, 0, shard), *ways(2, 8)),
        ((1, 7, 0, shard), *ways(3, 10)),
        ((4, 12, 0, shard), *ways(5, 13), *ways(6, 15)),
    ]
    return late(blocks, plan, beside["first"]), sums, beside["update"]


def local(
    layer_input,
    norm_gain,
    kv_weight,
    kv_cotangent,
    pseudo_grad,
    outer_momentum,
    global_params,
    local_params,
):
    small = lax.axis_size("fsdp") == 8
    ring = Plane() if small else Ring()
    tokens_in = layer_input[0]
    weight_shard = kv_weight[0]
    cotangent = kv_cotangent[0]
    rows, width = tokens_in.shape
    shard, cols = weight_shard.shape

    own = scale_rows(weight_shard, norm_gain)
    positions = (ring.me * rows + jnp.arange(rows, dtype=jnp.int32)) % SEQ_LEN
    cosine, sine = rope_tables(positions)
    scale = 1.0 / math.sqrt(rows * ring.count)
    pairs, halved = replica_pairs(after(pseudo_grad[0], own))
    kv_grad, inv, far, near, last = first_part(
        ring, tokens_in, after(cotangent, pairs), cosine, sine, shard, scale
    )
    order = [0]
    for d in range(1, ring.half):
        order += [-d, d]
    order.append(ring.half)
    at = [ring.devices_at(order).astype(jnp.int32)]
    if small:
        at0, at1, at2, at3 = ring.at
        flags = [at1, at2, ~at1, ~at2, at1 | at2, at3, at0]
        at.append(jnp.stack(flags).astype(jnp.int32))
    at = jnp.concatenate(at)

    def early(blocks, plan):
        return early_part(at, tokens_in, kv_grad, inv, blocks, plan, shard)

    def late(blocks, plan, carry=()):
        return late_part(at, tokens_in, kv_grad, inv, cosine, sine, blocks, plan, shard, carry)

    def update(total):
        if isinstance(total, tuple):
            total = total[0].astype(f32) + total[1].astype(f32)
        average = total / lax.axis_size("replica")
        momentum_new = momentum_rate * outer_momentum + average
        global_new = global_params - outer_rate * (average + momentum_rate * momentum_new)
        local_new = (
            mixing_rate * local_params[0].astype(f32) + (1.0 - mixing_rate) * global_new
        ).astype(bf16)
        return momentum_new, global_new, local_new

    exchange = exchange_plane if small else exchange_ring
    (kv_out, input_grad), sums, updated = exchange(
        ring, own, far, near, (pairs, halved), early, late, update
    )
    momentum_new, global_new, local_new = updated
    weight_grad, gain_grad = last_part(last, weight_shard, norm_gain, sums)

    return (
        kv_out[None],
        input_grad[None],
        weight_grad,
        gain_grad,
        momentum_new,
        global_new,
        local_new[None],
    )


def solution(mesh):
    in_specs = (
        P("replica", "fsdp", None),
        P("replica", "fsdp"),
        P("replica", "fsdp", None),
        P("replica", "fsdp", None),
        P("replica", "fsdp", None),
        P("fsdp", None),
        P("fsdp", None),
        P("replica", "fsdp", None),
    )
    out_specs = (
        P("replica", "fsdp", None),
        P("replica", "fsdp", None),
        P("replica", "fsdp", None),
        P("replica", "fsdp"),
        P("fsdp", None),
        P("fsdp", None),
        P("replica", "fsdp", None),
    )
    return jax.shard_map(local, mesh=mesh, in_specs=in_specs, out_specs=out_specs, check_vma=False)
```

```python
import functools
import math

import jax
import jax.numpy as jnp
from jax import lax
from jax.experimental import pallas as pl
from jax.experimental.pallas import tpu as pltpu
from jax.sharding import PartitionSpec as P

HEAD = 128
SEQ_LEN = 4096


FLAGS = 7

epsilon = 1e-05
rope_base = 500000.0
momentum_rate = 0.9
outer_rate = 0.7
mixing_rate = 0.5

f32, bf16 = jnp.float32, jnp.bfloat16


class Ring:
    def __init__(self):
        self.count = lax.axis_size("fsdp")
        self.half = self.count // 2
        walk = list(range(0, self.count, 2)) + list(range(self.count - 1, 0, -2))
        after = walk[1:] + walk[:1]
        self.right = list(zip(walk, after))
        self.left = list(zip(after, walk))
        self.me = lax.axis_index("fsdp")
        self.spot = jnp.where(
            self.me % 2 == 0, self.me // 2, self.count - 1 - self.me // 2
        )

    def devices_at(self, distances):
        spot = (self.spot + self.count + jnp.array(distances, jnp.int32)) % self.count
        return jnp.where(spot < self.half, 2 * spot, 2 * (self.count - 1 - spot) + 1)

    def to_right(self, value):
        return lax.ppermute(value, "fsdp", self.right)

    def to_left(self, value):
        return lax.ppermute(value, "fsdp", self.left)


class Plane(Ring):
    def __init__(self):
        super().__init__()
        self.at = [self.spot % 4 == i for i in range(4)]

    def over_chord(self, value):
        return lax.ppermute(value, "fsdp", [(2, 3), (3, 2), (4, 5), (5, 4)])


def after(value, *others):
    return lax.optimization_barrier((value, others))[0]


def rope_tables(positions):
    half = HEAD // 2
    index_f = jnp.arange(half, dtype=f32)
    inverse = jnp.exp(index_f * (-2.0 * math.log(rope_base) / HEAD))
    angle = positions.astype(f32)[:, None] * inverse[None, :]
    cosine, sine = jnp.cos(angle), jnp.sin(angle)
    return jnp.concatenate([cosine, cosine], axis=1), jnp.concatenate([-sine, sine], axis=1)


def scale_kernel(weight, gain, out):
    gains = jnp.broadcast_to(gain[...].astype(f32), (8, weight.shape[0])).T
    out[...] = (weight[...].astype(f32) * gains[:, :1]).astype(bf16)


def scale_rows(weight, gain):
    shard, cols = weight.shape
    return pl.pallas_call(
        scale_kernel,
        grid=(shard // HEAD,),
        in_specs=[
            pl.BlockSpec((HEAD, cols), lambda i: (i, 0)),
            pl.BlockSpec((1, HEAD), lambda i: (0, i)),
        ],
        out_specs=pl.BlockSpec((HEAD, cols), lambda i: (i, 0)),
        out_shape=jax.ShapeDtypeStruct((shard, cols), bf16),
        compiler_params=pltpu.CompilerParams(vmem_limit_bytes=16 * 2**20),
        cost_estimate=pl.CostEstimate(
            flops=shard * cols, bytes_accessed=4 * shard * cols, transcendentals=0
        ),
        name="scale_rows",
    )(weight, gain)


def first_kernel(scale, at, x_in, cotangent, cosine, sine, *refs):
    kv_out, inv_out, far_out, near, last_out, kv_grad, inv, far, last, x, sem, x_sem = refs
    step = pl.program_id(0)
    copies = [
        pltpu.make_async_copy(here, there, sem.at[i])
        for i, (here, there) in enumerate(
            ((kv_grad, kv_out), (inv, inv_out), (far, far_out), (last, last_out))
        )
    ]
    width = x.shape[1]
    shard = far.shape[0]
    kvw = cotangent.shape[1] // 2

    @pl.when(step == 0)
    def _():
        loads = []
        for i, c in enumerate(range(0, width, shard)):
            there = x.at[:, c : c + shard]
            loads.append(pltpu.make_async_copy(x_in.at[:, c : c + shard], there, x_sem.at[i]))
            loads[i].start()
        total = jnp.zeros((x.shape[0], HEAD), f32)
        for i, load in enumerate(loads):
            load.wait()
            for c in range(i * shard, (i + 1) * shard, HEAD):
                part = x[:, c : c + HEAD].astype(f32)
                total = total + part * part
        mean = jnp.sum(total, axis=1, keepdims=True) / width
        inv[...] = jnp.broadcast_to(lax.rsqrt(mean + epsilon), inv.shape)
        for c in range(0, kvw, HEAD):
            part = cotangent[:, c : c + HEAD].astype(f32)
            turned = pltpu.roll(part, HEAD // 2, 1)
            kv_grad[:, c : c + HEAD] = (part * cosine[...] - turned * sine[...]).astype(bf16)
        kv_grad[:, kvw:] = cotangent[:, kvw:]
        copies[0].start()
        copies[1].start()

    block = x[:, pl.ds(pl.multiple_of(at[step] * shard, shard), shard)]
    normed = (block.astype(f32) * inv[:, :1]).astype(bf16)
    term = (
        lax.dot_general(normed, kv_grad[...], (((0,), (0,)), ((), ())), preferred_element_type=f32)
        * scale
    )

    @pl.when(step == 0)
    def _():
        far[...] = term.astype(bf16)
        copies[2].start()

    @pl.when((step > 0) & (step < pl.num_programs(0) - 1))
    def _():
        near[0] = term

    @pl.when(step == pl.num_programs(0) - 1)
    def _():
        last[...] = term
        copies[3].start()
        for copy in copies:
            copy.wait()


def first_part(ring, tokens_in, cotangent, cosine, sine, shard, scale):
    rows, width = tokens_in.shape
    cols = cotangent.shape[1]
    order = [ring.half]
    for d in range(ring.half - 1, 0, -1):
        order += [d, -d]
    order.append(0)
    n = ring.count
    fixed = lambda k, at: (0, 0)
    there = pl.BlockSpec(memory_space=pltpu.HBM)
    return pl.pallas_call(
        functools.partial(first_kernel, scale),
        grid_spec=pltpu.PrefetchScalarGridSpec(
            num_scalar_prefetch=1,
            grid=(n,),
            in_specs=[
                pl.BlockSpec(memory_space=pl.ANY),
                pl.BlockSpec((rows, cols), fixed),
                pl.BlockSpec((rows, HEAD), fixed),
                pl.BlockSpec((rows, HEAD), fixed),
            ],
            out_specs=[
                there,
                there,
                there,
                pl.BlockSpec((1, shard, cols), lambda k, at: (jnp.clip(k - 1, 0, n - 3), 0, 0)),
                there,
            ],
            scratch_shapes=[
                pltpu.VMEM((rows, cols), bf16),
                pltpu.VMEM((rows, HEAD), f32),
                pltpu.VMEM((shard, cols), bf16),
                pltpu.VMEM((shard, cols), f32),
                pltpu.VMEM((rows, width), bf16),
                pltpu.SemaphoreType.DMA((4,)),
                pltpu.SemaphoreType.DMA((n,)),
            ],
        ),
        out_shape=[
            jax.ShapeDtypeStruct((rows, cols), bf16),
            jax.ShapeDtypeStruct((rows, HEAD), f32),
            jax.ShapeDtypeStruct((shard, cols), bf16),
            jax.ShapeDtypeStruct((n - 2, shard, cols), f32),
            jax.ShapeDtypeStruct((shard, cols), f32),
        ],
        compiler_params=pltpu.CompilerParams(vmem_limit_bytes=60 * 2**20),
        cost_estimate=pl.CostEstimate(
            flops=2 * rows * width * cols,
            bytes_accessed=2 * rows * width + 4 * width * cols,
            transcendentals=0,
        ),
        name="norm_and_weight_terms",
    )(ring.devices_at(order), tokens_in, cotangent, cosine, sine)


def last_kernel(count, own, weight, gain, *refs):
    came, (weight_grad, gain_grad) = refs[:count], refs[-2:]
    term = own[...]
    for ref in came:
        term = term + ref[...].astype(f32)
    product = term * weight[...].astype(f32)
    rows, cols = product.shape
    lanes = product[:, :HEAD]
    for c in range(HEAD, cols, HEAD):
        lanes = lanes + product[:, c : c + HEAD]
    gain_grad[...] = jnp.sum(lanes.T, axis=0, keepdims=True)
    gains = jnp.broadcast_to(gain[...].astype(f32), (8, rows)).T
    weight_grad[0] = term * gains[:, :1]


def last_part(own, weight, gain, sums):
    shard, cols = weight.shape
    many = len(sums)
    tile = HEAD
    tiles = shard // many // tile
    outs = None
    for h, came in enumerate(sums):
        row = lambda i, h=h: h * tiles + i
        specs = [
            pl.BlockSpec((tile, cols), lambda i, row=row: (row(i), 0)),
            pl.BlockSpec((tile, cols), lambda i, row=row: (row(i), 0)),
            pl.BlockSpec((1, tile), lambda i, row=row: (0, row(i))),
        ]
        for ref in came:
            whole = ref.shape[0] == shard
            at = row if whole else lambda i: i
            specs.append(pl.BlockSpec((tile, cols), lambda i, at=at: (at(i), 0)))
        operands = [own, weight, gain, *came]
        if outs is not None:
            specs += [pl.BlockSpec(memory_space=pl.ANY)] * 2
        outs = pl.pallas_call(
            functools.partial(last_kernel, len(came)),
            grid=(tiles,),
            in_specs=specs,
            out_specs=[
                pl.BlockSpec((1, tile, cols), lambda i, row=row: (0, row(i), 0)),
                pl.BlockSpec((1, tile), lambda i, row=row: (0, row(i))),
            ],
            out_shape=[
                jax.ShapeDtypeStruct((1, shard, cols), f32),
                jax.ShapeDtypeStruct((1, shard), f32),
            ],
            input_output_aliases=(
                {} if outs is None else {len(operands): 0, len(operands) + 1: 1}
            ),
            compiler_params=pltpu.CompilerParams(vmem_limit_bytes=16 * 2**20),
            cost_estimate=pl.CostEstimate(
                flops=shard // many * cols * 8,
                bytes_accessed=shard // many * cols * 14,
                transcendentals=0,
            ),
            name="sum_of_terms",
        )(*operands, *(outs or ()))
    return outs


def start_blocks(plan, at, blocks, ws, w_sem, ks):
    shard = ws.shape[0] // len(plan)
    for k in ks:
        for flag, block, start, stop in plan[k]:
            there = ws.at[k * shard + start : k * shard + stop]
            copy = pltpu.make_async_copy(blocks[block], there, w_sem.at[k])
            if flag is None:
                copy.start()
            else:

                @pl.when(at[at.shape[0] - FLAGS + flag] == 1)
                def _(copy=copy):
                    copy.start()


def wait_block(ws, w_sem, k, shard):
    there = ws.at[k * shard : (k + 1) * shard]
    pltpu.make_async_copy(there, there, w_sem.at[k]).wait()


def columns(at, k, shard):
    return pl.ds(pl.multiple_of(at[k] * shard, shard), shard)


def lane_sums(product):
    total = product[:, :HEAD]
    for c in range(HEAD, product.shape[1], HEAD):
        total = total + product[:, c : c + HEAD]
    return total


def grad_of(kv_grad, weight):
    return lax.dot_general(
        kv_grad[...], weight, (((1,), (1,)), ((), ())), preferred_element_type=f32
    )


def early_kernel(plan, at, x, kv_grad, inv, *refs):
    blocks, (sums, grads, xs, ws, ng, x_sem, w_sem, g_sem) = refs[:-8], refs[-8:]
    n = len(plan)
    shard = xs.shape[2]

    def x_copy(k):
        return pltpu.make_async_copy(x.at[:, columns(at, k, shard)], xs.at[k], x_sem.at[k])

    def g_copy(k):
        return pltpu.make_async_copy(ng.at[k], grads.at[k], g_sem.at[k])

    for k in range(n):
        x_copy(k).start()
        start_blocks(plan, at, blocks, ws, w_sem, [k])
    total = None
    for k in range(n):
        x_copy(k).wait()
        wait_block(ws, w_sem, k, shard)
        grad = grad_of(kv_grad, ws[k * shard : (k + 1) * shard, :])
        ng[k] = grad
        g_copy(k).start()
        product = lane_sums(grad * (xs[k].astype(f32) * inv[:, :1]))
        total = product if total is None else total + product
    sums[...] = total
    for k in range(n):
        g_copy(k).wait()


def late_kernel(plan, done, at, x, kv_grad, inv, cosine, sine, *refs):
    own = 9
    blocks, refs = refs[:-own], refs[-own:]
    if done:
        sums0, grads0, *blocks = blocks
    kv_out, input_grad, xs, hs, ws, ng, x_sem, w_sem, g_sem = refs
    n = len(plan)
    rows, width = x.shape
    shard = xs.shape[2]
    cols = ws.shape[1]
    kvw = cols // 2

    def x_copy(k):
        return pltpu.make_async_copy(x.at[:, columns(at, k, shard)], xs.at[k], x_sem.at[k])

    def o_copy(k):
        return pltpu.make_async_copy(xs.at[k], input_grad.at[:, columns(at, k, shard)], x_sem.at[k])

    order = [*range(done, n), *range(done)]
    for k in order:
        x_copy(k).start()
        start_blocks(plan, at, blocks, ws, w_sem, [k])
    if done:
        load = pltpu.make_async_copy(grads0, ng.at[:done], g_sem.at[0])
        load.start()
        total = sums0[...]
    else:
        total = jnp.zeros((rows, HEAD), f32)
    for k in order:
        x_copy(k).wait()
        normed = xs[k].astype(f32) * inv[:, :1]
        hs[:, k * shard : (k + 1) * shard] = normed.astype(bf16)
        if k >= done:
            wait_block(ws, w_sem, k, shard)
            grad = grad_of(kv_grad, ws[k * shard : (k + 1) * shard, :])
            ng[k] = grad
            total = total + lane_sums(grad * normed)
    mean = jnp.sum(total, axis=1, keepdims=True) / width
    if done:
        load.wait()
    for k in range(done):
        wait_block(ws, w_sem, k, shard)

    def project(i, keys):
        tile = 2 * HEAD
        at_column = pl.ds(pl.multiple_of(i * tile, tile), tile)
        pre = jnp.dot(hs[...], ws[:, at_column], preferred_element_type=f32)
        if keys:
            turned = [pltpu.roll(pre[:, c : c + HEAD], HEAD // 2, 1) for c in (0, HEAD)]
            pre = jnp.concatenate(
                [
                    pre[:, c : c + HEAD] * cosine[...] + part * sine[...]
                    for c, part in zip((0, HEAD), turned)
                ],
                axis=1,
            )
        kv_out[:, at_column] = pre.astype(bf16)

    def finish(k):
        scale = inv[:, :1]
        normed = xs[k].astype(f32) * scale
        xs[k] = (scale * (ng[k] - normed * mean)).astype(bf16)
        o_copy(k).start()

    lax.fori_loop(0, n, lambda k, c: (finish(k), c)[1], 0)
    tiles = kvw // (2 * HEAD)
    lax.fori_loop(0, tiles, lambda i, c: (project(i, True), c)[1], 0)
    lax.fori_loop(tiles, 2 * tiles, lambda i, c: (project(i, False), c)[1], 0)
    lax.fori_loop(0, n, lambda k, c: (o_copy(k).wait(), c)[1], 0)


def pick_blocks(blocks, plan):
    used = sorted({entry[1] for entries in plan for entry in entries})
    plan = tuple(
        tuple((flag, used.index(block), *rest) for flag, block, *rest in entries)
        for entries in plan
    )
    return [blocks[i] for i in used], plan


def early_part(at, tokens_in, kv_grad, inv, blocks, plan, shard):
    rows, width = tokens_in.shape
    cols = kv_grad.shape[1]
    n = len(plan)
    blocks, plan = pick_blocks(blocks, plan)
    whole = pl.BlockSpec(memory_space=pltpu.VMEM)
    there = pl.BlockSpec(memory_space=pl.ANY)
    return pl.pallas_call(
        functools.partial(early_kernel, plan),
        in_specs=[pl.BlockSpec(memory_space=pltpu.SMEM), there, whole, whole]
        + [there] * len(blocks),
        out_specs=[whole, there],
        out_shape=[
            jax.ShapeDtypeStruct((rows, HEAD), f32),
            jax.ShapeDtypeStruct((n, rows, shard), f32),
        ],
        scratch_shapes=[
            pltpu.VMEM((n, rows, shard), bf16),
            pltpu.VMEM((n * shard, cols), bf16),
            pltpu.VMEM((n, rows, shard), f32),
        ]
        + [pltpu.SemaphoreType.DMA((n,))] * 3,
        compiler_params=pltpu.CompilerParams(vmem_limit_bytes=40 * 2**20),
        cost_estimate=pl.CostEstimate(
            flops=2 * rows * shard * n * cols,
            bytes_accessed=shard * n * (6 * rows + 2 * cols),
            transcendentals=0,
        ),
        name="project_first",
    )(at, tokens_in, kv_grad, inv, *blocks)


def late_part(at, tokens_in, kv_grad, inv, cosine, sine, blocks, plan, shard, carry=()):
    rows, width = tokens_in.shape
    cols = kv_grad.shape[1]
    n = len(plan)
    done = carry[1].shape[0] if carry else 0
    blocks, plan = pick_blocks(blocks, plan)
    whole = pl.BlockSpec(memory_space=pltpu.VMEM)
    there = pl.BlockSpec(memory_space=pl.ANY)
    return pl.pallas_call(
        functools.partial(late_kernel, plan, done),
        in_specs=[pl.BlockSpec(memory_space=pltpu.SMEM), there]
        + [whole] * 4
        + [whole, there][: len(carry)]
        + [there] * len(blocks),
        out_specs=[whole, there],
        out_shape=[
            jax.ShapeDtypeStruct((rows, cols), bf16),
            jax.ShapeDtypeStruct((rows, width), bf16),
        ],
        scratch_shapes=[
            pltpu.VMEM((n, rows, shard), bf16),
            pltpu.VMEM((rows, n * shard), bf16),
            pltpu.VMEM((n * shard, cols), bf16),
            pltpu.VMEM((n, rows, shard), f32),
        ]
        + [pltpu.SemaphoreType.DMA((n,))] * 3,
        compiler_params=pltpu.CompilerParams(vmem_limit_bytes=48 * 2**20),
        cost_estimate=pl.CostEstimate(
            flops=4 * rows * width * cols,
            bytes_accessed=4 * rows * width + 2 * width * cols,
            transcendentals=0,
        ),
        name="project_last",
    )(at, tokens_in, kv_grad, inv, cosine, sine, *carry, *blocks)


def replica_pairs(value):
    if lax.axis_size("replica") != 4:
        return lax.psum(value, "replica"), False
    value = value.astype(bf16)
    return (value.astype(f32) + replica_swap(value, 1).astype(f32)).astype(bf16), True


def replica_swap(value, step):
    return lax.ppermute(value, "replica", [(r, r ^ step) for r in range(4)])


def exchange_ring(ring, own, far, near, pseudo, early, late, update):
    pairs, halved = pseudo
    total = (pairs, replica_swap(pairs, 2) if halved else jnp.zeros((), f32))
    shard, cut = own.shape[0], own.shape[0] // 2
    blocks = [own]
    from_left = from_right = own
    for d in range(1, ring.half):
        from_left, from_right = ring.to_right(from_left), ring.to_left(from_right)
        blocks += [from_left, from_right]
    from_left, from_right = after((from_left, from_right), total)
    blocks += [ring.to_right(from_left[:cut]), ring.to_left(from_right[cut:])]
    last = len(blocks) - 2
    plan = [((None, k, 0, shard),) for k in range(last)]
    plan.append(((None, last, 0, cut), (None, last + 1, cut, shard)))

    far = after(far, blocks[1], blocks[2])
    from_left, from_right = ring.to_right(far[:cut]), ring.to_left(far[cut:])
    for k in range(0, 2 * (ring.half - 1), 2):
        from_left, from_right = lax.optimization_barrier((from_left, from_right))
        if k == 0:
            from_left = jnp.pad(from_left, ((0, shard - cut), (0, 0)))
            from_right = jnp.pad(from_right, ((cut, 0), (0, 0)))
        from_left = ring.to_right((near[k] + from_left.astype(f32)).astype(bf16))
        from_right = ring.to_left((near[k + 1] + from_right.astype(f32)).astype(bf16))
    sums = [(from_left, from_right)]
    return late(blocks, plan), sums, update(total)


ORDER = {"sum": (-1, 3), "pair": (-1, 4), "inner": (4, None), "far": (1, 5), "partner": (7, None), "first": (6, 7), "update": (4, 7)}
CHAIN = True


def exchange_plane(plane, own, far, near, pseudo, early, late, update):
    shard = own.shape[0]
    at0, at1, at2, at3 = plane.at
    zero = jnp.zeros((), f32)
    pieces = [(0, shard // 2), (shard // 2, shard)]
    halves = range(2)
    wide = lambda v: v.astype(f32)
    pick = jnp.where
    sent, crossed, beside = [own], [own], {}

    def part(value, h):
        return value[pieces[h][0] : pieces[h][1]]

    def chord(value):
        crossed[0] = plane.over_chord(after(value, sent[0], crossed[0] if CHAIN else own))
        return crossed[0]

    def ring(step, to_right, to_left):
        sent[0] = to_right, to_left
        came = lax.optimization_barrier([plane.to_right(to_right), plane.to_left(to_left)])
        for name, (begin, _) in ORDER.items():
            if begin == step:
                beside[name] = tasks[name]()
        return came

    def later(step, *values):
        names = [name for name, (_, end) in ORDER.items() if end == step]
        awaited = [beside[name] for name in names]
        values, awaited = lax.optimization_barrier((after(values, sent[0]), awaited))
        beside.update(zip(names, awaited))
        return values

    ways = lambda flag, at: tuple((flag, at + h, *pieces[h]) for h in halves)
    by_way = lambda steps: [steps[h][way] for way in range(2) for h in halves]
    near_plan = [((None, k, 0, shard),) for k in range(3)] + [ways(None, 3), ways(None, 5)]
    tasks = {
        "far": lambda: chord(pick(at2, *first)),
        "inner": lambda: chord(far),
        "partner": lambda: chord(pick(at1, near[1], near[0]).astype(bf16)),
        "first": lambda: early([after(own, sent[0]), *first, *by_way(two)], near_plan),
        "update": lambda: update(after((pairs, beside["sum"]), sent[0])),
    }

    first = ring(None, own, own)
    beside["pair"] = chord(own)
    pairs, first_swap = pseudo
    came = replica_swap(pairs, 2) if first_swap else jnp.zeros((), f32)
    first, far = lax.optimization_barrier((first, far))
    beside["sum"] = came
    two = [ring(0, *(part(side, 0) for side in first))]
    two.append(ring(1, *(part(side, 1) for side in later(1, *first))))
    three = []
    for h in halves:
        left, right = later(2 + h, *two[h])
        terms = part(far, h)
        three.append(ring(2 + h, pick(at0, terms, left), pick(at3, terms, right)))
    four = []
    for h in halves:
        left, right = later(4 + h, *three[h])
        to_right = wide(part(near[0], h)) + pick(at1, wide(left), zero)
        to_left = wide(part(near[1], h)) + pick(at2, wide(right), zero)
        to_right = pick(at2, left, to_right.astype(bf16))
        to_left = pick(at1, right, to_left.astype(bf16))
        four.append(ring(4 + h, to_right, to_left))
    five = []
    for h in halves:
        left, right = later(6 + h, *four[h])
        to_right = part(near[2], h) + pick(at3, zero, wide(left))
        to_left = part(near[3], h) + pick(at0, zero, wide(right))
        five.append(ring(6 + h, to_right.astype(bf16), to_left.astype(bf16)))
    six = []
    for h in halves:
        left, right = later(8 + h, *five[h])
        over = wide(part(beside["inner"], h))
        to_right = part(near[4], h) + wide(left) + pick(at1, over, zero)
        to_left = part(near[5], h) + wide(right) + pick(at2, over, zero)
        six.append(ring(8 + h, to_right.astype(bf16), to_left.astype(bf16)))
    sums = [(*six[h], beside["partner"]) for h in halves]

    blocks = [own, *first, *by_way(two), beside["pair"], *by_way(three), beside["far"], *by_way(four)]
    plan = near_plan + [
        ((0, 7, 0, shard), *ways(2, 8)),
        ((1, 7, 0, shard), *ways(3, 10)),
        ((4, 12, 0, shard), *ways(5, 13), *ways(6, 15)),
    ]
    return late(blocks, plan, beside["first"]), sums, beside["update"]


def local(
    layer_input,
    norm_gain,
    kv_weight,
    kv_cotangent,
    pseudo_grad,
    outer_momentum,
    global_params,
    local_params,
):
    small = lax.axis_size("fsdp") == 8
    ring = Plane() if small else Ring()
    tokens_in = layer_input[0]
    weight_shard = kv_weight[0]
    cotangent = kv_cotangent[0]
    rows, width = tokens_in.shape
    shard, cols = weight_shard.shape

    own = scale_rows(weight_shard, norm_gain)
    positions = (ring.me * rows + jnp.arange(rows, dtype=jnp.int32)) % SEQ_LEN
    cosine, sine = rope_tables(positions)
    scale = 1.0 / math.sqrt(rows * ring.count)
    pairs, halved = replica_pairs(after(pseudo_grad[0], own))
    kv_grad, inv, far, near, last = first_part(
        ring, tokens_in, after(cotangent, pairs), cosine, sine, shard, scale
    )
    order = [0]
    for d in range(1, ring.half):
        order += [-d, d]
    order.append(ring.half)
    at = [ring.devices_at(order).astype(jnp.int32)]
    if small:
        at0, at1, at2, at3 = ring.at
        flags = [at1, at2, ~at1, ~at2, at1 | at2, at3, at0]
        at.append(jnp.stack(flags).astype(jnp.int32))
    at = jnp.concatenate(at)

    def early(blocks, plan):
        return early_part(at, tokens_in, kv_grad, inv, blocks, plan, shard)

    def late(blocks, plan, carry=()):
        return late_part(at, tokens_in, kv_grad, inv, cosine, sine, blocks, plan, shard, carry)

    def update(total):
        if isinstance(total, tuple):
            total = total[0].astype(f32) + total[1].astype(f32)
        average = total / lax.axis_size("replica")
        momentum_new = momentum_rate * outer_momentum + average
        global_new = global_params - outer_rate * (average + momentum_rate * momentum_new)
        local_new = (
            mixing_rate * local_params[0].astype(f32) + (1.0 - mixing_rate) * global_new
        ).astype(bf16)
        return momentum_new, global_new, local_new

    exchange = exchange_plane if small else exchange_ring
    (kv_out, input_grad), sums, updated = exchange(
        ring, own, far, near, (pairs, halved), early, late, update
    )
    momentum_new, global_new, local_new = updated
    weight_grad, gain_grad = last_part(last, weight_shard, norm_gain, sums)

    return (
        kv_out[None],
        input_grad[None],
        weight_grad,
        gain_grad,
        momentum_new,
        global_new,
        local_new[None],
    )


def solution(mesh):
    in_specs = (
        P("replica", "fsdp", None),
        P("replica", "fsdp"),
        P("replica", "fsdp", None),
        P("replica", "fsdp", None),
        P("replica", "fsdp", None),
        P("fsdp", None),
        P("fsdp", None),
        P("replica", "fsdp", None),
    )
    out_specs = (
        P("replica", "fsdp", None),
        P("replica", "fsdp", None),
        P("replica", "fsdp", None),
        P("replica", "fsdp"),
        P("fsdp", None),
        P("fsdp", None),
        P("replica", "fsdp", None),
    )
    return jax.shard_map(local, mesh=mesh, in_specs=in_specs, out_specs=out_specs, check_vma=False)
```

```python
import functools
import math

import jax
import jax.numpy as jnp
from jax import lax
from jax.experimental import pallas as pl
from jax.experimental.pallas import tpu as pltpu
from jax.sharding import PartitionSpec as P

HEAD = 128
SEQ_LEN = 4096


FLAGS = 7

epsilon = 1e-05
rope_base = 500000.0
momentum_rate = 0.9
outer_rate = 0.7
mixing_rate = 0.5

f32, bf16 = jnp.float32, jnp.bfloat16


class Ring:
    def __init__(self):
        self.count = lax.axis_size("fsdp")
        self.half = self.count // 2
        walk = list(range(0, self.count, 2)) + list(range(self.count - 1, 0, -2))
        after = walk[1:] + walk[:1]
        self.right = list(zip(walk, after))
        self.left = list(zip(after, walk))
        self.me = lax.axis_index("fsdp")
        self.spot = jnp.where(
            self.me % 2 == 0, self.me // 2, self.count - 1 - self.me // 2
        )

    def devices_at(self, distances):
        spot = (self.spot + self.count + jnp.array(distances, jnp.int32)) % self.count
        return jnp.where(spot < self.half, 2 * spot, 2 * (self.count - 1 - spot) + 1)

    def to_right(self, value):
        return lax.ppermute(value, "fsdp", self.right)

    def to_left(self, value):
        return lax.ppermute(value, "fsdp", self.left)


class Plane(Ring):
    def __init__(self):
        super().__init__()
        self.at = [self.spot % 4 == i for i in range(4)]

    def over_chord(self, value):
        return lax.ppermute(value, "fsdp", [(2, 3), (3, 2), (4, 5), (5, 4)])


def after(value, *others):
    return lax.optimization_barrier((value, others))[0]


def rope_tables(positions):
    half = HEAD // 2
    index_f = jnp.arange(half, dtype=f32)
    inverse = jnp.exp(index_f * (-2.0 * math.log(rope_base) / HEAD))
    angle = positions.astype(f32)[:, None] * inverse[None, :]
    cosine, sine = jnp.cos(angle), jnp.sin(angle)
    return jnp.concatenate([cosine, cosine], axis=1), jnp.concatenate([-sine, sine], axis=1)


def scale_kernel(weight, gain, out):
    gains = jnp.broadcast_to(gain[...].astype(f32), (8, weight.shape[0])).T
    out[...] = (weight[...].astype(f32) * gains[:, :1]).astype(bf16)


def scale_rows(weight, gain):
    shard, cols = weight.shape
    return pl.pallas_call(
        scale_kernel,
        grid=(shard // HEAD,),
        in_specs=[
            pl.BlockSpec((HEAD, cols), lambda i: (i, 0)),
            pl.BlockSpec((1, HEAD), lambda i: (0, i)),
        ],
        out_specs=pl.BlockSpec((HEAD, cols), lambda i: (i, 0)),
        out_shape=jax.ShapeDtypeStruct((shard, cols), bf16),
        compiler_params=pltpu.CompilerParams(vmem_limit_bytes=16 * 2**20),
        cost_estimate=pl.CostEstimate(
            flops=shard * cols, bytes_accessed=4 * shard * cols, transcendentals=0
        ),
        name="scale_rows",
    )(weight, gain)


def first_kernel(scale, at, x, cotangent, cosine, sine, kv_grad, inv, far, near, last):
    step = pl.program_id(0)
    width = x.shape[1]
    shard = far.shape[0]
    kvw = cotangent.shape[1] // 2

    @pl.when(step == 0)
    def _():
        total = jnp.zeros((x.shape[0], HEAD), f32)
        for c in range(0, width, HEAD):
            part = x[:, c : c + HEAD].astype(f32)
            total = total + part * part
        mean = jnp.sum(total, axis=1, keepdims=True) / width
        inv[...] = jnp.broadcast_to(lax.rsqrt(mean + epsilon), inv.shape)
        for c in range(0, kvw, HEAD):
            part = cotangent[:, c : c + HEAD].astype(f32)
            turned = pltpu.roll(part, HEAD // 2, 1)
            kv_grad[:, c : c + HEAD] = (part * cosine[...] - turned * sine[...]).astype(bf16)
        kv_grad[:, kvw:] = cotangent[:, kvw:]

    block = x[:, pl.ds(pl.multiple_of(at[step] * shard, shard), shard)]
    normed = (block.astype(f32) * inv[:, :1]).astype(bf16)
    term = (
        lax.dot_general(normed, kv_grad[...], (((0,), (0,)), ((), ())), preferred_element_type=f32)
        * scale
    )

    @pl.when(step == 0)
    def _():
        far[...] = term.astype(bf16)

    @pl.when((step > 0) & (step < pl.num_programs(0) - 1))
    def _():
        near[0] = term

    @pl.when(step == pl.num_programs(0) - 1)
    def _():
        last[...] = term


def first_part(ring, tokens_in, cotangent, cosine, sine, shard, scale):
    rows, width = tokens_in.shape
    cols = cotangent.shape[1]
    order = [ring.half]
    for d in range(ring.half - 1, 0, -1):
        order += [d, -d]
    order.append(0)
    n = ring.count
    fixed = lambda k, at: (0, 0)
    return pl.pallas_call(
        functools.partial(first_kernel, scale),
        grid_spec=pltpu.PrefetchScalarGridSpec(
            num_scalar_prefetch=1,
            grid=(n,),
            in_specs=[
                pl.BlockSpec((rows, width), fixed),
                pl.BlockSpec((rows, cols), fixed),
                pl.BlockSpec((rows, HEAD), fixed),
                pl.BlockSpec((rows, HEAD), fixed),
            ],
            out_specs=[
                pl.BlockSpec((rows, cols), fixed),
                pl.BlockSpec((rows, HEAD), fixed),
                pl.BlockSpec((shard, cols), fixed),
                pl.BlockSpec((1, shard, cols), lambda k, at: (jnp.clip(k - 1, 0, n - 3), 0, 0)),
                pl.BlockSpec((shard, cols), fixed),
            ],
        ),
        out_shape=[
            jax.ShapeDtypeStruct((rows, cols), bf16),
            jax.ShapeDtypeStruct((rows, HEAD), f32),
            jax.ShapeDtypeStruct((shard, cols), bf16),
            jax.ShapeDtypeStruct((n - 2, shard, cols), f32),
            jax.ShapeDtypeStruct((shard, cols), f32),
        ],
        compiler_params=pltpu.CompilerParams(vmem_limit_bytes=40 * 2**20),
        cost_estimate=pl.CostEstimate(
            flops=2 * rows * width * cols,
            bytes_accessed=2 * rows * width + 4 * width * cols,
            transcendentals=0,
        ),
        name="norm_and_weight_terms",
    )(ring.devices_at(order), tokens_in, cotangent, cosine, sine)


def last_kernel(count, own, weight, gain, *refs):
    came, (weight_grad, gain_grad) = refs[:count], refs[-2:]
    term = own[...]
    for ref in came:
        term = term + ref[...].astype(f32)
    product = term * weight[...].astype(f32)
    rows, cols = product.shape
    lanes = product[:, :HEAD]
    for c in range(HEAD, cols, HEAD):
        lanes = lanes + product[:, c : c + HEAD]
    gain_grad[...] = jnp.sum(lanes.T, axis=0, keepdims=True)
    gains = jnp.broadcast_to(gain[...].astype(f32), (8, rows)).T
    weight_grad[0] = term * gains[:, :1]


def last_part(own, weight, gain, sums):
    shard, cols = weight.shape
    many = len(sums)
    tile = HEAD
    tiles = shard // many // tile
    outs = None
    for h, came in enumerate(sums):
        row = lambda i, h=h: h * tiles + i
        specs = [
            pl.BlockSpec((tile, cols), lambda i, row=row: (row(i), 0)),
            pl.BlockSpec((tile, cols), lambda i, row=row: (row(i), 0)),
            pl.BlockSpec((1, tile), lambda i, row=row: (0, row(i))),
        ]
        for ref in came:
            whole = ref.shape[0] == shard
            at = row if whole else lambda i: i
            specs.append(pl.BlockSpec((tile, cols), lambda i, at=at: (at(i), 0)))
        operands = [own, weight, gain, *came]
        if outs is not None:
            specs += [pl.BlockSpec(memory_space=pl.ANY)] * 2
        outs = pl.pallas_call(
            functools.partial(last_kernel, len(came)),
            grid=(tiles,),
            in_specs=specs,
            out_specs=[
                pl.BlockSpec((1, tile, cols), lambda i, row=row: (0, row(i), 0)),
                pl.BlockSpec((1, tile), lambda i, row=row: (0, row(i))),
            ],
            out_shape=[
                jax.ShapeDtypeStruct((1, shard, cols), f32),
                jax.ShapeDtypeStruct((1, shard), f32),
            ],
            input_output_aliases=(
                {} if outs is None else {len(operands): 0, len(operands) + 1: 1}
            ),
            compiler_params=pltpu.CompilerParams(vmem_limit_bytes=16 * 2**20),
            cost_estimate=pl.CostEstimate(
                flops=shard // many * cols * 8,
                bytes_accessed=shard // many * cols * 14,
                transcendentals=0,
            ),
            name="sum_of_terms",
        )(*operands, *(outs or ()))
    return outs


def start_blocks(plan, at, blocks, ws, w_sem, ks):
    shard = ws.shape[0] // len(plan)
    for k in ks:
        for flag, block, start, stop in plan[k]:
            there = ws.at[k * shard + start : k * shard + stop]
            copy = pltpu.make_async_copy(blocks[block], there, w_sem.at[k])
            if flag is None:
                copy.start()
            else:

                @pl.when(at[at.shape[0] - FLAGS + flag] == 1)
                def _(copy=copy):
                    copy.start()


def wait_block(ws, w_sem, k, shard):
    there = ws.at[k * shard : (k + 1) * shard]
    pltpu.make_async_copy(there, there, w_sem.at[k]).wait()


def columns(at, k, shard):
    return pl.ds(pl.multiple_of(at[k] * shard, shard), shard)


def lane_sums(product):
    total = product[:, :HEAD]
    for c in range(HEAD, product.shape[1], HEAD):
        total = total + product[:, c : c + HEAD]
    return total


def grad_of(kv_grad, weight):
    return lax.dot_general(
        kv_grad[...], weight, (((1,), (1,)), ((), ())), preferred_element_type=f32
    )


def early_kernel(plan, at, x, kv_grad, inv, *refs):
    blocks, (sums, grads, xs, ws, ng, x_sem, w_sem, g_sem) = refs[:-8], refs[-8:]
    n = len(plan)
    shard = xs.shape[2]

    def x_copy(k):
        return pltpu.make_async_copy(x.at[:, columns(at, k, shard)], xs.at[k], x_sem.at[k])

    def g_copy(k):
        return pltpu.make_async_copy(ng.at[k], grads.at[k], g_sem.at[k])

    for k in range(n):
        x_copy(k).start()
        start_blocks(plan, at, blocks, ws, w_sem, [k])
    total = None
    for k in range(n):
        x_copy(k).wait()
        wait_block(ws, w_sem, k, shard)
        grad = grad_of(kv_grad, ws[k * shard : (k + 1) * shard, :])
        ng[k] = grad
        g_copy(k).start()
        product = lane_sums(grad * (xs[k].astype(f32) * inv[:, :1]))
        total = product if total is None else total + product
    sums[...] = total
    for k in range(n):
        g_copy(k).wait()


def late_kernel(plan, done, at, x, kv_grad, inv, cosine, sine, *refs):
    own = 9
    blocks, refs = refs[:-own], refs[-own:]
    if done:
        sums0, grads0, *blocks = blocks
    kv_out, input_grad, xs, hs, ws, ng, x_sem, w_sem, g_sem = refs
    n = len(plan)
    rows, width = x.shape
    shard = xs.shape[2]
    cols = ws.shape[1]
    kvw = cols // 2

    def x_copy(k):
        return pltpu.make_async_copy(x.at[:, columns(at, k, shard)], xs.at[k], x_sem.at[k])

    def o_copy(k):
        return pltpu.make_async_copy(xs.at[k], input_grad.at[:, columns(at, k, shard)], x_sem.at[k])

    order = [*range(done, n), *range(done)]
    for k in order:
        x_copy(k).start()
        start_blocks(plan, at, blocks, ws, w_sem, [k])
    if done:
        load = pltpu.make_async_copy(grads0, ng.at[:done], g_sem.at[0])
        load.start()
        total = sums0[...]
    else:
        total = jnp.zeros((rows, HEAD), f32)
    for k in order:
        x_copy(k).wait()
        normed = xs[k].astype(f32) * inv[:, :1]
        hs[:, k * shard : (k + 1) * shard] = normed.astype(bf16)
        if k >= done:
            wait_block(ws, w_sem, k, shard)
            grad = grad_of(kv_grad, ws[k * shard : (k + 1) * shard, :])
            ng[k] = grad
            total = total + lane_sums(grad * normed)
    mean = jnp.sum(total, axis=1, keepdims=True) / width
    if done:
        load.wait()
    for k in range(done):
        wait_block(ws, w_sem, k, shard)

    def project(i, keys):
        tile = 2 * HEAD
        at_column = pl.ds(pl.multiple_of(i * tile, tile), tile)
        pre = jnp.dot(hs[...], ws[:, at_column], preferred_element_type=f32)
        if keys:
            turned = [pltpu.roll(pre[:, c : c + HEAD], HEAD // 2, 1) for c in (0, HEAD)]
            pre = jnp.concatenate(
                [
                    pre[:, c : c + HEAD] * cosine[...] + part * sine[...]
                    for c, part in zip((0, HEAD), turned)
                ],
                axis=1,
            )
        kv_out[:, at_column] = pre.astype(bf16)

    def finish(k):
        scale = inv[:, :1]
        normed = xs[k].astype(f32) * scale
        xs[k] = (scale * (ng[k] - normed * mean)).astype(bf16)
        o_copy(k).start()

    lax.fori_loop(0, n, lambda k, c: (finish(k), c)[1], 0)
    tiles = kvw // (2 * HEAD)
    lax.fori_loop(0, tiles, lambda i, c: (project(i, True), c)[1], 0)
    lax.fori_loop(tiles, 2 * tiles, lambda i, c: (project(i, False), c)[1], 0)
    lax.fori_loop(0, n, lambda k, c: (o_copy(k).wait(), c)[1], 0)


def pick_blocks(blocks, plan):
    used = sorted({entry[1] for entries in plan for entry in entries})
    plan = tuple(
        tuple((flag, used.index(block), *rest) for flag, block, *rest in entries)
        for entries in plan
    )
    return [blocks[i] for i in used], plan


def early_part(at, tokens_in, kv_grad, inv, blocks, plan, shard):
    rows, width = tokens_in.shape
    cols = kv_grad.shape[1]
    n = len(plan)
    blocks, plan = pick_blocks(blocks, plan)
    whole = pl.BlockSpec(memory_space=pltpu.VMEM)
    there = pl.BlockSpec(memory_space=pl.ANY)
    return pl.pallas_call(
        functools.partial(early_kernel, plan),
        in_specs=[pl.BlockSpec(memory_space=pltpu.SMEM), there, whole, whole]
        + [there] * len(blocks),
        out_specs=[whole, there],
        out_shape=[
            jax.ShapeDtypeStruct((rows, HEAD), f32),
            jax.ShapeDtypeStruct((n, rows, shard), f32),
        ],
        scratch_shapes=[
            pltpu.VMEM((n, rows, shard), bf16),
            pltpu.VMEM((n * shard, cols), bf16),
            pltpu.VMEM((n, rows, shard), f32),
        ]
        + [pltpu.SemaphoreType.DMA((n,))] * 3,
        compiler_params=pltpu.CompilerParams(vmem_limit_bytes=40 * 2**20),
        cost_estimate=pl.CostEstimate(
            flops=2 * rows * shard * n * cols,
            bytes_accessed=shard * n * (6 * rows + 2 * cols),
            transcendentals=0,
        ),
        name="project_first",
    )(at, tokens_in, kv_grad, inv, *blocks)


def late_part(at, tokens_in, kv_grad, inv, cosine, sine, blocks, plan, shard, carry=()):
    rows, width = tokens_in.shape
    cols = kv_grad.shape[1]
    n = len(plan)
    done = carry[1].shape[0] if carry else 0
    blocks, plan = pick_blocks(blocks, plan)
    whole = pl.BlockSpec(memory_space=pltpu.VMEM)
    there = pl.BlockSpec(memory_space=pl.ANY)
    return pl.pallas_call(
        functools.partial(late_kernel, plan, done),
        in_specs=[pl.BlockSpec(memory_space=pltpu.SMEM), there]
        + [whole] * 4
        + [whole, there][: len(carry)]
        + [there] * len(blocks),
        out_specs=[whole, there],
        out_shape=[
            jax.ShapeDtypeStruct((rows, cols), bf16),
            jax.ShapeDtypeStruct((rows, width), bf16),
        ],
        scratch_shapes=[
            pltpu.VMEM((n, rows, shard), bf16),
            pltpu.VMEM((rows, n * shard), bf16),
            pltpu.VMEM((n * shard, cols), bf16),
            pltpu.VMEM((n, rows, shard), f32),
        ]
        + [pltpu.SemaphoreType.DMA((n,))] * 3,
        compiler_params=pltpu.CompilerParams(vmem_limit_bytes=48 * 2**20),
        cost_estimate=pl.CostEstimate(
            flops=4 * rows * width * cols,
            bytes_accessed=4 * rows * width + 2 * width * cols,
            transcendentals=0,
        ),
        name="project_last",
    )(at, tokens_in, kv_grad, inv, cosine, sine, *carry, *blocks)


def replica_pairs(value):
    if lax.axis_size("replica") != 4:
        return lax.psum(value, "replica"), False
    value = value.astype(bf16)
    return (value.astype(f32) + replica_swap(value, 1).astype(f32)).astype(bf16), True


def replica_swap(value, step):
    return lax.ppermute(value, "replica", [(r, r ^ step) for r in range(4)])


def exchange_ring(ring, own, far, near, pseudo, early, late, update):
    pairs, halved = pseudo
    total = (pairs, replica_swap(pairs, 2) if halved else jnp.zeros((), f32))
    shard, cut = own.shape[0], own.shape[0] // 2
    blocks = [own]
    from_left = from_right = own
    for d in range(1, ring.half):
        from_left, from_right = ring.to_right(from_left), ring.to_left(from_right)
        blocks += [from_left, from_right]
    from_left, from_right = after((from_left, from_right), total)
    blocks += [ring.to_right(from_left[:cut]), ring.to_left(from_right[cut:])]
    last = len(blocks) - 2
    plan = [((None, k, 0, shard),) for k in range(last)]
    plan.append(((None, last, 0, cut), (None, last + 1, cut, shard)))

    far = after(far, blocks[1], blocks[2])
    from_left, from_right = ring.to_right(far[:cut]), ring.to_left(far[cut:])
    for k in range(0, 2 * (ring.half - 1), 2):
        from_left, from_right = lax.optimization_barrier((from_left, from_right))
        if k == 0:
            from_left = jnp.pad(from_left, ((0, shard - cut), (0, 0)))
            from_right = jnp.pad(from_right, ((cut, 0), (0, 0)))
        from_left = ring.to_right((near[k] + from_left.astype(f32)).astype(bf16))
        from_right = ring.to_left((near[k + 1] + from_right.astype(f32)).astype(bf16))
    sums = [(from_left, from_right)]
    return late(blocks, plan), sums, update(total)


ORDER = {"sum": (-1, 1), "pair": (-1, 3), "inner": (2, 7), "far": (1, 5), "partner": (7, None), "first": (2, 3), "update": (5, 9)}
CHAIN = True


def exchange_plane(plane, own, far, near, pseudo, early, late, update):
    shard = own.shape[0]
    at0, at1, at2, at3 = plane.at
    zero = jnp.zeros((), f32)
    pieces = [(0, shard // 2), (shard // 2, shard)]
    halves = range(2)
    wide = lambda v: v.astype(f32)
    pick = jnp.where
    sent, crossed, beside = [own], [own], {}

    def part(value, h):
        return value[pieces[h][0] : pieces[h][1]]

    def chord(value):
        crossed[0] = plane.over_chord(after(value, sent[0], crossed[0] if CHAIN else own))
        return crossed[0]

    def ring(step, to_right, to_left):
        sent[0] = to_right, to_left
        came = lax.optimization_barrier([plane.to_right(to_right), plane.to_left(to_left)])
        for name, (begin, _) in ORDER.items():
            if begin == step:
                beside[name] = tasks[name]()
        return came

    def later(step, *values):
        names = [name for name, (_, end) in ORDER.items() if end == step]
        awaited = [beside[name] for name in names]
        values, awaited = lax.optimization_barrier((after(values, sent[0]), awaited))
        beside.update(zip(names, awaited))
        return values

    ways = lambda flag, at: tuple((flag, at + h, *pieces[h]) for h in halves)
    by_way = lambda steps: [steps[h][way] for way in range(2) for h in halves]
    near_plan = [((None, k, 0, shard),) for k in range(3)] + [ways(None, 3), ways(None, 5)]
    tasks = {
        "far": lambda: chord(pick(at2, *first)),
        "inner": lambda: chord(far),
        "partner": lambda: chord(pick(at1, near[1], near[0]).astype(bf16)),
        "first": lambda: early([after(own, sent[0]), *first, *by_way(two)], near_plan),
        "update": lambda: update(after((pairs, beside["sum"]), sent[0])),
    }

    first = ring(None, own, own)
    beside["pair"] = chord(own)
    pairs, first_swap = pseudo
    came = replica_swap(pairs, 2) if first_swap else jnp.zeros((), f32)
    first, far = lax.optimization_barrier((first, far))
    beside["sum"] = came
    two = [ring(0, *(part(side, 0) for side in first))]
    two.append(ring(1, *(part(side, 1) for side in later(1, *first))))
    three = []
    for h in halves:
        left, right = later(2 + h, *two[h])
        terms = part(far, h)
        three.append(ring(2 + h, pick(at0, terms, left), pick(at3, terms, right)))
    four = []
    for h in halves:
        left, right = later(4 + h, *three[h])
        to_right = wide(part(near[0], h)) + pick(at1, wide(left), zero)
        to_left = wide(part(near[1], h)) + pick(at2, wide(right), zero)
        to_right = pick(at2, left, to_right.astype(bf16))
        to_left = pick(at1, right, to_left.astype(bf16))
        four.append(ring(4 + h, to_right, to_left))
    five = []
    for h in halves:
        left, right = later(6 + h, *four[h])
        to_right = part(near[2], h) + pick(at3, zero, wide(left))
        to_left = part(near[3], h) + pick(at0, zero, wide(right))
        five.append(ring(6 + h, to_right.astype(bf16), to_left.astype(bf16)))
    six = []
    for h in halves:
        left, right = later(8 + h, *five[h])
        over = wide(part(beside["inner"], h))
        to_right = part(near[4], h) + wide(left) + pick(at1, over, zero)
        to_left = part(near[5], h) + wide(right) + pick(at2, over, zero)
        six.append(ring(8 + h, to_right.astype(bf16), to_left.astype(bf16)))
    sums = [(*six[h], beside["partner"]) for h in halves]

    blocks = [own, *first, *by_way(two), beside["pair"], *by_way(three), beside["far"], *by_way(four)]
    plan = near_plan + [
        ((0, 7, 0, shard), *ways(2, 8)),
        ((1, 7, 0, shard), *ways(3, 10)),
        ((4, 12, 0, shard), *ways(5, 13), *ways(6, 15)),
    ]
    return late(blocks, plan, beside["first"]), sums, beside["update"]


def local(
    layer_input,
    norm_gain,
    kv_weight,
    kv_cotangent,
    pseudo_grad,
    outer_momentum,
    global_params,
    local_params,
):
    small = lax.axis_size("fsdp") == 8
    ring = Plane() if small else Ring()
    tokens_in = layer_input[0]
    weight_shard = kv_weight[0]
    cotangent = kv_cotangent[0]
    rows, width = tokens_in.shape
    shard, cols = weight_shard.shape

    own = scale_rows(weight_shard, norm_gain)
    positions = (ring.me * rows + jnp.arange(rows, dtype=jnp.int32)) % SEQ_LEN
    cosine, sine = rope_tables(positions)
    scale = 1.0 / math.sqrt(rows * ring.count)
    pairs, halved = replica_pairs(after(pseudo_grad[0], own))
    kv_grad, inv, far, near, last = first_part(
        ring, tokens_in, after(cotangent, pairs), cosine, sine, shard, scale
    )
    order = [0]
    for d in range(1, ring.half):
        order += [-d, d]
    order.append(ring.half)
    at = [ring.devices_at(order).astype(jnp.int32)]
    if small:
        at0, at1, at2, at3 = ring.at
        flags = [at1, at2, ~at1, ~at2, at1 | at2, at3, at0]
        at.append(jnp.stack(flags).astype(jnp.int32))
    at = jnp.concatenate(at)

    def early(blocks, plan):
        return early_part(at, tokens_in, kv_grad, inv, blocks, plan, shard)

    def late(blocks, plan, carry=()):
        return late_part(at, tokens_in, kv_grad, inv, cosine, sine, blocks, plan, shard, carry)

    def update(total):
        if isinstance(total, tuple):
            total = total[0].astype(f32) + total[1].astype(f32)
        average = total / lax.axis_size("replica")
        momentum_new = momentum_rate * outer_momentum + average
        global_new = global_params - outer_rate * (average + momentum_rate * momentum_new)
        local_new = (
            mixing_rate * local_params[0].astype(f32) + (1.0 - mixing_rate) * global_new
        ).astype(bf16)
        return momentum_new, global_new, local_new

    exchange = exchange_plane if small else exchange_ring
    (kv_out, input_grad), sums, updated = exchange(
        ring, own, far, near, (pairs, halved), early, late, update
    )
    momentum_new, global_new, local_new = updated
    weight_grad, gain_grad = last_part(last, weight_shard, norm_gain, sums)

    return (
        kv_out[None],
        input_grad[None],
        weight_grad,
        gain_grad,
        momentum_new,
        global_new,
        local_new[None],
    )


def solution(mesh):
    in_specs = (
        P("replica", "fsdp", None),
        P("replica", "fsdp"),
        P("replica", "fsdp", None),
        P("replica", "fsdp", None),
        P("replica", "fsdp", None),
        P("fsdp", None),
        P("fsdp", None),
        P("replica", "fsdp", None),
    )
    out_specs = (
        P("replica", "fsdp", None),
        P("replica", "fsdp", None),
        P("replica", "fsdp", None),
        P("replica", "fsdp"),
        P("fsdp", None),
        P("fsdp", None),
        P("replica", "fsdp", None),
    )
    return jax.shard_map(local, mesh=mesh, in_specs=in_specs, out_specs=out_specs, check_vma=False)
```

```python
import functools
import math

import jax
import jax.numpy as jnp
from jax import lax
from jax.experimental import pallas as pl
from jax.experimental.pallas import tpu as pltpu
from jax.sharding import PartitionSpec as P

HEAD = 128
SEQ_LEN = 4096


FLAGS = 7

epsilon = 1e-05
rope_base = 500000.0
momentum_rate = 0.9
outer_rate = 0.7
mixing_rate = 0.5

f32, bf16 = jnp.float32, jnp.bfloat16


class Ring:
    def __init__(self):
        self.count = lax.axis_size("fsdp")
        self.half = self.count // 2
        walk = list(range(0, self.count, 2)) + list(range(self.count - 1, 0, -2))
        after = walk[1:] + walk[:1]
        self.right = list(zip(walk, after))
        self.left = list(zip(after, walk))
        self.me = lax.axis_index("fsdp")
        self.spot = jnp.where(
            self.me % 2 == 0, self.me // 2, self.count - 1 - self.me // 2
        )

    def devices_at(self, distances):
        spot = (self.spot + self.count + jnp.array(distances, jnp.int32)) % self.count
        return jnp.where(spot < self.half, 2 * spot, 2 * (self.count - 1 - spot) + 1)

    def to_right(self, value):
        return lax.ppermute(value, "fsdp", self.right)

    def to_left(self, value):
        return lax.ppermute(value, "fsdp", self.left)


class Plane(Ring):
    def __init__(self):
        super().__init__()
        self.at = [self.spot % 4 == i for i in range(4)]

    def over_chord(self, value):
        return lax.ppermute(value, "fsdp", [(2, 3), (3, 2), (4, 5), (5, 4)])


def after(value, *others):
    return lax.optimization_barrier((value, others))[0]


def rope_tables(positions):
    half = HEAD // 2
    index_f = jnp.arange(half, dtype=f32)
    inverse = jnp.exp(index_f * (-2.0 * math.log(rope_base) / HEAD))
    angle = positions.astype(f32)[:, None] * inverse[None, :]
    cosine, sine = jnp.cos(angle), jnp.sin(angle)
    return jnp.concatenate([cosine, cosine], axis=1), jnp.concatenate([-sine, sine], axis=1)


def scale_kernel(weight, gain, out):
    gains = jnp.broadcast_to(gain[...].astype(f32), (8, weight.shape[0])).T
    out[...] = (weight[...].astype(f32) * gains[:, :1]).astype(bf16)


def scale_rows(weight, gain):
    shard, cols = weight.shape
    return pl.pallas_call(
        scale_kernel,
        grid=(shard // HEAD,),
        in_specs=[
            pl.BlockSpec((HEAD, cols), lambda i: (i, 0)),
            pl.BlockSpec((1, HEAD), lambda i: (0, i)),
        ],
        out_specs=pl.BlockSpec((HEAD, cols), lambda i: (i, 0)),
        out_shape=jax.ShapeDtypeStruct((shard, cols), bf16),
        compiler_params=pltpu.CompilerParams(vmem_limit_bytes=16 * 2**20),
        cost_estimate=pl.CostEstimate(
            flops=shard * cols, bytes_accessed=4 * shard * cols, transcendentals=0
        ),
        name="scale_rows",
    )(weight, gain)


def first_kernel(scale, at, x, cotangent, cosine, sine, kv_grad, inv, far, near, last):
    step = pl.program_id(0)
    width = x.shape[1]
    shard = far.shape[0]
    kvw = cotangent.shape[1] // 2

    @pl.when(step == 0)
    def _():
        total = jnp.zeros((x.shape[0], HEAD), f32)
        for c in range(0, width, HEAD):
            part = x[:, c : c + HEAD].astype(f32)
            total = total + part * part
        mean = jnp.sum(total, axis=1, keepdims=True) / width
        inv[...] = jnp.broadcast_to(lax.rsqrt(mean + epsilon), inv.shape)
        for c in range(0, kvw, HEAD):
            part = cotangent[:, c : c + HEAD].astype(f32)
            turned = pltpu.roll(part, HEAD // 2, 1)
            kv_grad[:, c : c + HEAD] = (part * cosine[...] - turned * sine[...]).astype(bf16)
        kv_grad[:, kvw:] = cotangent[:, kvw:]

    block = x[:, pl.ds(pl.multiple_of(at[step] * shard, shard), shard)]
    normed = (block.astype(f32) * inv[:, :1]).astype(bf16)
    term = (
        lax.dot_general(normed, kv_grad[...], (((0,), (0,)), ((), ())), preferred_element_type=f32)
        * scale
    )

    @pl.when(step == 0)
    def _():
        far[...] = term.astype(bf16)

    @pl.when((step > 0) & (step < pl.num_programs(0) - 1))
    def _():
        near[0] = term

    @pl.when(step == pl.num_programs(0) - 1)
    def _():
        last[...] = term


def first_part(ring, tokens_in, cotangent, cosine, sine, shard, scale):
    rows, width = tokens_in.shape
    cols = cotangent.shape[1]
    order = [ring.half]
    for d in range(ring.half - 1, 0, -1):
        order += [d, -d]
    order.append(0)
    n = ring.count
    fixed = lambda k, at: (0, 0)
    return pl.pallas_call(
        functools.partial(first_kernel, scale),
        grid_spec=pltpu.PrefetchScalarGridSpec(
            num_scalar_prefetch=1,
            grid=(n,),
            in_specs=[
                pl.BlockSpec((rows, width), fixed),
                pl.BlockSpec((rows, cols), fixed),
                pl.BlockSpec((rows, HEAD), fixed),
                pl.BlockSpec((rows, HEAD), fixed),
            ],
            out_specs=[
                pl.BlockSpec((rows, cols), fixed),
                pl.BlockSpec((rows, HEAD), fixed),
                pl.BlockSpec((shard, cols), fixed),
                pl.BlockSpec((1, shard, cols), lambda k, at: (jnp.clip(k - 1, 0, n - 3), 0, 0)),
                pl.BlockSpec((shard, cols), fixed),
            ],
        ),
        out_shape=[
            jax.ShapeDtypeStruct((rows, cols), bf16),
            jax.ShapeDtypeStruct((rows, HEAD), f32),
            jax.ShapeDtypeStruct((shard, cols), bf16),
            jax.ShapeDtypeStruct((n - 2, shard, cols), f32),
            jax.ShapeDtypeStruct((shard, cols), f32),
        ],
        compiler_params=pltpu.CompilerParams(vmem_limit_bytes=40 * 2**20),
        cost_estimate=pl.CostEstimate(
            flops=2 * rows * width * cols,
            bytes_accessed=2 * rows * width + 4 * width * cols,
            transcendentals=0,
        ),
        name="norm_and_weight_terms",
    )(ring.devices_at(order), tokens_in, cotangent, cosine, sine)


def last_kernel(count, own, weight, gain, *refs):
    came, (weight_grad, gain_grad) = refs[:count], refs[-2:]
    term = own[...]
    for ref in came:
        term = term + ref[...].astype(f32)
    product = term * weight[...].astype(f32)
    rows, cols = product.shape
    lanes = product[:, :HEAD]
    for c in range(HEAD, cols, HEAD):
        lanes = lanes + product[:, c : c + HEAD]
    gain_grad[...] = jnp.sum(lanes.T, axis=0, keepdims=True)
    gains = jnp.broadcast_to(gain[...].astype(f32), (8, rows)).T
    weight_grad[0] = term * gains[:, :1]


def last_part(own, weight, gain, sums):
    shard, cols = weight.shape
    many = len(sums)
    tile = HEAD
    tiles = shard // many // tile
    outs = None
    for h, came in enumerate(sums):
        row = lambda i, h=h: h * tiles + i
        specs = [
            pl.BlockSpec((tile, cols), lambda i, row=row: (row(i), 0)),
            pl.BlockSpec((tile, cols), lambda i, row=row: (row(i), 0)),
            pl.BlockSpec((1, tile), lambda i, row=row: (0, row(i))),
        ]
        for ref in came:
            whole = ref.shape[0] == shard
            at = row if whole else lambda i: i
            specs.append(pl.BlockSpec((tile, cols), lambda i, at=at: (at(i), 0)))
        operands = [own, weight, gain, *came]
        if outs is not None:
            specs += [pl.BlockSpec(memory_space=pl.ANY)] * 2
        outs = pl.pallas_call(
            functools.partial(last_kernel, len(came)),
            grid=(tiles,),
            in_specs=specs,
            out_specs=[
                pl.BlockSpec((1, tile, cols), lambda i, row=row: (0, row(i), 0)),
                pl.BlockSpec((1, tile), lambda i, row=row: (0, row(i))),
            ],
            out_shape=[
                jax.ShapeDtypeStruct((1, shard, cols), f32),
                jax.ShapeDtypeStruct((1, shard), f32),
            ],
            input_output_aliases=(
                {} if outs is None else {len(operands): 0, len(operands) + 1: 1}
            ),
            compiler_params=pltpu.CompilerParams(vmem_limit_bytes=16 * 2**20),
            cost_estimate=pl.CostEstimate(
                flops=shard // many * cols * 8,
                bytes_accessed=shard // many * cols * 14,
                transcendentals=0,
            ),
            name="sum_of_terms",
        )(*operands, *(outs or ()))
    return outs


def start_blocks(plan, at, blocks, ws, w_sem, ks):
    shard = ws.shape[0] // len(plan)
    for k in ks:
        for flag, block, start, stop in plan[k]:
            there = ws.at[k * shard + start : k * shard + stop]
            copy = pltpu.make_async_copy(blocks[block], there, w_sem.at[k])
            if flag is None:
                copy.start()
            else:

                @pl.when(at[at.shape[0] - FLAGS + flag] == 1)
                def _(copy=copy):
                    copy.start()


def wait_block(ws, w_sem, k, shard):
    there = ws.at[k * shard : (k + 1) * shard]
    pltpu.make_async_copy(there, there, w_sem.at[k]).wait()


def columns(at, k, shard):
    return pl.ds(pl.multiple_of(at[k] * shard, shard), shard)


def lane_sums(product):
    total = product[:, :HEAD]
    for c in range(HEAD, product.shape[1], HEAD):
        total = total + product[:, c : c + HEAD]
    return total


def grad_of(kv_grad, weight):
    return lax.dot_general(
        kv_grad[...], weight, (((1,), (1,)), ((), ())), preferred_element_type=f32
    )


def early_kernel(plan, at, x, kv_grad, inv, *refs):
    blocks, (sums, grads, xs, ws, ng, x_sem, w_sem, g_sem) = refs[:-8], refs[-8:]
    n = len(plan)
    shard = xs.shape[2]

    def x_copy(k):
        return pltpu.make_async_copy(x.at[:, columns(at, k, shard)], xs.at[k], x_sem.at[k])

    def g_copy(k):
        return pltpu.make_async_copy(ng.at[k], grads.at[k], g_sem.at[k])

    for k in range(n):
        x_copy(k).start()
        start_blocks(plan, at, blocks, ws, w_sem, [k])
    total = None
    for k in range(n):
        x_copy(k).wait()
        wait_block(ws, w_sem, k, shard)
        grad = grad_of(kv_grad, ws[k * shard : (k + 1) * shard, :])
        ng[k] = grad
        g_copy(k).start()
        product = lane_sums(grad * (xs[k].astype(f32) * inv[:, :1]))
        total = product if total is None else total + product
    sums[...] = total
    for k in range(n):
        g_copy(k).wait()


def late_kernel(plan, done, at, x, kv_grad, inv, cosine, sine, *refs):
    own = 9
    blocks, refs = refs[:-own], refs[-own:]
    if done:
        sums0, grads0, *blocks = blocks
    kv_out, input_grad, xs, hs, ws, ng, x_sem, w_sem, g_sem = refs
    n = len(plan)
    rows, width = x.shape
    shard = xs.shape[2]
    cols = ws.shape[1]
    kvw = cols // 2

    def x_copy(k):
        return pltpu.make_async_copy(x.at[:, columns(at, k, shard)], xs.at[k], x_sem.at[k])

    def o_copy(k):
        return pltpu.make_async_copy(xs.at[k], input_grad.at[:, columns(at, k, shard)], x_sem.at[k])

    order = [*range(done, n), *range(done)]
    for k in order:
        x_copy(k).start()
        start_blocks(plan, at, blocks, ws, w_sem, [k])
    if done:
        load = pltpu.make_async_copy(grads0, ng.at[:done], g_sem.at[0])
        load.start()
        total = sums0[...]
    else:
        total = jnp.zeros((rows, HEAD), f32)
    for k in order:
        x_copy(k).wait()
        normed = xs[k].astype(f32) * inv[:, :1]
        hs[:, k * shard : (k + 1) * shard] = normed.astype(bf16)
        if k >= done:
            wait_block(ws, w_sem, k, shard)
            grad = grad_of(kv_grad, ws[k * shard : (k + 1) * shard, :])
            ng[k] = grad
            total = total + lane_sums(grad * normed)
    mean = jnp.sum(total, axis=1, keepdims=True) / width
    if done:
        load.wait()
    for k in range(done):
        wait_block(ws, w_sem, k, shard)

    def project(i, keys):
        tile = 2 * HEAD
        at_column = pl.ds(pl.multiple_of(i * tile, tile), tile)
        pre = jnp.dot(hs[...], ws[:, at_column], preferred_element_type=f32)
        if keys:
            turned = [pltpu.roll(pre[:, c : c + HEAD], HEAD // 2, 1) for c in (0, HEAD)]
            pre = jnp.concatenate(
                [
                    pre[:, c : c + HEAD] * cosine[...] + part * sine[...]
                    for c, part in zip((0, HEAD), turned)
                ],
                axis=1,
            )
        kv_out[:, at_column] = pre.astype(bf16)

    def finish(k):
        scale = inv[:, :1]
        normed = xs[k].astype(f32) * scale
        xs[k] = (scale * (ng[k] - normed * mean)).astype(bf16)
        o_copy(k).start()

    lax.fori_loop(0, n, lambda k, c: (finish(k), c)[1], 0)
    tiles = kvw // (2 * HEAD)
    lax.fori_loop(0, tiles, lambda i, c: (project(i, True), c)[1], 0)
    lax.fori_loop(tiles, 2 * tiles, lambda i, c: (project(i, False), c)[1], 0)
    lax.fori_loop(0, n, lambda k, c: (o_copy(k).wait(), c)[1], 0)


def pick_blocks(blocks, plan):
    used = sorted({entry[1] for entries in plan for entry in entries})
    plan = tuple(
        tuple((flag, used.index(block), *rest) for flag, block, *rest in entries)
        for entries in plan
    )
    return [blocks[i] for i in used], plan


def early_part(at, tokens_in, kv_grad, inv, blocks, plan, shard):
    rows, width = tokens_in.shape
    cols = kv_grad.shape[1]
    n = len(plan)
    blocks, plan = pick_blocks(blocks, plan)
    whole = pl.BlockSpec(memory_space=pltpu.VMEM)
    there = pl.BlockSpec(memory_space=pl.ANY)
    return pl.pallas_call(
        functools.partial(early_kernel, plan),
        in_specs=[pl.BlockSpec(memory_space=pltpu.SMEM), there, whole, whole]
        + [there] * len(blocks),
        out_specs=[whole, there],
        out_shape=[
            jax.ShapeDtypeStruct((rows, HEAD), f32),
            jax.ShapeDtypeStruct((n, rows, shard), f32),
        ],
        scratch_shapes=[
            pltpu.VMEM((n, rows, shard), bf16),
            pltpu.VMEM((n * shard, cols), bf16),
            pltpu.VMEM((n, rows, shard), f32),
        ]
        + [pltpu.SemaphoreType.DMA((n,))] * 3,
        compiler_params=pltpu.CompilerParams(vmem_limit_bytes=40 * 2**20),
        cost_estimate=pl.CostEstimate(
            flops=2 * rows * shard * n * cols,
            bytes_accessed=shard * n * (6 * rows + 2 * cols),
            transcendentals=0,
        ),
        name="project_first",
    )(at, tokens_in, kv_grad, inv, *blocks)


def late_part(at, tokens_in, kv_grad, inv, cosine, sine, blocks, plan, shard, carry=()):
    rows, width = tokens_in.shape
    cols = kv_grad.shape[1]
    n = len(plan)
    done = carry[1].shape[0] if carry else 0
    blocks, plan = pick_blocks(blocks, plan)
    whole = pl.BlockSpec(memory_space=pltpu.VMEM)
    there = pl.BlockSpec(memory_space=pl.ANY)
    return pl.pallas_call(
        functools.partial(late_kernel, plan, done),
        in_specs=[pl.BlockSpec(memory_space=pltpu.SMEM), there]
        + [whole] * 4
        + [whole, there][: len(carry)]
        + [there] * len(blocks),
        out_specs=[whole, there],
        out_shape=[
            jax.ShapeDtypeStruct((rows, cols), bf16),
            jax.ShapeDtypeStruct((rows, width), bf16),
        ],
        scratch_shapes=[
            pltpu.VMEM((n, rows, shard), bf16),
            pltpu.VMEM((rows, n * shard), bf16),
            pltpu.VMEM((n * shard, cols), bf16),
            pltpu.VMEM((n, rows, shard), f32),
        ]
        + [pltpu.SemaphoreType.DMA((n,))] * 3,
        compiler_params=pltpu.CompilerParams(vmem_limit_bytes=48 * 2**20),
        cost_estimate=pl.CostEstimate(
            flops=4 * rows * width * cols,
            bytes_accessed=4 * rows * width + 2 * width * cols,
            transcendentals=0,
        ),
        name="project_last",
    )(at, tokens_in, kv_grad, inv, cosine, sine, *carry, *blocks)


def replica_pairs(value):
    if lax.axis_size("replica") != 4:
        return lax.psum(value, "replica"), False
    value = value.astype(bf16)
    return (value.astype(f32) + replica_swap(value, 1).astype(f32)).astype(bf16), True


def replica_swap(value, step):
    return lax.ppermute(value, "replica", [(r, r ^ step) for r in range(4)])


def exchange_ring(ring, own, far, near, pseudo, early, late, update):
    pairs, halved = pseudo
    total = (pairs, replica_swap(pairs, 2) if halved else jnp.zeros((), f32))
    shard, cut = own.shape[0], own.shape[0] // 2
    blocks = [own]
    from_left = from_right = own
    for d in range(1, ring.half):
        from_left, from_right = ring.to_right(from_left), ring.to_left(from_right)
        blocks += [from_left, from_right]
    from_left, from_right = after((from_left, from_right), total)
    blocks += [ring.to_right(from_left[:cut]), ring.to_left(from_right[cut:])]
    last = len(blocks) - 2
    plan = [((None, k, 0, shard),) for k in range(last)]
    plan.append(((None, last, 0, cut), (None, last + 1, cut, shard)))

    far = after(far, blocks[1], blocks[2])
    from_left, from_right = ring.to_right(far[:cut]), ring.to_left(far[cut:])
    for k in range(0, 2 * (ring.half - 1), 2):
        from_left, from_right = lax.optimization_barrier((from_left, from_right))
        if k == 0:
            from_left = jnp.pad(from_left, ((0, shard - cut), (0, 0)))
            from_right = jnp.pad(from_right, ((cut, 0), (0, 0)))
        from_left = ring.to_right((near[k] + from_left.astype(f32)).astype(bf16))
        from_right = ring.to_left((near[k + 1] + from_right.astype(f32)).astype(bf16))
    sums = [(from_left, from_right)]
    return late(blocks, plan), sums, update(total)


ORDER = {"sum": (-1, 1), "pair": (-1, 3), "inner": (2, 7), "far": (1, 5), "partner": (7, None), "first": (2, 4), "update": (5, 9)}
CHAIN = True


def exchange_plane(plane, own, far, near, pseudo, early, late, update):
    shard = own.shape[0]
    at0, at1, at2, at3 = plane.at
    zero = jnp.zeros((), f32)
    pieces = [(0, shard // 2), (shard // 2, shard)]
    halves = range(2)
    wide = lambda v: v.astype(f32)
    pick = jnp.where
    sent, crossed, beside = [own], [own], {}

    def part(value, h):
        return value[pieces[h][0] : pieces[h][1]]

    def chord(value):
        crossed[0] = plane.over_chord(after(value, sent[0], crossed[0] if CHAIN else own))
        return crossed[0]

    def ring(step, to_right, to_left):
        sent[0] = to_right, to_left
        came = lax.optimization_barrier([plane.to_right(to_right), plane.to_left(to_left)])
        for name, (begin, _) in ORDER.items():
            if begin == step:
                beside[name] = tasks[name]()
        return came

    def later(step, *values):
        names = [name for name, (_, end) in ORDER.items() if end == step]
        awaited = [beside[name] for name in names]
        values, awaited = lax.optimization_barrier((after(values, sent[0]), awaited))
        beside.update(zip(names, awaited))
        return values

    ways = lambda flag, at: tuple((flag, at + h, *pieces[h]) for h in halves)
    by_way = lambda steps: [steps[h][way] for way in range(2) for h in halves]
    near_plan = [((None, k, 0, shard),) for k in range(3)] + [ways(None, 3), ways(None, 5)]
    tasks = {
        "far": lambda: chord(pick(at2, *first)),
        "inner": lambda: chord(far),
        "partner": lambda: chord(pick(at1, near[1], near[0]).astype(bf16)),
        "first": lambda: early([after(own, sent[0]), *first, *by_way(two)], near_plan),
        "update": lambda: update(after((pairs, beside["sum"]), sent[0])),
    }

    first = ring(None, own, own)
    beside["pair"] = chord(own)
    pairs, first_swap = pseudo
    came = replica_swap(pairs, 2) if first_swap else jnp.zeros((), f32)
    first, far = lax.optimization_barrier((first, far))
    beside["sum"] = came
    two = [ring(0, *(part(side, 0) for side in first))]
    two.append(ring(1, *(part(side, 1) for side in later(1, *first))))
    three = []
    for h in halves:
        left, right = later(2 + h, *two[h])
        terms = part(far, h)
        three.append(ring(2 + h, pick(at0, terms, left), pick(at3, terms, right)))
    four = []
    for h in halves:
        left, right = later(4 + h, *three[h])
        to_right = wide(part(near[0], h)) + pick(at1, wide(left), zero)
        to_left = wide(part(near[1], h)) + pick(at2, wide(right), zero)
        to_right = pick(at2, left, to_right.astype(bf16))
        to_left = pick(at1, right, to_left.astype(bf16))
        four.append(ring(4 + h, to_right, to_left))
    five = []
    for h in halves:
        left, right = later(6 + h, *four[h])
        to_right = part(near[2], h) + pick(at3, zero, wide(left))
        to_left = part(near[3], h) + pick(at0, zero, wide(right))
        five.append(ring(6 + h, to_right.astype(bf16), to_left.astype(bf16)))
    six = []
    for h in halves:
        left, right = later(8 + h, *five[h])
        over = wide(part(beside["inner"], h))
        to_right = part(near[4], h) + wide(left) + pick(at1, over, zero)
        to_left = part(near[5], h) + wide(right) + pick(at2, over, zero)
        six.append(ring(8 + h, to_right.astype(bf16), to_left.astype(bf16)))
    sums = [(*six[h], beside["partner"]) for h in halves]

    blocks = [own, *first, *by_way(two), beside["pair"], *by_way(three), beside["far"], *by_way(four)]
    plan = near_plan + [
        ((0, 7, 0, shard), *ways(2, 8)),
        ((1, 7, 0, shard), *ways(3, 10)),
        ((4, 12, 0, shard), *ways(5, 13), *ways(6, 15)),
    ]
    return late(blocks, plan, beside["first"]), sums, beside["update"]


def local(
    layer_input,
    norm_gain,
    kv_weight,
    kv_cotangent,
    pseudo_grad,
    outer_momentum,
    global_params,
    local_params,
):
    small = lax.axis_size("fsdp") == 8
    ring = Plane() if small else Ring()
    tokens_in = layer_input[0]
    weight_shard = kv_weight[0]
    cotangent = kv_cotangent[0]
    rows, width = tokens_in.shape
    shard, cols = weight_shard.shape

    own = scale_rows(weight_shard, norm_gain)
    positions = (ring.me * rows + jnp.arange(rows, dtype=jnp.int32)) % SEQ_LEN
    cosine, sine = rope_tables(positions)
    scale = 1.0 / math.sqrt(rows * ring.count)
    pairs, halved = replica_pairs(after(pseudo_grad[0], own))
    kv_grad, inv, far, near, last = first_part(
        ring, tokens_in, after(cotangent, pairs), cosine, sine, shard, scale
    )
    order = [0]
    for d in range(1, ring.half):
        order += [-d, d]
    order.append(ring.half)
    at = [ring.devices_at(order).astype(jnp.int32)]
    if small:
        at0, at1, at2, at3 = ring.at
        flags = [at1, at2, ~at1, ~at2, at1 | at2, at3, at0]
        at.append(jnp.stack(flags).astype(jnp.int32))
    at = jnp.concatenate(at)

    def early(blocks, plan):
        return early_part(at, tokens_in, kv_grad, inv, blocks, plan, shard)

    def late(blocks, plan, carry=()):
        return late_part(at, tokens_in, kv_grad, inv, cosine, sine, blocks, plan, shard, carry)

    def update(total):
        if isinstance(total, tuple):
            total = total[0].astype(f32) + total[1].astype(f32)
        average = total / lax.axis_size("replica")
        momentum_new = momentum_rate * outer_momentum + average
        global_new = global_params - outer_rate * (average + momentum_rate * momentum_new)
        local_new = (
            mixing_rate * local_params[0].astype(f32) + (1.0 - mixing_rate) * global_new
        ).astype(bf16)
        return momentum_new, global_new, local_new

    exchange = exchange_plane if small else exchange_ring
    (kv_out, input_grad), sums, updated = exchange(
        ring, own, far, near, (pairs, halved), early, late, update
    )
    momentum_new, global_new, local_new = updated
    weight_grad, gain_grad = last_part(last, weight_shard, norm_gain, sums)

    return (
        kv_out[None],
        input_grad[None],
        weight_grad,
        gain_grad,
        momentum_new,
        global_new,
        local_new[None],
    )


def solution(mesh):
    in_specs = (
        P("replica", "fsdp", None),
        P("replica", "fsdp"),
        P("replica", "fsdp", None),
        P("replica", "fsdp", None),
        P("replica", "fsdp", None),
        P("fsdp", None),
        P("fsdp", None),
        P("replica", "fsdp", None),
    )
    out_specs = (
        P("replica", "fsdp", None),
        P("replica", "fsdp", None),
        P("replica", "fsdp", None),
        P("replica", "fsdp"),
        P("fsdp", None),
        P("fsdp", None),
        P("replica", "fsdp", None),
    )
    return jax.shard_map(local, mesh=mesh, in_specs=in_specs, out_specs=out_specs, check_vma=False)
```
